128 devices in a mesh: dp: 2 (over y_hi), row: 16 (over y_lo, z, core), col: 4 (over x).
Axes of the slice: x: 4, y: 4 (y_hi: 2, y_lo: 2; y = y_hi * 2 + y_lo), z: 4, core: 2. Of those that a mesh axis runs over, the one named last changes fastest.
Arguments:
- features: bfloat16 [2, 320, 320, 512], P('dp', 'row', 'col'), parts along dimension 0, may hold values from -6 to 6
- hole_mask: int32 [2, 320, 320], P('dp', 'row', 'col'), parts along dimension 0, may hold values 0 or 1
- cotangent: bfloat16 [2, 320, 320, 512], P('dp', 'row', 'col'), parts along dimension 0, may hold values from -6 to 6
- w_local: bfloat16 [3, 3, 512, 128], replicated, may hold values from -0.09375 to 0.09375
- w_cross: bfloat16 [3, 3, 128, 384], replicated, may hold values from -0.1875 to 0.1875
- w_in: bfloat16 [384, 192], replicated, may hold values from -0.3125 to 0.3125
- w_freq: bfloat16 [384, 384], replicated, may hold values from -0.3125 to 0.3125
- w_out: bfloat16 [192, 384], replicated, may hold values from -0.4375 to 0.4375
Outputs:
- output: bfloat16 [2, 320, 320, 512], P('dp', ('row', 'col')), parts along dimension 0
- grad_features: bfloat16 [2, 320, 320, 512], P('dp', ('row', 'col')), parts along dimension 0
- grad_local: float32 [6, 3, 512, 128], P('dp'), parts along dimension 0
- grad_cross: float32 [6, 3, 128, 384], P('dp'), parts along dimension 0
- grad_in: float32 [768, 192], P('dp'), parts along dimension 0
- grad_freq: float32 [768, 384], P('dp'), parts along dimension 0
- grad_out: float32 [384, 384], P('dp'), parts along dimension 0
The draws below stay inside these ranges and needn't reach their ends.
There are 2 independent parts, one for each index of `dp`. The reference program is written for one: setup_inputs(seed, part) draws one part's arguments, and reference() takes and returns one part's arrays. A program takes and returns all parts, laid end to end along the dimension named above; an argument that names none is the same for every part. Nothing has to cross between parts.
All inputs are finite; a program needn't handle non-finite values. No bound on the sum of `hole_mask` on one device may be relied on, other than what follows from the above.
Results may differ from the reference program's by a relative error of at most 0.025.
Values may be sent and summed in bfloat16 or wider, within the bound.
No kernel may reach another device: no remote copies, remote signals or barrier semaphores. Data moves between devices by JAX's collectives and lax.ppermute only.
A program may use at most 128 MiB of HBM per device.

```python
import jax
import jax.numpy as jnp
from jax import lax

B = 1
H = 320
W = 320
CL = 128
CG = 384
CS = 192
CH = 512


def place_ends(entries, own_key, low, top_value):
    longest = entries.shape.index(max(entries.shape))
    spots = []
    for shift in (0, 1):
        where = [jax.random.randint(jax.random.fold_in(own_key, axis), (), 0, length) for axis, length in enumerate(entries.shape)]
        where[longest] = (where[longest] + shift) % entries.shape[longest]
        spots.append(tuple(where))
    return entries.at[spots[0]].set(low).at[spots[1]].set(top_value)


def steps_of(stream_key, extent, shards, smallest, largest):
    def one(axis_at, parts):
        steps = jax.random.uniform(jax.random.fold_in(jax.random.fold_in(stream_key, 6), axis_at), (parts,), jnp.float32, smallest / len(shards), largest / len(shards))
        return jnp.repeat(jnp.exp(steps), extent[axis_at] // parts).reshape((-1,) + (1,) * (len(extent) - axis_at - 1))

    loudness = one(*shards[0])
    for cut in shards[1:]:
        loudness = loudness * one(*cut)
    return loudness


def normal_values(own_key, extent, width, bound, shards=(), dtype=jnp.bfloat16):
    entries = width * jax.random.normal(own_key, extent, jnp.float32)
    if shards:
        entries = entries * steps_of(own_key, extent, shards, -0.22, 0.18)
    return jnp.clip(entries, -bound, bound).astype(dtype)


def setup_inputs(seed: int = 0, part: int = 0) -> dict:
    seeds = jax.random.split(jax.random.key(seed), 9)
    part_splits = jax.random.split(jax.random.fold_in(seeds[8], part), 9)
    features = normal_values(part_splits[0], (B, H, W, CH), 1.0, 6.0, ((1, 16), (2, 4)))
    hole_mask = place_ends((jax.random.randint(part_splits[1], (B, H, W), 0, 4) < 1).astype(jnp.int32), jax.random.fold_in(part_splits[1], 1), 0, 1)
    cotangent = normal_values(part_splits[2], (B, H, W, CH), 1.0, 6.0, ((1, 16), (2, 4)))
    w_local = normal_values(seeds[3], (3, 3, CH, CL), (9 * CH) ** -0.5, 0.09375)
    w_cross = normal_values(seeds[4], (3, 3, CL, CG), (9 * CL) ** -0.5, 0.1875)
    w_in = normal_values(seeds[5], (CG, CS), CG ** -0.5, 0.3125)
    w_freq = normal_values(seeds[6], (2 * CS, 2 * CS), (2 * CS) ** -0.5, 0.3125)
    w_out = normal_values(seeds[7], (CS, CG), CS ** -0.5, 0.4375)
    return {"features": features, "hole_mask": hole_mask, "cotangent": cotangent, "w_local": w_local, "w_cross": w_cross, "w_in": w_in, "w_freq": w_freq, "w_out": w_out}


def conv_valid(padded, kernel):
    return lax.conv_general_dilated(padded, kernel, (1, 1), "VALID", dimension_numbers=("NHWC", "HWIO", "NHWC"), preferred_element_type=jnp.float32)


def pad_map(field):
    return jnp.pad(field, ((0, 0), (1, 1), (1, 1), (0, 0)))


def silu_slope(value):
    sigma = jax.nn.sigmoid(value)
    return sigma * (1.0 + value * (1.0 - sigma))


def flipped(kernel):
    return jnp.transpose(kernel[::-1, ::-1], (0, 1, 3, 2))


def correlate(padded, grads):
    rows, cols = grads.shape[1], grads.shape[2]
    grads_f = grads.astype(jnp.float32)
    kernel_rows = []
    for row_off in range(3):
        row_terms = []
        for col_off in range(3):
            window = padded[:, row_off:row_off + rows, col_off:col_off + cols, :].astype(jnp.float32)
            row_terms.append(jnp.einsum("bhwc,bhwd->cd", window, grads_f))
        kernel_rows.append(jnp.stack(row_terms))
    return jnp.stack(kernel_rows)


def project(field, matrix):
    return jnp.einsum("bhwc,cd->bhwd", field.astype(jnp.float32), matrix.astype(jnp.float32))


def spectrum(field):
    whole = jnp.fft.fft2(field.astype(jnp.float32), axes=(1, 2), norm="ortho")
    return jnp.real(whole), jnp.imag(whole)


def inverse_real(real_part, imag_part):
    return jnp.real(jnp.fft.ifft2(lax.complex(real_part, imag_part), axes=(1, 2), norm="ortho"))


def reference(features, hole_mask, cotangent, w_local, w_cross, w_in, w_freq, w_out):
    keep_mask = (1 - hole_mask).astype(jnp.bfloat16)[..., None]
    masked = features * keep_mask
    padded = pad_map(masked)
    pre_local = conv_valid(padded, w_local)
    pre_cross = conv_valid(padded[..., :CL], w_cross)
    pre_unit = project(masked[..., CL:], w_in)
    unit_act = jax.nn.silu(pre_unit).astype(jnp.bfloat16)
    spec_real, spec_imag = spectrum(unit_act)
    stacked = jnp.concatenate([spec_real, spec_imag], -1).astype(jnp.bfloat16)
    pre_freq = project(stacked, w_freq)
    mixed_act = jax.nn.silu(pre_freq)
    back_field = inverse_real(mixed_act[..., :CS], mixed_act[..., CS:]).astype(jnp.bfloat16)
    joined = (unit_act.astype(jnp.float32) + back_field.astype(jnp.float32)).astype(jnp.bfloat16)
    pre_global = pre_cross + project(joined, w_out)
    output = jnp.concatenate([jax.nn.silu(pre_local), jax.nn.silu(pre_global)], -1).astype(jnp.bfloat16)
    cot_f = cotangent.astype(jnp.float32)
    d_local = (cot_f[..., :CL] * silu_slope(pre_local)).astype(jnp.bfloat16)
    d_global = (cot_f[..., CL:] * silu_slope(pre_global)).astype(jnp.bfloat16)
    grad_out = jnp.einsum("bhwc,bhwd->cd", joined.astype(jnp.float32), d_global.astype(jnp.float32))
    d_joined = project(d_global, jnp.transpose(w_out)).astype(jnp.bfloat16)
    dz_real, dz_imag = spectrum(d_joined)
    d_freq = (jnp.concatenate([dz_real, dz_imag], -1) * silu_slope(pre_freq)).astype(jnp.bfloat16)
    grad_freq = jnp.einsum("bhwc,bhwd->cd", stacked.astype(jnp.float32), d_freq.astype(jnp.float32))
    d_stacked = project(d_freq, jnp.transpose(w_freq))
    d_back = inverse_real(d_stacked[..., :CS], d_stacked[..., CS:]).astype(jnp.bfloat16)
    d_unit = ((d_joined.astype(jnp.float32) + d_back.astype(jnp.float32)) * silu_slope(pre_unit)).astype(jnp.bfloat16)
    grad_in = jnp.einsum("bhwc,bhwd->cd", masked[..., CL:].astype(jnp.float32), d_unit.astype(jnp.float32))
    grad_local = correlate(padded, d_local)
    grad_cross = correlate(padded[..., :CL], d_global)
    d_pad = pad_map(jnp.concatenate([d_local, d_global], -1))
    d_masked = conv_valid(d_pad[..., :CL], flipped(w_local))
    d_cross = conv_valid(d_pad[..., CL:], flipped(w_cross))
    d_proj = project(d_unit, jnp.transpose(w_in))
    d_masked = d_masked + jnp.concatenate([d_cross, d_proj], -1)
    grad_features = (d_masked * keep_mask.astype(jnp.float32)).astype(jnp.bfloat16)
    return output, grad_features, grad_local, grad_cross, grad_in, grad_freq, grad_out
```

```python
import functools
import math

import jax
import jax.numpy as jnp
import numpy as np
from jax import lax
from jax.sharding import PartitionSpec as P

AXES = ("row", "col")
HOLE = 64.0


def dot(a, b, dims=((1,), (0,))):
    return lax.dot_general(a, b, (dims, ((), ())), preferred_element_type=jnp.float32)


def line_tables(rows, width, count, lines, slots):
    cos = np.zeros((count, slots, rows, width), np.float32)
    sin = np.zeros((count, slots, rows, width), np.float32)
    freq = lines * np.arange(count)[:, None] + np.arange(lines)[None]
    angle = 2.0 * np.pi * (freq[..., None] * np.arange(width) % width) / width
    valid = (freq <= width // 2)[..., None]
    for y in range(rows):
        cos[:, y * lines : (y + 1) * lines, y] = np.cos(angle) * valid
        sin[:, y * lines : (y + 1) * lines, y] = np.sin(angle) * valid
    shape = (count * slots, rows * width)
    return cos.reshape(shape).astype(jnp.bfloat16), sin.reshape(shape).astype(jnp.bfloat16)


def column_tables(rows, count, lines, slots):
    height = rows * count
    cos = np.zeros((count, slots, count, slots), np.float32)
    sin = np.zeros((count, slots, count, slots), np.float32)
    h = np.arange(height).reshape(count, rows)
    angle = 2.0 * np.pi * (h[:, :, None, None] * h[None, None] % height) / height
    for y in range(rows):
        for z in range(rows):
            for j in range(lines):
                cos[:, y * lines + j, :, z * lines + j] = np.cos(angle[:, y, :, z])
                sin[:, y * lines + j, :, z * lines + j] = np.sin(angle[:, y, :, z])
    shape = (count * slots, count * slots)
    return cos.reshape(shape).astype(jnp.bfloat16), sin.reshape(shape).astype(jnp.bfloat16)


def silu_slope(value):
    sigma = jax.nn.sigmoid(value)
    return sigma * (1.0 + value * (1.0 - sigma))


def swap(x, count):
    return lax.all_to_all(x.reshape(count, -1, x.shape[-1]), AXES, 0, 0, tiled=True).reshape(x.shape)


def to_rows(field, cols):
    h, w, c = field.shape
    out = lax.all_to_all(field.reshape(cols, h // cols, w, c), "col", 0, 0, tiled=True)
    return jnp.transpose(out, (1, 0, 2, 3)).reshape(h // cols, w * cols, c)


def with_halo(field, count):
    down = lax.ppermute(field[-1:], AXES, [(i, i + 1) for i in range(count - 1)])
    up = lax.ppermute(field[:1], AXES, [(i + 1, i) for i in range(count - 1)])
    return jnp.concatenate([down, field, up], 0)


def conv(padded, kernel):
    return lax.conv_general_dilated(
        padded[None],
        kernel,
        (1, 1),
        ((0, 0), (1, 1)),
        dimension_numbers=("NHWC", "HWIO", "NHWC"),
        preferred_element_type=jnp.float32,
    )[0].reshape(-1, kernel.shape[-1])


def taps(padded, flip):
    rows, width, c = padded.shape[0] - 2, padded.shape[1], padded.shape[2]
    wide = jnp.pad(padded, ((0, 0), (1, 1), (0, 0)))
    parts = []
    for i in range(3):
        for j in range(3):
            y, x = (2 - i, 2 - j) if flip else (i, j)
            parts.append(wide[y : y + rows, x : x + width])
    return jnp.concatenate(parts, -1).reshape(rows * width, 9 * c)


def shards(features, hole_mask, cotangent, w_local, w_cross, w_in, w_freq, w_out):
    cols = lax.axis_size("col")
    count = lax.axis_size("row") * cols
    me = lax.axis_index(AXES)
    _, h, w, ch = features.shape
    rows, width = h // cols, w * cols
    height = rows * count
    cl = w_local.shape[3]
    cg = w_cross.shape[3]
    cs = w_in.shape[1]
    lines = -(-(width // 2 + 1) // count)
    slots = -(-(rows * lines) // 16) * 16
    tw_cos, tw_sin = line_tables(rows, width, count, lines, slots)
    th_cos, th_sin = column_tables(rows, count, lines, slots)
    norm_w, norm_h = 1.0 / math.sqrt(width), 1.0 / math.sqrt(height)
    freq = lines * me + jnp.arange(slots) % lines
    weight = jnp.where((freq == 0) | (freq * 2 == width), 0.5, jnp.where(freq * 2 < width, 1.0, 0.0))
    weight = jnp.tile(weight.astype(jnp.float32), count)[:, None]
    bf = jnp.bfloat16

    def forward(u):
        x = jnp.concatenate([dot(tw_cos, u) * norm_w, dot(tw_sin, u) * -norm_w], -1).astype(bf)
        x = swap(x, count)
        p, q = dot(th_cos, x), dot(th_sin, x)
        return (p[:, :cs] + q[:, cs:]) * norm_h, (p[:, cs:] - q[:, :cs]) * norm_h

    def inverse(re, im):
        x = jnp.concatenate([re, im], -1).astype(bf)
        p, q = dot(th_cos, x), dot(th_sin, x)
        x = jnp.concatenate([p[:, :cs] - q[:, cs:], p[:, cs:] + q[:, :cs]], -1) * norm_h
        x = swap(x.astype(bf), count)
        first = ((0,), (0,))
        return (dot(tw_cos, x[:, :cs], first) - dot(tw_sin, x[:, cs:], first)) * norm_w

    marked = jnp.where(hole_mask[0][..., None] == 1, HOLE, features[0]).astype(bf)
    marked = to_rows(marked, cols)
    keep = marked[..., :1] < 0.5 * HOLE
    masked = jnp.where(keep, marked, 0).astype(bf)
    cot = to_rows(cotangent[0], cols).reshape(-1, ch)
    flat = masked.reshape(-1, ch)
    pre_unit = dot(flat[:, cl:], w_in)
    unit = jax.nn.silu(pre_unit).astype(bf)
    spec_re, spec_im = forward(unit)
    st_re, st_im = spec_re.astype(bf), spec_im.astype(bf)
    part_re, part_im = dot(st_re, w_freq[:cs]), dot(st_im, w_freq[cs:])
    pre_pos, pre_neg = part_re + part_im, part_re - part_im
    mix_pos, mix_neg = jax.nn.silu(pre_pos), jax.nn.silu(pre_neg)
    back = inverse(
        weight * (mix_pos[:, :cs] + mix_neg[:, :cs]), weight * (mix_pos[:, cs:] - mix_neg[:, cs:])
    ).astype(bf)
    joined = (unit.astype(jnp.float32) + back.astype(jnp.float32)).astype(bf)

    padded = with_halo(masked, count)
    pre_local = conv(padded, w_local)
    windows = taps(padded[..., :cl], False)
    pre_cross = dot(windows, w_cross.reshape(9 * cl, cg))
    pre_global = pre_cross + dot(joined, w_out)
    output = jnp.concatenate([jax.nn.silu(pre_local), jax.nn.silu(pre_global)], -1).astype(bf)
    cot_f = cot.astype(jnp.float32)
    d_local = (cot_f[:, :cl] * silu_slope(pre_local)).astype(bf)
    d_global = (cot_f[:, cl:] * silu_slope(pre_global)).astype(bf)
    d_joined = dot(d_global, w_out, ((1,), (1,))).astype(bf)
    dz_re, dz_im = forward(d_joined)
    slope_pos, slope_neg = silu_slope(pre_pos), silu_slope(pre_neg)
    dz = jnp.concatenate([dz_re, dz_im], -1)
    dz_conj = jnp.concatenate([dz_re, -dz_im], -1)
    d_pos = (dz * slope_pos).astype(bf).astype(jnp.float32)
    d_neg = (dz_conj * slope_neg).astype(bf).astype(jnp.float32)
    d_sum = (weight * (d_pos + d_neg)).astype(bf)
    d_diff = (weight * (d_pos - d_neg)).astype(bf)
    first = ((0,), (0,))
    last = ((1,), (1,))
    grad_freq = jnp.concatenate([dot(st_re, d_sum, first), dot(st_im, d_diff, first)], 0)
    d_back = inverse(dot(d_sum, w_freq[:cs], last), dot(d_diff, w_freq[cs:], last)).astype(bf)
    d_unit = (
        (d_joined.astype(jnp.float32) + d_back.astype(jnp.float32)) * silu_slope(pre_unit)
    ).astype(bf)

    grad_out = dot(joined, d_global, first)
    grad_cross = dot(windows, d_global, first)
    d_pad = with_halo(jnp.concatenate([d_local, d_global], -1).reshape(rows, width, ch), count)
    d_windows = taps(d_pad[..., :cl], True)
    grad_local = dot(flat, d_windows, first)
    w_local_t = jnp.transpose(w_local, (0, 1, 3, 2)).reshape(9 * cl, ch)
    d_masked = dot(d_windows, w_local_t)
    d_cross = conv(d_pad[..., cl:], jnp.transpose(w_cross[::-1, ::-1], (0, 1, 3, 2)))
    d_proj = dot(d_unit, w_in, last)
    d_masked = d_masked + jnp.concatenate([d_cross, d_proj], -1)
    grad_features = jnp.where(keep.reshape(-1, 1), d_masked, 0.0).astype(bf)
    grad_in = dot(flat[:, cl:], d_unit, first)

    def reduce_all(terms):
        flats = [t.reshape(count, -1, t.shape[-1]).reshape(count, -1, 128) for t in terms]
        sizes = [f.shape[1] for f in flats]
        x = jnp.concatenate(flats, 1).astype(bf)
        x = lax.all_to_all(x, AXES, 0, 0, tiled=True)
        x = x.astype(jnp.float32).sum(0).astype(bf)
        x = lax.all_to_all(jnp.broadcast_to(x[None], (count,) + x.shape), AXES, 0, 0, tiled=True)
        outs, at = [], 0
        for t, size in zip(terms, sizes):
            outs.append(x[:, at : at + size].reshape(t.shape).astype(jnp.float32))
            at += size
        return outs

    grad_local, grad_cross, grad_freq, grad_out = reduce_all([grad_local, grad_cross, grad_freq, grad_out])
    (grad_in,) = reduce_all([grad_in])
    grad_local = jnp.transpose(grad_local.reshape(ch, 3, 3, cl), (1, 2, 0, 3))
    grad_cross = grad_cross.reshape(3, 3, cl, cg)
    shape = (1, rows, width, ch)
    return output.reshape(shape), grad_features.reshape(shape), grad_local, grad_cross, grad_in, grad_freq, grad_out


def solution(mesh):
    return jax.shard_map(
        shards,
        mesh=mesh,
        in_specs=(
            P("dp", "row", "col", None),
            P("dp", "row", "col"),
            P("dp", "row", "col", None),
            P(),
            P(),
            P(),
            P(),
            P(),
        ),
        out_specs=(
            P("dp", ("row", "col"), None, None),
            P("dp", ("row", "col"), None, None),
            P("dp", None, None, None),
            P("dp", None, None, None),
            P("dp", None),
            P("dp", None),
            P("dp", None),
        ),
        check_vma=False,
    )
```

```python
import functools
import math

import jax
import jax.numpy as jnp
import numpy as np
from jax import lax
from jax.experimental import pallas as pl
from jax.experimental.pallas import tpu as pltpu
from jax.sharding import PartitionSpec as P

AXES = ("row", "col")
HOLE = 64.0
BF = jnp.bfloat16
F32 = jnp.float32
ROWS_OF = ((0,), (0,))


def dot(a, b, dims=((1,), (0,))):
    return lax.dot_general(a, b, (dims, ((), ())), preferred_element_type=F32)


def line_tables(rows, width, count, lines, slots):
    cos = np.zeros((rows, count, slots, width), np.float32)
    sin = np.zeros((rows, count, slots, width), np.float32)
    freq = lines * np.arange(count)[:, None] + np.arange(lines)[None]
    angle = 2.0 * np.pi * (freq[..., None] * np.arange(width) % width) / width
    valid = (freq <= width // 2)[..., None]
    for y in range(rows):
        cos[y, :, y * lines : (y + 1) * lines] = np.cos(angle) * valid
        sin[y, :, y * lines : (y + 1) * lines] = np.sin(angle) * valid
    shape = (rows, count * slots, width)
    return cos.reshape(shape).astype(BF), sin.reshape(shape).astype(BF)


def column_tables(rows, count, lines, slots):
    height = rows * count
    cos = np.zeros((count, slots, count, slots), np.float32)
    sin = np.zeros((count, slots, count, slots), np.float32)
    h = np.arange(height).reshape(count, rows)
    angle = 2.0 * np.pi * (h[:, :, None, None] * h[None, None] % height) / height
    for y in range(rows):
        for z in range(rows):
            for j in range(lines):
                cos[:, y * lines + j, :, z * lines + j] = np.cos(angle[:, y, :, z])
                sin[:, y * lines + j, :, z * lines + j] = np.sin(angle[:, y, :, z])
    shape = (count * slots, count * slots)
    return cos.reshape(shape).astype(BF), sin.reshape(shape).astype(BF)


def slope_and_silu(value):
    sigma = 1.0 / (1.0 + jnp.exp(-value))
    return sigma * (1.0 + value * (1.0 - sigma)), value * sigma


def lanes_below(shape, bound):
    return lax.broadcasted_iota(jnp.int32, shape, 1) < bound


def packed(re, im):
    mid = jnp.where(lanes_below(re[:, 128:].shape, 64), re[:, 128:], im[:, 128:])
    return jnp.concatenate([re[:, :128], mid, im[:, :128]], 1)


def turned(p, q, sign):
    mid = pltpu.roll(q[:, 128:256], 64, 1)
    flip = jnp.where(lanes_below(mid.shape, 64), sign, -sign)
    return jnp.concatenate(
        [p[:, :128] + sign * q[:, 256:], p[:, 128:256] + flip * mid, p[:, 256:] - sign * q[:, :128]], 1
    )


def pack_order(cs):
    return [(0, 128), (128, cs), (cs + 128, 2 * cs), (cs, cs + 128)]


def pack_dim(x, dim, cs):
    return jnp.concatenate([lax.slice_in_dim(x, a, b, axis=dim) for a, b in pack_order(cs)], dim)


def unpack_dim(x, dim, cs):
    cuts = [(0, 128), (128, cs), (256, 384), (cs, 256)]
    return jnp.concatenate([lax.slice_in_dim(x, a, b, axis=dim) for a, b in cuts], dim)


def call(body, name, grid, ins, outs, scratch=(), flops=0, bytes_=0):
    def spec(shape, block, index):
        if block is None:
            zeros = (0,) * len(shape)
            return pl.BlockSpec(shape, lambda *_: zeros)
        return pl.BlockSpec(block, index)

    return pl.pallas_call(
        body,
        grid=grid,
        in_specs=[spec(a.shape, block, index) for a, block, index in ins],
        out_specs=[spec(shape, block, index) for shape, _, block, index in outs],
        out_shape=[jax.ShapeDtypeStruct(shape, dtype) for shape, dtype, _, _ in outs],
        scratch_shapes=list(scratch),
        compiler_params=pltpu.CompilerParams(vmem_limit_bytes=56 << 20),
        cost_estimate=pl.CostEstimate(flops=flops, bytes_accessed=bytes_, transcendentals=0),
        name=name,
    )(*[a for a, _, _ in ins])


def head_kernel(norm, cl, marked, w_in, tc, ts, masked, unit, sent, acc_c, acc_s):
    y = pl.program_id(0)
    x = marked[...].reshape(-1, marked.shape[-1])
    keep = x[:, :1].astype(F32) < 0.5 * HOLE
    x = jnp.where(keep, x, jnp.zeros_like(x))
    masked[0] = x
    u = slope_and_silu(dot(x[:, cl:], w_in[...]))[1].astype(BF)
    unit[0] = u
    transform_out(y, norm, u, tc, ts, sent, acc_c, acc_s)


def transform_out(y, norm, u, tc, ts, sent, acc_c, acc_s):
    re, im = dot(tc[0], u), dot(ts[0], u)

    @pl.when(y == 0)
    def _():
        acc_c[...] = re
        acc_s[...] = im

    @pl.when(y > 0)
    def _():
        acc_c[...] += re
        acc_s[...] += im

    @pl.when(y == pl.num_programs(0) - 1)
    def _():
        sent[...] = packed(acc_c[...] * norm, acc_s[...] * -norm).astype(BF)


def frequency_kernel(norm, tile, got, tc, ts, w_freq, weight, sign, stacked, sent, z):
    def first(k, carry):
        rows = pl.ds(pl.multiple_of(k * tile, tile), tile)
        spec = turned(dot(tc[rows, :], got[...]), dot(ts[rows, :], got[...]), 1.0) * norm
        st = spec.astype(BF)
        stacked[rows, :] = st
        pos = slope_and_silu(dot(st, w_freq[...]))[1]
        neg = slope_and_silu(dot((st.astype(F32) * sign[...]).astype(BF), w_freq[...]))[1]
        z[rows, :] = (weight[rows, :] * (pos + sign[...] * neg)).astype(BF)
        return carry

    def second(k, carry):
        rows = pl.ds(pl.multiple_of(k * tile, tile), tile)
        sent[rows, :] = (turned(dot(tc[rows, :], z[...]), dot(ts[rows, :], z[...]), -1.0) * norm).astype(BF)
        return carry

    steps = got.shape[0] // tile
    lax.fori_loop(0, steps, first, 0)
    lax.fori_loop(0, steps, second, 0)


def frequency_back_kernel(
    norm, tile, got, tc, ts, w_freq, w_freq_t, weight, sign, stacked, sent, grad, z, acc_p, acc_m
):
    acc_p[...] = jnp.zeros_like(acc_p)
    acc_m[...] = jnp.zeros_like(acc_m)

    def first(k, carry):
        rows = pl.ds(pl.multiple_of(k * tile, tile), tile)
        dz = turned(dot(tc[rows, :], got[...]), dot(ts[rows, :], got[...]), 1.0) * norm
        st = stacked[rows, :]
        pos = slope_and_silu(dot(st, w_freq[...]))[0]
        neg = slope_and_silu(dot((st.astype(F32) * sign[...]).astype(BF), w_freq[...]))[0]
        pos = (dz * pos).astype(BF).astype(F32)
        neg = (dz * sign[...] * neg).astype(BF).astype(F32)
        total = (weight[rows, :] * (pos + neg)).astype(BF)
        delta = (weight[rows, :] * (pos - neg)).astype(BF)
        acc_p[...] += dot(st[:, :256], total, ROWS_OF)
        acc_m[...] += dot(st[:, 128:], delta, ROWS_OF)
        re = dot(total, w_freq_t[:, :256])
        im = dot(delta, w_freq_t[:, 128:])
        mid = jnp.where(lanes_below((tile, 128), 64), re[:, 128:], im[:, :128])
        z[rows, :] = jnp.concatenate([re[:, :128], mid, im[:, 128:]], 1).astype(BF)
        return carry

    def second(k, carry):
        rows = pl.ds(pl.multiple_of(k * tile, tile), tile)
        sent[rows, :] = (turned(dot(tc[rows, :], z[...]), dot(ts[rows, :], z[...]), -1.0) * norm).astype(BF)
        return carry

    steps = got.shape[0] // tile
    lax.fori_loop(0, steps, first, 0)
    lax.fori_loop(0, steps, second, 0)
    grad[0:192, :] = acc_p[0:192, :].astype(BF)
    grad[192:256, :] = acc_m[64:128, :].astype(BF)
    grad[256:384, :] = acc_m[128:256, :].astype(BF)


def imag_first(got):
    mid = pltpu.roll(got[:, 128:256].astype(F32), 64, 1).astype(BF)
    return jnp.concatenate([got[:, 256:], mid], 1)


def middle_kernel(
    norm, cl, got, tct, tst, tc, ts, unit, pre, cot, w_out, w_out_t,
    output, d_out, d_joined, sent, grad, got_s, acc_c, acc_s, acc_g,
):
    y = pl.program_id(0)

    @pl.when(y == 0)
    def _():
        got_s[...] = imag_first(got[...])

    back = ((dot(tct[0], got[:, :256]) - dot(tst[0], got_s[...])) * norm).astype(BF)
    joined = (unit[0].astype(F32) + back.astype(F32)).astype(BF)
    pre_all = jnp.concatenate([pre[0, :, :cl], pre[0, :, cl:] + dot(joined, w_out[...])], 1)
    slope, silu = slope_and_silu(pre_all)
    output[0] = silu.astype(BF)
    d = (cot[...].reshape(-1, cot.shape[-1]).astype(F32) * slope).astype(BF)
    d_out[0] = d
    dj = dot(d[:, cl:], w_out_t[...]).astype(BF)
    d_joined[0] = dj
    g = dot(joined, d[:, cl:], ROWS_OF)

    @pl.when(y == 0)
    def _():
        acc_g[...] = g

    @pl.when(y > 0)
    def _():
        acc_g[...] += g

    transform_out(y, norm, dj, tc, ts, sent, acc_c, acc_s)

    @pl.when(y == pl.num_programs(0) - 1)
    def _():
        grad[...] = acc_g[0 : grad.shape[0], :].astype(BF)


def tail_kernel(
    norm, cl, got, tct, tst, masked, marked, d_joined, d_conv, w_in, w_in_t, grad_features, grad, got_s, acc_g
):
    y = pl.program_id(0)

    @pl.when(y == 0)
    def _():
        got_s[...] = imag_first(got[...])

    back = ((dot(tct[0], got[:, :256]) - dot(tst[0], got_s[...])) * norm).astype(BF)
    x = masked[0, :, cl:]
    slope = slope_and_silu(dot(x, w_in[...]))[0]
    du = ((d_joined[0].astype(F32) + back.astype(F32)) * slope).astype(BF)
    g = dot(x, du, ROWS_OF)

    @pl.when(y == 0)
    def _():
        acc_g[...] = g

    @pl.when(y > 0)
    def _():
        acc_g[...] += g

    keep = marked[...].reshape(-1, marked.shape[-1])[:, :1].astype(F32) < 0.5 * HOLE
    total = jnp.concatenate([d_conv[0, :, :cl], d_conv[0, :, cl:] + dot(du, w_in_t[...])], 1)
    grad_features[0] = jnp.where(keep, total, 0.0).astype(BF)

    @pl.when(y == pl.num_programs(0) - 1)
    def _():
        grad[...] = acc_g[...].astype(BF)


def shifted(x, step):
    n = x.shape[0]
    at = lax.broadcasted_iota(jnp.int32, x.shape, 0)
    if step == 1:
        return jnp.where(at == 0, 0.0, pltpu.roll(x, 1, 0))
    return jnp.where(at == n - 1, 0.0, pltpu.roll(x, n - 1, 0))


def three(x):
    f = x.astype(F32)
    return jnp.concatenate([shifted(f, -1).astype(BF), x, shifted(f, 1).astype(BF)], 1)


def conv_kernel(cl, above, masked, below, w_local, w_cross, pre, pad):
    y = pl.program_id(0)
    rows = masked.shape[0]

    @pl.when(y == 0)
    def _():
        pad[0] = above[0]
        pad[1 : rows + 1] = masked[...]
        pad[rows + 1] = below[0]

    local = dot(pad[y], w_local[0]) + dot(pad[y + 1], w_local[1]) + dot(pad[y + 2], w_local[2])
    near = jnp.concatenate([pad[y, :, :cl], pad[y + 1, :, :cl], pad[y + 2, :, :cl]], 1)
    cross = dot(near, w_cross[...])
    c, g = cl, w_cross.shape[1] // 3
    pre[0, :, :cl] = shifted(local[:, :c], 1) + local[:, c : 2 * c] + shifted(local[:, 2 * c :], -1)
    pre[0, :, cl:] = shifted(cross[:, :g], 1) + cross[:, g : 2 * g] + shifted(cross[:, 2 * g :], -1)


def conv_grad_kernel(cl, above, masked, below, d_out, g_local, g_cross, pad, acc_l, acc_c):
    y = pl.program_id(0)
    rows = masked.shape[0]

    @pl.when(y == 0)
    def _():
        pad[0] = above[0]
        pad[1 : rows + 1] = masked[...]
        pad[rows + 1] = below[0]
        acc_l[...] = jnp.zeros_like(acc_l)
        acc_c[...] = jnp.zeros_like(acc_c)

    d_local = three(d_out[0, :, :cl])
    d_global = three(d_out[0, :, cl:])
    g = d_global.shape[1] // 3
    for i in range(3):
        x = pad[y + i]
        acc_l[i] += dot(x, d_local, ROWS_OF)
        acc_c[i] += dot(x[:, :cl], d_global, ROWS_OF)

    @pl.when(y == pl.num_programs(0) - 1)
    def _():
        for i in range(3):
            g_local[i] = acc_l[i].astype(BF)
            for j in range(3):
                g_cross[i, j] = acc_c[i, :, j * g : (j + 1) * g].astype(BF)


def conv_back_kernel(cl, above, d_out, below, w_local, w_cross, d_conv, pad_l, pad_g):
    y = pl.program_id(0)
    rows = d_out.shape[0]

    @pl.when(y == 0)
    def _():
        for k in range(rows + 2):
            line = above[0] if k == 0 else below[0] if k == rows + 1 else d_out[k - 1]
            pad_l[k] = three(line[:, :cl])
            pad_g[k] = three(line[:, cl:])

    total = dot(pad_l[y + 2], w_local[0]) + dot(pad_l[y + 1], w_local[1]) + dot(pad_l[y], w_local[2])
    cross = dot(pad_g[y + 2], w_cross[0]) + dot(pad_g[y + 1], w_cross[1]) + dot(pad_g[y], w_cross[2])
    d_conv[0, :, :cl] = total[:, :cl] + cross
    d_conv[0, :, cl:] = total[:, cl:]


def swap(x, count):
    return lax.all_to_all(x.reshape(count, -1, x.shape[-1]), AXES, 0, 0, tiled=True).reshape(x.shape)


def to_rows(field, cols):
    h, w, c = field.shape
    return lax.all_to_all(field.reshape(cols, h // cols, w, c), "col", 0, 0, tiled=True)


def edges(field, count):
    down = lax.ppermute(field[-1:], AXES, [(i, i + 1) for i in range(count - 1)])
    up = lax.ppermute(field[:1], AXES, [(i + 1, i) for i in range(count - 1)])
    return down, up


def scatter_sum(x, count):
    x = lax.all_to_all(x.reshape(count, -1, x.shape[-1]), AXES, 0, 0, tiled=True)
    return x.astype(F32).sum(0).astype(BF)


def gather(x, count):
    x = lax.all_to_all(jnp.broadcast_to(x[None], (count,) + x.shape), AXES, 0, 0, tiled=True)
    return x.reshape(-1, x.shape[-1])


def tie(value, *after):
    return lax.optimization_barrier((value,) + after)[0]


def shards(features, hole_mask, cotangent, w_local, w_cross, w_in, w_freq, w_out):
    cols = lax.axis_size("col")
    count = lax.axis_size("row") * cols
    me = lax.axis_index(AXES)
    _, h, w, ch = features.shape
    rows, width = h // cols, w * cols
    height = rows * count
    cl, cg, cs = w_local.shape[3], w_cross.shape[3], w_in.shape[1]
    lines = -(-(width // 2 + 1) // count)
    slots = -(-(rows * lines) // 16) * 16
    n = count * slots
    tile = min(256, n)
    tc, ts = line_tables(rows, width, count, lines, slots)
    tct, tst = jnp.asarray(tc.transpose(0, 2, 1)), jnp.asarray(ts.transpose(0, 2, 1))
    tc, ts = jnp.asarray(tc), jnp.asarray(ts)
    hc, hs = (jnp.asarray(t) for t in column_tables(rows, count, lines, slots))
    norm_w, norm_h = 1.0 / math.sqrt(width), 1.0 / math.sqrt(height)
    freq = lines * me + jnp.arange(slots) % lines
    weight = jnp.where((freq == 0) | (freq * 2 == width), 0.5, jnp.where(freq * 2 < width, 1.0, 0.0))
    weight = jnp.tile(weight.astype(F32), count)[:, None]
    sign = np.where((np.arange(384) < 192), 1.0, -1.0).astype(np.float32)
    sign = jnp.asarray(sign[None])

    w_in_d = jnp.concatenate([w_in, w_in[:, 128:]], 1)
    w_in_t = jnp.pad(w_in.T, ((0, 64), (0, 0)))
    w_out_z = jnp.pad(w_out, ((0, 64), (0, 0)))
    w_out_t = jnp.concatenate([w_out, w_out[128:]], 0).T
    w_freq_p = pack_dim(pack_dim(w_freq, 0, cs), 1, cs)
    w_freq_t = w_freq_p.T
    wl = jnp.transpose(w_local, (0, 2, 1, 3)).reshape(3, ch, 3 * cl)
    wc = jnp.transpose(w_cross, (0, 2, 1, 3)).reshape(3 * cl, 3 * cg)
    wl_t = jnp.transpose(w_local, (0, 1, 3, 2)).reshape(3, 3 * cl, ch)
    wc_t = jnp.transpose(w_cross, (0, 1, 3, 2)).reshape(3, 3 * cg, cl)

    at_y = lambda y: (y, 0, 0)
    one_row = lambda c: (1, width, c)
    blocks = lambda c: (cols, 1, w, c)
    at_blocks = lambda y: (0, y, 0, 0)
    line_table = (1, n, width)
    back_table = (1, width, n)
    wide = (rows, width, ch)
    pix = rows * width
    vm = pltpu.VMEM

    marked = jnp.where(hole_mask[0][..., None] == 1, HOLE, features[0]).astype(BF)
    marked = to_rows(marked, cols)
    cot = to_rows(tie(cotangent[0], marked), cols)

    masked, unit, sent = call(
        functools.partial(head_kernel, norm_w, cl),
        "head",
        (rows,),
        [(marked, blocks(ch), at_blocks), (w_in_d, None, None), (tc, line_table, at_y), (ts, line_table, at_y)],
        [(wide, BF, one_row(ch), at_y), ((rows, width, 256), BF, one_row(256), at_y), ((n, 384), BF, None, None)],
        [vm((n, 256), F32), vm((n, 256), F32)],
        flops=4 * n * pix * 256, bytes_=12 << 20,
    )
    got = swap(sent, count)
    above, below = edges(masked, count)
    (pre,) = call(
        functools.partial(conv_kernel, cl),
        "conv",
        (rows,),
        [(above, None, None), (masked, None, None), (below, None, None), (wl, None, None), (wc, None, None)],
        [(wide, F32, one_row(ch), at_y)],
        [vm((rows + 2, width, ch), BF)],
        flops=18 * pix * (ch * cl + cl * cg), bytes_=9 << 20,
    )
    stacked, sent = call(
        functools.partial(frequency_kernel, norm_h, tile),
        "frequency",
        (1,),
        [(got, None, None), (hc, None, None), (hs, None, None), (w_freq_p, None, None), (weight, None, None), (sign, None, None)],
        [((n, 384), BF, None, None), ((n, 384), BF, None, None)],
        [vm((n, 384), BF)],
        flops=8 * n * n * 384, bytes_=7 << 20,
    )
    got = swap(sent, count)
    cot = tie(cot, got)
    output, d_out, d_joined, sent, grad_out = call(
        functools.partial(middle_kernel, norm_w, cl),
        "middle",
        (rows,),
        [
            (got, None, None), (tct, back_table, at_y), (tst, back_table, at_y), (tc, line_table, at_y),
            (ts, line_table, at_y), (unit, one_row(256), at_y), (pre, one_row(ch), at_y), (cot, blocks(ch), at_blocks),
            (w_out_z, None, None), (w_out_t, None, None),
        ],
        [
            (wide, BF, one_row(ch), at_y), (wide, BF, one_row(ch), at_y), ((rows, width, 256), BF, one_row(256), at_y),
            ((n, 384), BF, None, None), ((cs, cg), BF, None, None),
        ],
        [vm((n, 256), BF), vm((n, 256), F32), vm((n, 256), F32), vm((256, cg), F32)],
        flops=8 * n * pix * 256, bytes_=24 << 20,
    )
    got = swap(sent, count)
    grad_local, grad_cross = call(
        functools.partial(conv_grad_kernel, cl),
        "conv_grad",
        (rows,),
        [(above, None, None), (masked, None, None), (below, None, None), (d_out, one_row(ch), at_y)],
        [((3, ch, 3 * cl), BF, None, None), ((3, 3, cl, cg), BF, None, None)],
        [vm((rows + 2, width, ch), BF), vm((3, ch, 3 * cl), F32), vm((3, cl, 3 * cg), F32)],
        flops=18 * pix * (ch * cl + cl * cg), bytes_=7 << 20,
    )
    d_above, d_below = edges(d_out, count)
    got = tie(got, grad_local)
    sent, grad_freq = call(
        functools.partial(frequency_back_kernel, norm_h, tile),
        "frequency_back",
        (1,),
        [
            (got, None, None), (hc, None, None), (hs, None, None), (w_freq_p, None, None), (w_freq_t, None, None),
            (weight, None, None), (sign, None, None), (stacked, None, None),
        ],
        [((n, 384), BF, None, None), ((384, 384), BF, None, None)],
        [vm((n, 384), BF), vm((256, 384), F32), vm((256, 384), F32)],
        flops=8 * n * n * 384, bytes_=8 << 20,
    )
    got = swap(sent, count)
    pieces = [grad_local.reshape(-1, 384), grad_cross.reshape(-1, 384), grad_freq, grad_out]
    sizes = [p.shape[0] for p in pieces]
    room = -(-sum(sizes) // (16 * count)) * 16 * count
    early = scatter_sum(jnp.pad(jnp.concatenate(pieces, 0), ((0, room - sum(sizes)), (0, 0))), count)
    (d_conv,) = call(
        functools.partial(conv_back_kernel, cl),
        "conv_back",
        (rows,),
        [(d_above, None, None), (d_out, None, None), (d_below, None, None), (wl_t, None, None), (wc_t, None, None)],
        [(wide, F32, one_row(ch), at_y)],
        [vm((rows + 2, width, 3 * cl), BF), vm((rows + 2, width, 3 * cg), BF)],
        flops=18 * pix * (ch * cl + cl * cg), bytes_=9 << 20,
    )
    grad_features, grad_in = call(
        functools.partial(tail_kernel, norm_w, cl),
        "tail",
        (rows,),
        [
            (got, None, None), (tct, back_table, at_y), (tst, back_table, at_y), (masked, one_row(ch), at_y),
            (marked, blocks(128), at_blocks), (d_joined, one_row(256), at_y), (d_conv, one_row(ch), at_y),
            (w_in_d, None, None), (w_in_t, None, None),
        ],
        [(wide, BF, one_row(ch), at_y), ((cg, 256), BF, None, None)],
        [vm((n, 256), BF), vm((cg, 256), F32)],
        flops=4 * n * pix * 256, bytes_=16 << 20,
    )
    early = gather(early, count)
    outs, at = [], 0
    for size in sizes:
        outs.append(early[at : at + size].astype(F32))
        at += size
    grad_local, grad_cross, grad_freq, grad_out = outs
    late = gather(scatter_sum(grad_in[:, :cs].reshape(-1, 128), count), count)
    grad_in = late.reshape(cg, cs).astype(F32)
    grad_local = jnp.transpose(grad_local.reshape(3, ch, 3, cl), (0, 2, 1, 3))
    grad_cross = grad_cross.reshape(3, 3, cl, cg)
    grad_freq = unpack_dim(unpack_dim(grad_freq, 0, cs), 1, cs)
    return output[None], grad_features[None], grad_local, grad_cross, grad_in, grad_freq, grad_out


def solution(mesh):
    return jax.shard_map(
        shards,
        mesh=mesh,
        in_specs=(
            P("dp", "row", "col", None),
            P("dp", "row", "col"),
            P("dp", "row", "col", None),
            P(),
            P(),
            P(),
            P(),
            P(),
        ),
        out_specs=(
            P("dp", ("row", "col"), None, None),
            P("dp", ("row", "col"), None, None),
            P("dp", None, None, None),
            P("dp", None, None, None),
            P("dp", None),
            P("dp", None),
            P("dp", None),
        ),
        check_vma=False,
    )
```

```python
import functools
import math

import jax
import jax.numpy as jnp
import numpy as np
from jax import lax
from jax.experimental import pallas as pl
from jax.experimental.pallas import tpu as pltpu
from jax.sharding import PartitionSpec as P

AXES = ("row", "col")
HOLE = 64.0
BF = jnp.bfloat16
F32 = jnp.float32
ROWS_OF = ((0,), (0,))


def dot(a, b, dims=((1,), (0,))):
    return lax.dot_general(a, b, (dims, ((), ())), preferred_element_type=F32)


def line_tables(rows, width, count, lines, slots):
    cos = np.zeros((rows, count, slots, width), np.float32)
    sin = np.zeros((rows, count, slots, width), np.float32)
    freq = lines * np.arange(count)[:, None] + np.arange(lines)[None]
    angle = 2.0 * np.pi * (freq[..., None] * np.arange(width) % width) / width
    valid = (freq <= width // 2)[..., None]
    for y in range(rows):
        cos[y, :, y * lines : (y + 1) * lines] = np.cos(angle) * valid
        sin[y, :, y * lines : (y + 1) * lines] = np.sin(angle) * valid
    shape = (rows, count * slots, width)
    return cos.reshape(shape).astype(BF), sin.reshape(shape).astype(BF)


def column_tables(rows, count, lines, slots):
    height = rows * count
    cos = np.zeros((count, slots, count, slots), np.float32)
    sin = np.zeros((count, slots, count, slots), np.float32)
    h = np.arange(height).reshape(count, rows)
    angle = 2.0 * np.pi * (h[:, :, None, None] * h[None, None] % height) / height
    for y in range(rows):
        for z in range(rows):
            for j in range(lines):
                cos[:, y * lines + j, :, z * lines + j] = np.cos(angle[:, y, :, z])
                sin[:, y * lines + j, :, z * lines + j] = np.sin(angle[:, y, :, z])
    shape = (count * slots, count * slots)
    return cos.reshape(shape).astype(BF), sin.reshape(shape).astype(BF)


def slope_and_silu(value):
    sigma = 1.0 / (1.0 + jnp.exp(-value))
    return sigma * (1.0 + value * (1.0 - sigma)), value * sigma


def lanes_below(shape, bound):
    return lax.broadcasted_iota(jnp.int32, shape, 1) < bound


def packed(re, im):
    mid = jnp.where(lanes_below(re[:, 128:].shape, 64), re[:, 128:], im[:, 128:])
    return jnp.concatenate([re[:, :128], mid, im[:, :128]], 1)


def turned(p, q, sign):
    mid = pltpu.roll(q[:, 128:256], 64, 1)
    flip = jnp.where(lanes_below(mid.shape, 64), sign, -sign)
    return jnp.concatenate(
        [p[:, :128] + sign * q[:, 256:], p[:, 128:256] + flip * mid, p[:, 256:] - sign * q[:, :128]], 1
    )


def natural_lanes(x):
    mid, im = x[:, 128:256], pltpu.roll(x[:, 256:], 64, 1)
    low = lanes_below(mid.shape, 64)
    return jnp.concatenate([x[:, :128], jnp.where(low, mid, im), jnp.where(low, im, mid)], 1)


def pack_order(cs):
    return [(0, 128), (128, cs), (cs + 128, 2 * cs), (cs, cs + 128)]


def pack_dim(x, dim, cs):
    return jnp.concatenate([lax.slice_in_dim(x, a, b, axis=dim) for a, b in pack_order(cs)], dim)


def call(body, name, grid, ins, outs, scratch=(), flops=0, bytes_=0):
    def spec(shape, block, index):
        if shape == (1, 1):
            return pl.BlockSpec(memory_space=pltpu.SMEM)
        if block is None:
            zeros = (0,) * len(shape)
            return pl.BlockSpec(shape, lambda *_: zeros)
        return pl.BlockSpec(block, index)

    return pl.pallas_call(
        body,
        grid=grid,
        in_specs=[spec(a.shape, block, index) for a, block, index in ins],
        out_specs=[spec(shape, block, index) for shape, _, block, index in outs],
        out_shape=[jax.ShapeDtypeStruct(shape, dtype) for shape, dtype, _, _ in outs],
        scratch_shapes=list(scratch),
        compiler_params=pltpu.CompilerParams(vmem_limit_bytes=56 << 20),
        cost_estimate=pl.CostEstimate(flops=flops, bytes_accessed=bytes_, transcendentals=0),
        name=name,
    )(*[a for a, _, _ in ins])


def head_kernel(norm, cl, marked, w_in, tc, ts, masked, unit, sent, acc_c, acc_s):
    y = pl.program_id(0)
    x = marked[...].reshape(-1, marked.shape[-1])
    keep = x[:, :1].astype(F32) < 0.5 * HOLE
    x = jnp.where(keep, x, jnp.zeros_like(x))
    masked[0] = x
    u = slope_and_silu(dot(x[:, cl:], w_in[...]))[1].astype(BF)
    unit[0] = u
    transform_out(y, norm, u, tc, ts, sent, acc_c, acc_s)


def transform_out(y, norm, u, tc, ts, sent, acc_c, acc_s):
    re, im = dot(tc[0], u), dot(ts[0], u)

    @pl.when(y == 0)
    def _():
        acc_c[...] = re
        acc_s[...] = im

    @pl.when(y > 0)
    def _():
        acc_c[...] += re
        acc_s[...] += im

    @pl.when(y == pl.num_programs(0) - 1)
    def _():
        sent[...] = packed(acc_c[...] * norm, acc_s[...] * -norm).astype(BF)


def frequency_kernel(norm, tile, got, tc, ts, w_freq, weight, sign, stacked, sent, z):
    def first(k, carry):
        rows = pl.ds(pl.multiple_of(k * tile, tile), tile)
        spec = turned(dot(tc[rows, :], got[...]), dot(ts[rows, :], got[...]), 1.0) * norm
        st = spec.astype(BF)
        stacked[rows, :] = st
        pos = slope_and_silu(dot(st, w_freq[...]))[1]
        neg = slope_and_silu(dot((st.astype(F32) * sign[...]).astype(BF), w_freq[...]))[1]
        z[rows, :] = (weight[rows, :] * (pos + sign[...] * neg)).astype(BF)
        return carry

    def second(k, carry):
        rows = pl.ds(pl.multiple_of(k * tile, tile), tile)
        sent[rows, :] = (turned(dot(tc[rows, :], z[...]), dot(ts[rows, :], z[...]), -1.0) * norm).astype(BF)
        return carry

    steps = got.shape[0] // tile
    lax.fori_loop(0, steps, first, 0)
    lax.fori_loop(0, steps, second, 0)


def frequency_back_kernel(
    norm, tile, got, tc, ts, w_freq, w_freq_t, weight, sign, stacked, sent, grad, z, acc_p, acc_m
):
    acc_p[...] = jnp.zeros_like(acc_p)
    acc_m[...] = jnp.zeros_like(acc_m)

    def first(k, carry):
        rows = pl.ds(pl.multiple_of(k * tile, tile), tile)
        dz = turned(dot(tc[rows, :], got[...]), dot(ts[rows, :], got[...]), 1.0) * norm
        st = stacked[rows, :]
        pos = slope_and_silu(dot(st, w_freq[...]))[0]
        neg = slope_and_silu(dot((st.astype(F32) * sign[...]).astype(BF), w_freq[...]))[0]
        pos = (dz * pos).astype(BF).astype(F32)
        neg = (dz * sign[...] * neg).astype(BF).astype(F32)
        total = (weight[rows, :] * (pos + neg)).astype(BF)
        delta = (weight[rows, :] * (pos - neg)).astype(BF)
        acc_p[...] += dot(st[:, :256], total, ROWS_OF)
        acc_m[...] += dot(st[:, 128:], delta, ROWS_OF)
        re = dot(total, w_freq_t[:, :256])
        im = dot(delta, w_freq_t[:, 128:])
        mid = jnp.where(lanes_below((tile, 128), 64), re[:, 128:], im[:, :128])
        z[rows, :] = jnp.concatenate([re[:, :128], mid, im[:, 128:]], 1).astype(BF)
        return carry

    def second(k, carry):
        rows = pl.ds(pl.multiple_of(k * tile, tile), tile)
        sent[rows, :] = (turned(dot(tc[rows, :], z[...]), dot(ts[rows, :], z[...]), -1.0) * norm).astype(BF)
        return carry

    steps = got.shape[0] // tile
    lax.fori_loop(0, steps, first, 0)
    lax.fori_loop(0, steps, second, 0)
    grad[0:192, :] = natural_lanes(acc_p[0:192, :]).astype(BF)
    grad[192:320, :] = natural_lanes(acc_m[128:256, :]).astype(BF)
    grad[320:384, :] = natural_lanes(acc_m[64:128, :]).astype(BF)


def imag_first(got):
    mid = pltpu.roll(got[:, 128:256].astype(F32), 64, 1).astype(BF)
    return jnp.concatenate([got[:, 256:], mid], 1)


def middle_kernel(
    norm, cl, cols, got, tct, tst, tc, ts, unit, pre, w_out, w_out_t, my_col, *refs,
):
    cots = refs[:cols]
    output, d_out, d_joined, sent, grad, got_s, cot, acc_c, acc_s, acc_g = refs[cols:]
    y = pl.program_id(0)
    w = cots[0].shape[1]
    for k in range(cols):
        at = lax.rem(my_col[0, 0] + (cols - k), cols)
        cot[pl.ds(pl.multiple_of(at * w, w), w), :] = cots[k][0]

    @pl.when(y == 0)
    def _():
        got_s[...] = imag_first(got[...])

    back = ((dot(tct[0], got[:, :256]) - dot(tst[0], got_s[...])) * norm).astype(BF)
    joined = (unit[0].astype(F32) + back.astype(F32)).astype(BF)
    pre_all = jnp.concatenate([pre[0, :, :cl], pre[0, :, cl:] + dot(joined, w_out[...])], 1)
    slope, silu = slope_and_silu(pre_all)
    output[0] = silu.astype(BF)
    d = (cot[...].astype(F32) * slope).astype(BF)
    d_out[0] = d
    dj = dot(d[:, cl:], w_out_t[...]).astype(BF)
    d_joined[0] = dj
    g = dot(joined, d[:, cl:], ROWS_OF)

    @pl.when(y == 0)
    def _():
        acc_g[...] = g

    @pl.when(y > 0)
    def _():
        acc_g[...] += g

    transform_out(y, norm, dj, tc, ts, sent, acc_c, acc_s)

    @pl.when(y == pl.num_programs(0) - 1)
    def _():
        grad[...] = acc_g[0 : grad.shape[0], :].astype(BF)


def tail_kernel(
    norm, cl, got, tct, tst, masked, marked, d_joined, d_conv, w_in, w_in_t, grad_freq,
    grad_features, late, got_s, acc_g,
):
    y = pl.program_id(0)

    @pl.when(y == 0)
    def _():
        got_s[...] = imag_first(got[...])

    back = ((dot(tct[0], got[:, :256]) - dot(tst[0], got_s[...])) * norm).astype(BF)
    x = masked[0, :, cl:]
    slope = slope_and_silu(dot(x, w_in[...]))[0]
    du = ((d_joined[0].astype(F32) + back.astype(F32)) * slope).astype(BF)
    g = dot(du, x, ROWS_OF)

    @pl.when(y == 0)
    def _():
        acc_g[...] = g

    @pl.when(y > 0)
    def _():
        acc_g[...] += g

    keep = marked[...].reshape(-1, marked.shape[-1])[:, :1].astype(F32) < 0.5 * HOLE
    total = jnp.concatenate([d_conv[0, :, :cl], d_conv[0, :, cl:] + dot(du, w_in_t[...])], 1)
    grad_features[0] = jnp.where(keep, total, 0.0).astype(BF)

    @pl.when(y == pl.num_programs(0) - 1)
    def _():
        at = 0
        for part, size in ((grad_freq, 384), (acc_g, 192)):
            for k in range(3):
                late[at : at + size, :] = part[0:size, k * 128 : (k + 1) * 128].astype(BF)
                at += size
        late[at:, :] = jnp.zeros((late.shape[0] - at, 128), BF)


def shifted(x, step):
    n = x.shape[0]
    at = lax.broadcasted_iota(jnp.int32, x.shape, 0)
    if step == 1:
        return jnp.where(at == 0, 0.0, pltpu.roll(x, 1, 0))
    return jnp.where(at == n - 1, 0.0, pltpu.roll(x, n - 1, 0))


def three(x):
    f = x.astype(F32)
    return jnp.concatenate([shifted(f, -1).astype(BF), x, shifted(f, 1).astype(BF)], 1)


def conv_kernel(cl, above, masked, below, w_local, w_cross, pre, pad):
    y = pl.program_id(0)
    rows = masked.shape[0]

    @pl.when(y == 0)
    def _():
        pad[0] = above[0]
        pad[1 : rows + 1] = masked[...]
        pad[rows + 1] = below[0]

    local = dot(pad[y], w_local[0]) + dot(pad[y + 1], w_local[1]) + dot(pad[y + 2], w_local[2])
    near = jnp.concatenate([pad[y, :, :cl], pad[y + 1, :, :cl], pad[y + 2, :, :cl]], 1)
    cross = dot(near, w_cross[...])
    c, g = cl, w_cross.shape[1] // 3
    pre[0, :, :cl] = shifted(local[:, :c], 1) + local[:, c : 2 * c] + shifted(local[:, 2 * c :], -1)
    pre[0, :, cl:] = shifted(cross[:, :g], 1) + cross[:, g : 2 * g] + shifted(cross[:, 2 * g :], -1)


def conv_grad_kernel(cl, above, masked, below, d_out, g_out, early, pad, acc_l, acc_c):
    y = pl.program_id(0)
    rows = masked.shape[0]

    @pl.when(y == 0)
    def _():
        pad[0] = above[0]
        pad[1 : rows + 1] = masked[...]
        pad[rows + 1] = below[0]
        acc_l[...] = jnp.zeros_like(acc_l)
        acc_c[...] = jnp.zeros_like(acc_c)

    d_local = three(d_out[0, :, :cl])
    d_global = three(d_out[0, :, cl:])
    g = d_global.shape[1] // 3
    for i in range(3):
        x = pad[y + i]
        acc_l[i] += dot(x, d_local, ROWS_OF)
        acc_c[i] += dot(x[:, :cl], d_global, ROWS_OF)

    @pl.when(y == pl.num_programs(0) - 1)
    def _():
        ch = masked.shape[2]
        for i in range(3):
            early[0, i * ch : (i + 1) * ch, :] = acc_l[i].astype(BF)
            for j in range(3):
                at = (3 * i + j) * cl
                early[1, at : at + cl, :] = acc_c[i, :, j * g : (j + 1) * g].astype(BF)
        at, size = 9 * cl, g_out.shape[0]
        early[1, at : at + size, :] = g_out[...]
        early[1, at + size :, :] = jnp.zeros((early.shape[1] - at - size, g), BF)


def unpack_kernel(cl, got, g_local, g_cross, g_out):
    rows, ch = got.shape[2], g_local.shape[2]
    for at in range(0, 3 * ch, 64):
        block = got[at // rows, 0, at % rows : at % rows + 64, :].astype(F32)
        for j in range(3):
            g_local[at // ch, j, at % ch : at % ch + 64, :] = block[:, j * cl : (j + 1) * cl]
    for at in range(0, 9 * cl + g_out.shape[0], 64):
        block = got[at // rows, 1, at % rows : at % rows + 64, :].astype(F32)
        if at < 9 * cl:
            g_cross[at : at + 64, :] = block
        else:
            g_out[at - 9 * cl : at - 9 * cl + 64, :] = block


def conv_back_kernel(cl, above, d_out, below, w_local, w_cross, d_conv, pad_l, pad_g):
    y = pl.program_id(0)
    rows = d_out.shape[0]

    @pl.when(y == 0)
    def _():
        for k in range(rows + 2):
            line = above[0] if k == 0 else below[0] if k == rows + 1 else d_out[k - 1]
            pad_l[k] = three(line[:, :cl])
            pad_g[k] = three(line[:, cl:])

    total = dot(pad_l[y + 2], w_local[0]) + dot(pad_l[y + 1], w_local[1]) + dot(pad_l[y], w_local[2])
    cross = dot(pad_g[y + 2], w_cross[0]) + dot(pad_g[y + 1], w_cross[1]) + dot(pad_g[y], w_cross[2])
    d_conv[0, :, :cl] = total[:, :cl] + cross
    d_conv[0, :, cl:] = total[:, cl:]


def swap(x, count):
    return lax.all_to_all(x.reshape(count, -1, x.shape[-1]), AXES, 0, 0, tiled=True).reshape(x.shape)


def to_rows(field, cols):
    h, w, c = field.shape
    return lax.all_to_all(field.reshape(cols, h // cols, w, c), "col", 0, 0, tiled=True)


def turn(field, cols):
    h, w, c = field.shape
    blocks = field.reshape(cols, h // cols, w, c)
    me = lax.axis_index("col")
    out = []
    for k in range(cols):
        part = lax.dynamic_index_in_dim(blocks, (me + k) % cols, 0, keepdims=False)
        out.append(lax.ppermute(part, "col", [(i, (i + k) % cols) for i in range(cols)]) if k else part)
    return out


def reduce_halves(early, count):
    pairs = lax.axis_size("row")
    cols = count // pairs
    core = lax.axis_index("row") % 2
    mine = lax.dynamic_index_in_dim(early, core, 0, keepdims=False)
    other = lax.dynamic_index_in_dim(early, 1 - core, 0, keepdims=False)
    other = lax.ppermute(other, "row", [(i, i ^ 1) for i in range(pairs)])
    total = (mine.astype(F32) + other.astype(F32)).astype(BF)
    groups = [[cols * r + c for r in range(k, pairs, 2) for c in range(cols)] for k in range(2)]
    got = lax.all_to_all(
        total.reshape(count // 2, -1, total.shape[-1]), AXES, 0, 0, axis_index_groups=groups, tiled=True
    )
    return total, got


def gather_halves(x, cols):
    me = lax.axis_index("col")
    parts = [x]
    for k in range(1, cols):
        parts.append(lax.ppermute(x, "col", [((i + k) % cols, i) for i in range(cols)]))
    both = jnp.concatenate(parts + parts[:-1], 0)
    size = x.shape[0]
    x = lax.dynamic_slice_in_dim(both, (cols - me) % cols * size, cols * size, 0)
    x = lax.all_gather(x, "row", axis=0)
    return x.reshape(x.shape[0] // 2, 2, *x.shape[1:])


def edges(field, count):
    down = lax.ppermute(field[-1:], AXES, [(i, i + 1) for i in range(count - 1)])
    up = lax.ppermute(field[:1], AXES, [(i + 1, i) for i in range(count - 1)])
    return down, up


def scatter_sum(x, count):
    x = lax.all_to_all(x.reshape(count, -1, x.shape[-1]), AXES, 0, 0, tiled=True)
    return x.astype(F32).sum(0).astype(BF)


def gather(x, count):
    x = lax.all_to_all(jnp.broadcast_to(x[None], (count,) + x.shape), AXES, 0, 0, tiled=True)
    return x.reshape(-1, x.shape[-1])


def tie(value, *after):
    return lax.optimization_barrier((value,) + after)[0]


def tied(*values):
    return lax.optimization_barrier(values)


def shards(features, hole_mask, cotangent, w_local, w_cross, w_in, w_freq, w_out):
    cols = lax.axis_size("col")
    count = lax.axis_size("row") * cols
    me = lax.axis_index(AXES)
    _, h, w, ch = features.shape
    rows, width = h // cols, w * cols
    height = rows * count
    cl, cg, cs = w_local.shape[3], w_cross.shape[3], w_in.shape[1]
    lines = -(-(width // 2 + 1) // count)
    slots = -(-(rows * lines) // 16) * 16
    n = count * slots
    tile = min(256, n)
    tc, ts = line_tables(rows, width, count, lines, slots)
    tct, tst = jnp.asarray(tc.transpose(0, 2, 1)), jnp.asarray(ts.transpose(0, 2, 1))
    tc, ts = jnp.asarray(tc), jnp.asarray(ts)
    hc, hs = (jnp.asarray(t) for t in column_tables(rows, count, lines, slots))
    norm_w, norm_h = 1.0 / math.sqrt(width), 1.0 / math.sqrt(height)
    freq = lines * me + jnp.arange(slots) % lines
    weight = jnp.where((freq == 0) | (freq * 2 == width), 0.5, jnp.where(freq * 2 < width, 1.0, 0.0))
    weight = jnp.tile(weight.astype(F32), count)[:, None]
    sign = np.where((np.arange(384) < 192), 1.0, -1.0).astype(np.float32)
    sign = jnp.asarray(sign[None])

    w_in_d = jnp.concatenate([w_in, w_in[:, 128:]], 1)
    w_in_t = jnp.pad(w_in.T, ((0, 64), (0, 0)))
    w_out_z = jnp.pad(w_out, ((0, 64), (0, 0)))
    w_out_t = jnp.concatenate([w_out, w_out[128:]], 0).T
    w_freq_p = pack_dim(pack_dim(w_freq, 0, cs), 1, cs)
    w_freq_t = w_freq_p.T
    wl = jnp.transpose(w_local, (0, 2, 1, 3)).reshape(3, ch, 3 * cl)
    wc = jnp.transpose(w_cross, (0, 2, 1, 3)).reshape(3 * cl, 3 * cg)
    wl_t = jnp.transpose(w_local, (0, 1, 3, 2)).reshape(3, 3 * cl, ch)
    wc_t = jnp.transpose(w_cross, (0, 1, 3, 2)).reshape(3, 3 * cg, cl)

    at_y = lambda y: (y, 0, 0)
    one_row = lambda c: (1, width, c)
    blocks = lambda c: (cols, 1, w, c)
    at_blocks = lambda y: (0, y, 0, 0)
    line_table = (1, n, width)
    back_table = (1, width, n)
    wide = (rows, width, ch)
    pix = rows * width
    vm = pltpu.VMEM

    marked = jnp.where(hole_mask[0][..., None] == 1, HOLE, features[0]).astype(BF)
    marked = to_rows(marked, cols)
    w_in_d, w_in_t, w_out_z, w_out_t, w_freq_p, w_freq_t, wl, wc, wl_t, wc_t, weight = tied(
        w_in_d, w_in_t, w_out_z, w_out_t, w_freq_p, w_freq_t, wl, wc, wl_t, wc_t, weight
    )
    cots = turn(tie(cotangent[0], marked), cols)
    my_col = lax.axis_index("col").astype(jnp.int32).reshape(1, 1)

    masked, unit, sent = call(
        functools.partial(head_kernel, norm_w, cl),
        "head",
        (rows,),
        [(marked, blocks(ch), at_blocks), (w_in_d, None, None), (tc, line_table, at_y), (ts, line_table, at_y)],
        [(wide, BF, one_row(ch), at_y), ((rows, width, 256), BF, one_row(256), at_y), ((n, 384), BF, None, None)],
        [vm((n, 256), F32), vm((n, 256), F32)],
        flops=4 * n * pix * 256, bytes_=12 << 20,
    )
    above, below = edges(masked, count)
    got = tie(swap(sent, count), above, below)
    (pre,) = call(
        functools.partial(conv_kernel, cl),
        "conv",
        (rows,),
        [(above, None, None), (masked, None, None), (below, None, None), (wl, None, None), (wc, None, None)],
        [(wide, F32, one_row(ch), at_y)],
        [vm((rows + 2, width, ch), BF)],
        flops=18 * pix * (ch * cl + cl * cg), bytes_=9 << 20,
    )
    stacked, sent = call(
        functools.partial(frequency_kernel, norm_h, tile),
        "frequency",
        (1,),
        [(got, None, None), (hc, None, None), (hs, None, None), (w_freq_p, None, None), (weight, None, None), (sign, None, None)],
        [((n, 384), BF, None, None), ((n, 384), BF, None, None)],
        [vm((n, 384), BF)],
        flops=8 * n * n * 384, bytes_=7 << 20,
    )
    sent, *cots = tied(sent, *cots)
    got = swap(sent, count)
    output, d_out, d_joined, sent, grad_out = call(
        functools.partial(middle_kernel, norm_w, cl, cols),
        "middle",
        (rows,),
        [
            (got, None, None), (tct, back_table, at_y), (tst, back_table, at_y), (tc, line_table, at_y),
            (ts, line_table, at_y), (unit, one_row(256), at_y), (pre, one_row(ch), at_y),
            (w_out_z, None, None), (w_out_t, None, None), (my_col, None, None),
        ]
        + [(c, (1, w, ch), at_y) for c in cots],
        [
            (wide, BF, one_row(ch), at_y), (wide, BF, one_row(ch), at_y), ((rows, width, 256), BF, one_row(256), at_y),
            ((n, 384), BF, None, None), ((cs, cg), BF, None, None),
        ],
        [vm((n, 256), BF), vm((width, ch), BF), vm((n, 256), F32), vm((n, 256), F32), vm((256, cg), F32)],
        flops=8 * n * pix * 256, bytes_=24 << 20,
    )
    got = swap(sent, count)
    d_above, d_below = edges(d_out, count)
    (early,) = call(
        functools.partial(conv_grad_kernel, cl),
        "conv_grad",
        (rows,),
        [(above, None, None), (masked, None, None), (below, None, None), (d_out, one_row(ch), at_y), (grad_out, None, None)],
        [((2, 3 * ch, 384), BF, None, None)],
        [vm((rows + 2, width, ch), BF), vm((3, ch, 3 * cl), F32), vm((3, cl, 3 * cg), F32)],
        flops=18 * pix * (ch * cl + cl * cg), bytes_=7 << 20,
    )
    total, early = reduce_halves(early, count)
    got = tied(got, d_above, d_below, total)[0]
    sent, grad_freq = call(
        functools.partial(frequency_back_kernel, norm_h, tile),
        "frequency_back",
        (1,),
        [
            (got, None, None), (hc, None, None), (hs, None, None), (w_freq_p, None, None), (w_freq_t, None, None),
            (weight, None, None), (sign, None, None), (stacked, None, None),
        ],
        [((n, 384), BF, None, None), ((384, 384), BF, None, None)],
        [vm((n, 384), BF), vm((256, 384), F32), vm((256, 384), F32)],
        flops=8 * n * n * 384, bytes_=8 << 20,
    )
    early = early.astype(F32).sum(0).astype(BF)
    sent, early = tied(sent, early)
    got = swap(sent, count)
    early = gather_halves(early, cols)
    (d_conv,) = call(
        functools.partial(conv_back_kernel, cl),
        "conv_back",
        (rows,),
        [(d_above, None, None), (d_out, None, None), (d_below, None, None), (wl_t, None, None), (wc_t, None, None)],
        [(wide, F32, one_row(ch), at_y)],
        [vm((rows + 2, width, 3 * cl), BF), vm((rows + 2, width, 3 * cg), BF)],
        flops=18 * pix * (ch * cl + cl * cg), bytes_=9 << 20,
    )
    got = tie(got, d_conv)
    late_rows = -(-(3 * 384 + 3 * cs) // (16 * count)) * 16 * count
    grad_features, late = call(
        functools.partial(tail_kernel, norm_w, cl),
        "tail",
        (rows,),
        [
            (got, None, None), (tct, back_table, at_y), (tst, back_table, at_y), (masked, one_row(ch), at_y),
            (marked, blocks(128), at_blocks), (d_joined, one_row(256), at_y), (d_conv, one_row(ch), at_y),
            (w_in_d, None, None), (w_in_t, None, None), (grad_freq, None, None),
        ],
        [(wide, BF, one_row(ch), at_y), ((late_rows, 128), BF, None, None)],
        [vm((n, 256), BF), vm((256, cg), F32)],
        flops=4 * n * pix * 256, bytes_=16 << 20,
    )
    late = scatter_sum(late, count)
    grad_local, grad_cross, grad_out = call(
        functools.partial(unpack_kernel, cl),
        "unpack",
        (1,),
        [(early, None, None)],
        [((3, 3, ch, cl), F32, None, None), ((9 * cl, cg), F32, None, None), ((cs, cg), F32, None, None)],
        flops=1, bytes_=7 << 20,
    )
    late = gather(late, count)
    grad_freq = jnp.concatenate([late[k * 384 : (k + 1) * 384] for k in range(3)], 1).astype(F32)
    at = 3 * 384
    grad_in = jnp.concatenate([late[at + k * cs : at + (k + 1) * cs] for k in range(3)], 1).astype(F32).T
    grad_cross = grad_cross.reshape(3, 3, cl, cg)
    return output[None], grad_features[None], grad_local, grad_cross, grad_in, grad_freq, grad_out


def solution(mesh):
    return jax.shard_map(
        shards,
        mesh=mesh,
        in_specs=(
            P("dp", "row", "col", None),
            P("dp", "row", "col"),
            P("dp", "row", "col", None),
            P(),
            P(),
            P(),
            P(),
            P(),
        ),
        out_specs=(
            P("dp", ("row", "col"), None, None),
            P("dp", ("row", "col"), None, None),
            P("dp", None, None, None),
            P("dp", None, None, None),
            P("dp", None),
            P("dp", None),
            P("dp", None),
        ),
        check_vma=False,
    )
```

```python
import functools
import math

import jax
import jax.numpy as jnp
import numpy as np
from jax import lax
from jax.experimental import pallas as pl
from jax.experimental.pallas import tpu as pltpu
from jax.sharding import PartitionSpec as P

AXES = ("row", "col")
HOLE = 64.0
BF = jnp.bfloat16
F32 = jnp.float32
ROWS_OF = ((0,), (0,))


def dot(a, b, dims=((1,), (0,))):
    return lax.dot_general(a, b, (dims, ((), ())), preferred_element_type=F32)


def line_tables(rows, width, count, lines, slots):
    cos = np.zeros((rows, count, slots, width), np.float32)
    sin = np.zeros((rows, count, slots, width), np.float32)
    freq = lines * np.arange(count)[:, None] + np.arange(lines)[None]
    angle = 2.0 * np.pi * (freq[..., None] * np.arange(width) % width) / width
    valid = (freq <= width // 2)[..., None]
    for y in range(rows):
        cos[y, :, y * lines : (y + 1) * lines] = np.cos(angle) * valid
        sin[y, :, y * lines : (y + 1) * lines] = np.sin(angle) * valid
    shape = (rows, count * slots, width)
    return cos.reshape(shape).astype(BF), sin.reshape(shape).astype(BF)


def column_tables(rows, count, lines, slots):
    height = rows * count
    cos = np.zeros((count, slots, count, slots), np.float32)
    sin = np.zeros((count, slots, count, slots), np.float32)
    h = np.arange(height).reshape(count, rows)
    angle = 2.0 * np.pi * (h[:, :, None, None] * h[None, None] % height) / height
    for y in range(rows):
        for z in range(rows):
            for j in range(lines):
                cos[:, y * lines + j, :, z * lines + j] = np.cos(angle[:, y, :, z])
                sin[:, y * lines + j, :, z * lines + j] = np.sin(angle[:, y, :, z])
    shape = (count * slots, count * slots)
    return cos.reshape(shape).astype(BF), sin.reshape(shape).astype(BF)


def slope_and_silu(value):
    sigma = 1.0 / (1.0 + jnp.exp(-value))
    return sigma * (1.0 + value * (1.0 - sigma)), value * sigma


def lanes_below(shape, bound):
    return lax.broadcasted_iota(jnp.int32, shape, 1) < bound


def packed(re, im):
    mid = jnp.where(lanes_below(re[:, 128:].shape, 64), re[:, 128:], im[:, 128:])
    return jnp.concatenate([re[:, :128], mid, im[:, :128]], 1)


def turned(p, q, sign):
    mid = pltpu.roll(q[:, 128:256], 64, 1)
    flip = jnp.where(lanes_below(mid.shape, 64), sign, -sign)
    return jnp.concatenate(
        [p[:, :128] + sign * q[:, 256:], p[:, 128:256] + flip * mid, p[:, 256:] - sign * q[:, :128]], 1
    )


def natural_lanes(x):
    mid, im = x[:, 128:256], pltpu.roll(x[:, 256:], 64, 1)
    low = lanes_below(mid.shape, 64)
    return jnp.concatenate([x[:, :128], jnp.where(low, mid, im), jnp.where(low, im, mid)], 1)


def pack_order(cs):
    return [(0, 128), (128, cs), (cs + 128, 2 * cs), (cs, cs + 128)]


def pack_dim(x, dim, cs):
    return jnp.concatenate([lax.slice_in_dim(x, a, b, axis=dim) for a, b in pack_order(cs)], dim)


def call(body, name, grid, ins, outs, scratch=(), flops=0, bytes_=0):
    def spec(shape, block, index):
        if shape == (1, 1):
            return pl.BlockSpec(memory_space=pltpu.SMEM)
        if block is None:
            zeros = (0,) * len(shape)
            return pl.BlockSpec(shape, lambda *_: zeros)
        return pl.BlockSpec(block, index)

    return pl.pallas_call(
        body,
        grid=grid,
        in_specs=[spec(a.shape, block, index) for a, block, index in ins],
        out_specs=[spec(shape, block, index) for shape, _, block, index in outs],
        out_shape=[jax.ShapeDtypeStruct(shape, dtype) for shape, dtype, _, _ in outs],
        scratch_shapes=list(scratch),
        compiler_params=pltpu.CompilerParams(vmem_limit_bytes=56 << 20),
        cost_estimate=pl.CostEstimate(flops=flops, bytes_accessed=bytes_, transcendentals=0),
        name=name,
    )(*[a for a, _, _ in ins])


def head_kernel(norm, cl, marked, w_in, tc, ts, masked, unit, sent, acc_c, acc_s):
    y = pl.program_id(0)
    x = marked[...].reshape(-1, marked.shape[-1])
    keep = x[:, :1].astype(F32) < 0.5 * HOLE
    x = jnp.where(keep, x, jnp.zeros_like(x))
    masked[0] = x
    u = slope_and_silu(dot(x[:, cl:], w_in[...]))[1].astype(BF)
    unit[0] = u
    transform_out(y, norm, u, tc, ts, sent, acc_c, acc_s)


def transform_out(y, norm, u, tc, ts, sent, acc_c, acc_s):
    re, im = dot(tc[0], u), dot(ts[0], u)

    @pl.when(y == 0)
    def _():
        acc_c[...] = re
        acc_s[...] = im

    @pl.when(y > 0)
    def _():
        acc_c[...] += re
        acc_s[...] += im

    @pl.when(y == pl.num_programs(0) - 1)
    def _():
        sent[...] = packed(acc_c[...] * norm, acc_s[...] * -norm).astype(BF)


def frequency_kernel(norm, tile, got, tc, ts, w_freq, weight, sign, stacked, sent, z):
    def first(k, carry):
        rows = pl.ds(pl.multiple_of(k * tile, tile), tile)
        spec = turned(dot(tc[rows, :], got[...]), dot(ts[rows, :], got[...]), 1.0) * norm
        st = spec.astype(BF)
        stacked[rows, :] = st
        pos = slope_and_silu(dot(st, w_freq[...]))[1]
        neg = slope_and_silu(dot((st.astype(F32) * sign[...]).astype(BF), w_freq[...]))[1]
        z[rows, :] = (weight[rows, :] * (pos + sign[...] * neg)).astype(BF)
        return carry

    def second(k, carry):
        rows = pl.ds(pl.multiple_of(k * tile, tile), tile)
        sent[rows, :] = (turned(dot(tc[rows, :], z[...]), dot(ts[rows, :], z[...]), -1.0) * norm).astype(BF)
        return carry

    steps = got.shape[0] // tile
    lax.fori_loop(0, steps, first, 0)
    lax.fori_loop(0, steps, second, 0)


def frequency_back_kernel(
    norm, tile, got, tc, ts, w_freq, w_freq_t, weight, sign, stacked, sent, grad, z, acc_p, acc_m
):
    acc_p[...] = jnp.zeros_like(acc_p)
    acc_m[...] = jnp.zeros_like(acc_m)

    def first(k, carry):
        rows = pl.ds(pl.multiple_of(k * tile, tile), tile)
        dz = turned(dot(tc[rows, :], got[...]), dot(ts[rows, :], got[...]), 1.0) * norm
        st = stacked[rows, :]
        pos = slope_and_silu(dot(st, w_freq[...]))[0]
        neg = slope_and_silu(dot((st.astype(F32) * sign[...]).astype(BF), w_freq[...]))[0]
        pos = (dz * pos).astype(BF).astype(F32)
        neg = (dz * sign[...] * neg).astype(BF).astype(F32)
        total = (weight[rows, :] * (pos + neg)).astype(BF)
        delta = (weight[rows, :] * (pos - neg)).astype(BF)
        acc_p[...] += dot(st[:, :256], total, ROWS_OF)
        acc_m[...] += dot(st[:, 128:], delta, ROWS_OF)
        re = dot(total, w_freq_t[:, :256])
        im = dot(delta, w_freq_t[:, 128:])
        mid = jnp.where(lanes_below((tile, 128), 64), re[:, 128:], im[:, :128])
        z[rows, :] = jnp.concatenate([re[:, :128], mid, im[:, 128:]], 1).astype(BF)
        return carry

    def second(k, carry):
        rows = pl.ds(pl.multiple_of(k * tile, tile), tile)
        sent[rows, :] = (turned(dot(tc[rows, :], z[...]), dot(ts[rows, :], z[...]), -1.0) * norm).astype(BF)
        return carry

    steps = got.shape[0] // tile
    lax.fori_loop(0, steps, first, 0)
    lax.fori_loop(0, steps, second, 0)
    grad[0:192, :] = natural_lanes(acc_p[0:192, :]).astype(BF)
    grad[192:320, :] = natural_lanes(acc_m[128:256, :]).astype(BF)
    grad[320:384, :] = natural_lanes(acc_m[64:128, :]).astype(BF)


def imag_first(got):
    mid = pltpu.roll(got[:, 128:256].astype(F32), 64, 1).astype(BF)
    return jnp.concatenate([got[:, 256:], mid], 1)


def middle_kernel(
    norm, cl, cols, got, tct, tst, tc, ts, unit, pre, w_out, w_out_t, my_col, *refs,
):
    cots = refs[:cols]
    output, d_out, d_joined, sent, grad, got_s, cot, acc_c, acc_s, acc_g = refs[cols:]
    y = pl.program_id(0)
    w = cots[0].shape[1]
    for k in range(cols):
        at = lax.rem(my_col[0, 0] + (cols - k), cols)
        cot[pl.ds(pl.multiple_of(at * w, w), w), :] = cots[k][0]

    @pl.when(y == 0)
    def _():
        got_s[...] = imag_first(got[...])

    back = ((dot(tct[0], got[:, :256]) - dot(tst[0], got_s[...])) * norm).astype(BF)
    joined = (unit[0].astype(F32) + back.astype(F32)).astype(BF)
    pre_all = jnp.concatenate([pre[0, :, :cl], pre[0, :, cl:] + dot(joined, w_out[...])], 1)
    slope, silu = slope_and_silu(pre_all)
    output[0] = silu.astype(BF)
    d = (cot[...].astype(F32) * slope).astype(BF)
    d_out[0] = d
    dj = dot(d[:, cl:], w_out_t[...]).astype(BF)
    d_joined[0] = dj
    g = dot(joined, d[:, cl:], ROWS_OF)

    @pl.when(y == 0)
    def _():
        acc_g[...] = g

    @pl.when(y > 0)
    def _():
        acc_g[...] += g

    transform_out(y, norm, dj, tc, ts, sent, acc_c, acc_s)

    @pl.when(y == pl.num_programs(0) - 1)
    def _():
        grad[...] = acc_g[0 : grad.shape[0], :].astype(BF)


def tail_kernel(
    norm, cl, got, tct, tst, masked, d_joined, w_in, grad_freq, d_unit, late, got_s, acc_g
):
    y = pl.program_id(0)

    @pl.when(y == 0)
    def _():
        got_s[...] = imag_first(got[...])

    back = ((dot(tct[0], got[:, :256]) - dot(tst[0], got_s[...])) * norm).astype(BF)
    x = masked[0, :, cl:]
    slope = slope_and_silu(dot(x, w_in[...]))[0]
    du = ((d_joined[0].astype(F32) + back.astype(F32)) * slope).astype(BF)
    g = dot(du, x, ROWS_OF)

    @pl.when(y == 0)
    def _():
        acc_g[...] = g

    @pl.when(y > 0)
    def _():
        acc_g[...] += g

    d_unit[0] = du

    @pl.when(y == pl.num_programs(0) - 1)
    def _():
        at = 0
        for part, size in ((grad_freq, 384), (acc_g, 192)):
            for k in range(3):
                late[at : at + size, :] = part[0:size, k * 128 : (k + 1) * 128].astype(BF)
                at += size
        late[at:, :] = jnp.zeros((late.shape[0] - at, 128), BF)


def finish_kernel(cl, marked, d_unit, d_conv, w_in_t, grad_features):
    keep = marked[...].reshape(-1, marked.shape[-1])[:, :1].astype(F32) < 0.5 * HOLE
    total = jnp.concatenate([d_conv[0, :, :cl], d_conv[0, :, cl:] + dot(d_unit[0], w_in_t[...])], 1)
    grad_features[0] = jnp.where(keep, total, 0.0).astype(BF)


def shifted(x, step):
    n = x.shape[0]
    at = lax.broadcasted_iota(jnp.int32, x.shape, 0)
    if step == 1:
        return jnp.where(at == 0, 0.0, pltpu.roll(x, 1, 0))
    return jnp.where(at == n - 1, 0.0, pltpu.roll(x, n - 1, 0))


def three(x):
    f = x.astype(F32)
    return jnp.concatenate([shifted(f, -1).astype(BF), x, shifted(f, 1).astype(BF)], 1)


def conv_kernel(cl, above, masked, below, w_local, w_cross, pre, pad):
    y = pl.program_id(0)
    rows = masked.shape[0]

    @pl.when(y == 0)
    def _():
        pad[0] = above[0]
        pad[1 : rows + 1] = masked[...]
        pad[rows + 1] = below[0]

    local = dot(pad[y], w_local[0]) + dot(pad[y + 1], w_local[1]) + dot(pad[y + 2], w_local[2])
    near = jnp.concatenate([pad[y, :, :cl], pad[y + 1, :, :cl], pad[y + 2, :, :cl]], 1)
    cross = dot(near, w_cross[...])
    c, g = cl, w_cross.shape[1] // 3
    pre[0, :, :cl] = shifted(local[:, :c], 1) + local[:, c : 2 * c] + shifted(local[:, 2 * c :], -1)
    pre[0, :, cl:] = shifted(cross[:, :g], 1) + cross[:, g : 2 * g] + shifted(cross[:, 2 * g :], -1)


def conv_grad_kernel(cl, above, masked, below, d_out, g_out, early, pad, acc_l, acc_c):
    y = pl.program_id(0)
    rows = masked.shape[0]

    @pl.when(y == 0)
    def _():
        pad[0] = above[0]
        pad[1 : rows + 1] = masked[...]
        pad[rows + 1] = below[0]
        acc_l[...] = jnp.zeros_like(acc_l)
        acc_c[...] = jnp.zeros_like(acc_c)

    d_local = three(d_out[0, :, :cl])
    d_global = three(d_out[0, :, cl:])
    g = d_global.shape[1] // 3
    for i in range(3):
        x = pad[y + i]
        acc_l[i] += dot(x, d_local, ROWS_OF)
        acc_c[i] += dot(x[:, :cl], d_global, ROWS_OF)

    @pl.when(y == pl.num_programs(0) - 1)
    def _():
        ch = masked.shape[2]
        for i in range(3):
            early[0, i * ch : (i + 1) * ch, :] = acc_l[i].astype(BF)
            for j in range(3):
                at = (3 * i + j) * cl
                early[1, at : at + cl, :] = acc_c[i, :, j * g : (j + 1) * g].astype(BF)
        at, size = 9 * cl, g_out.shape[0]
        early[1, at : at + size, :] = g_out[...]
        early[1, at + size :, :] = jnp.zeros((early.shape[1] - at - size, g), BF)


def unpack_kernel(cl, got, g_local, g_cross, g_out):
    rows, ch = got.shape[2], g_local.shape[2]
    for at in range(0, 3 * ch, 64):
        block = got[at // rows, 0, at % rows : at % rows + 64, :].astype(F32)
        for j in range(3):
            g_local[at // ch, j, at % ch : at % ch + 64, :] = block[:, j * cl : (j + 1) * cl]
    for at in range(0, 9 * cl + g_out.shape[0], 64):
        block = got[at // rows, 1, at % rows : at % rows + 64, :].astype(F32)
        if at < 9 * cl:
            g_cross[at : at + 64, :] = block
        else:
            g_out[at - 9 * cl : at - 9 * cl + 64, :] = block


def conv_back_kernel(cl, above, d_out, below, w_local, w_cross, d_conv, pad_l, pad_g):
    y = pl.program_id(0)
    rows = d_out.shape[0]

    @pl.when(y == 0)
    def _():
        for k in range(rows + 2):
            line = above[0] if k == 0 else below[0] if k == rows + 1 else d_out[k - 1]
            pad_l[k] = three(line[:, :cl])
            pad_g[k] = three(line[:, cl:])

    total = dot(pad_l[y + 2], w_local[0]) + dot(pad_l[y + 1], w_local[1]) + dot(pad_l[y], w_local[2])
    cross = dot(pad_g[y + 2], w_cross[0]) + dot(pad_g[y + 1], w_cross[1]) + dot(pad_g[y], w_cross[2])
    d_conv[0, :, :cl] = total[:, :cl] + cross
    d_conv[0, :, cl:] = total[:, cl:]


def swap(x, count):
    return lax.all_to_all(x.reshape(count, -1, x.shape[-1]), AXES, 0, 0, tiled=True).reshape(x.shape)


def to_rows(field, cols):
    h, w, c = field.shape
    return lax.all_to_all(field.reshape(cols, h // cols, w, c), "col", 0, 0, tiled=True)


def turn(field, cols):
    h, w, c = field.shape
    blocks = field.reshape(cols, h // cols, w, c)
    me = lax.axis_index("col")
    out = []
    for k in range(cols):
        part = lax.dynamic_index_in_dim(blocks, (me + k) % cols, 0, keepdims=False)
        out.append(lax.ppermute(part, "col", [(i, (i + k) % cols) for i in range(cols)]) if k else part)
    return out


def core_sum(early):
    pairs = lax.axis_size("row")
    core = lax.axis_index("row") % 2
    mine = lax.dynamic_index_in_dim(early, core, 0, keepdims=False)
    other = lax.dynamic_index_in_dim(early, 1 - core, 0, keepdims=False)
    other = lax.ppermute(other, "row", [(i, i ^ 1) for i in range(pairs)])
    return (mine.astype(F32) + other.astype(F32)).astype(BF)


def scatter_half(total, count):
    pairs = lax.axis_size("row")
    cols = count // pairs
    groups = [[cols * r + c for r in range(k, pairs, 2) for c in range(cols)] for k in range(2)]
    return lax.all_to_all(
        total.reshape(count // 2, -1, total.shape[-1]), AXES, 0, 0, axis_index_groups=groups, tiled=True
    )


def gather_halves(x, cols):
    me = lax.axis_index("col")
    parts = [x]
    for k in range(1, cols):
        parts.append(lax.ppermute(x, "col", [((i + k) % cols, i) for i in range(cols)]))
    both = jnp.concatenate(parts + parts[:-1], 0)
    size = x.shape[0]
    x = lax.dynamic_slice_in_dim(both, (cols - me) % cols * size, cols * size, 0)
    x = lax.all_gather(x, "row", axis=0)
    return x.reshape(x.shape[0] // 2, 2, *x.shape[1:])


def edges(field, count):
    down = lax.ppermute(field[-1:], AXES, [(i, i + 1) for i in range(count - 1)])
    up = lax.ppermute(field[:1], AXES, [(i + 1, i) for i in range(count - 1)])
    return down, up


def scatter_sum(x, count):
    x = lax.all_to_all(x.reshape(count, -1, x.shape[-1]), AXES, 0, 0, tiled=True)
    return x.astype(F32).sum(0).astype(BF)


def gather(x, count):
    x = lax.all_to_all(jnp.broadcast_to(x[None], (count,) + x.shape), AXES, 0, 0, tiled=True)
    return x.reshape(-1, x.shape[-1])


def tie(value, *after):
    return lax.optimization_barrier((value,) + after)[0]


def tied(*values):
    return lax.optimization_barrier(values)


def shards(features, hole_mask, cotangent, w_local, w_cross, w_in, w_freq, w_out):
    cols = lax.axis_size("col")
    count = lax.axis_size("row") * cols
    me = lax.axis_index(AXES)
    _, h, w, ch = features.shape
    rows, width = h // cols, w * cols
    height = rows * count
    cl, cg, cs = w_local.shape[3], w_cross.shape[3], w_in.shape[1]
    lines = -(-(width // 2 + 1) // count)
    slots = -(-(rows * lines) // 16) * 16
    n = count * slots
    tile = min(256, n)
    tc, ts = line_tables(rows, width, count, lines, slots)
    tct, tst = jnp.asarray(tc.transpose(0, 2, 1)), jnp.asarray(ts.transpose(0, 2, 1))
    tc, ts = jnp.asarray(tc), jnp.asarray(ts)
    hc, hs = (jnp.asarray(t) for t in column_tables(rows, count, lines, slots))
    norm_w, norm_h = 1.0 / math.sqrt(width), 1.0 / math.sqrt(height)
    freq = lines * me + jnp.arange(slots) % lines
    weight = jnp.where((freq == 0) | (freq * 2 == width), 0.5, jnp.where(freq * 2 < width, 1.0, 0.0))
    weight = jnp.tile(weight.astype(F32), count)[:, None]
    sign = np.where((np.arange(384) < 192), 1.0, -1.0).astype(np.float32)
    sign = jnp.asarray(sign[None])

    w_in_d = jnp.concatenate([w_in, w_in[:, 128:]], 1)
    w_in_t = jnp.pad(w_in.T, ((0, 64), (0, 0)))
    w_out_z = jnp.pad(w_out, ((0, 64), (0, 0)))
    w_out_t = jnp.concatenate([w_out, w_out[128:]], 0).T
    w_freq_p = pack_dim(pack_dim(w_freq, 0, cs), 1, cs)
    w_freq_t = w_freq_p.T
    wl = jnp.transpose(w_local, (0, 2, 1, 3)).reshape(3, ch, 3 * cl)
    wc = jnp.transpose(w_cross, (0, 2, 1, 3)).reshape(3 * cl, 3 * cg)
    wl_t = jnp.transpose(w_local, (0, 1, 3, 2)).reshape(3, 3 * cl, ch)
    wc_t = jnp.transpose(w_cross, (0, 1, 3, 2)).reshape(3, 3 * cg, cl)

    at_y = lambda y: (y, 0, 0)
    one_row = lambda c: (1, width, c)
    blocks = lambda c: (cols, 1, w, c)
    at_blocks = lambda y: (0, y, 0, 0)
    line_table = (1, n, width)
    back_table = (1, width, n)
    wide = (rows, width, ch)
    pix = rows * width
    vm = pltpu.VMEM

    marked = jnp.where(hole_mask[0][..., None] == 1, HOLE, features[0]).astype(BF)
    marked = to_rows(marked, cols)
    w_in_d, w_in_t, w_out_z, w_out_t, w_freq_p, w_freq_t, wl, wc, wl_t, wc_t, weight = tied(
        w_in_d, w_in_t, w_out_z, w_out_t, w_freq_p, w_freq_t, wl, wc, wl_t, wc_t, weight
    )
    cots = turn(tie(cotangent[0], marked), cols)
    my_col = lax.axis_index("col").astype(jnp.int32).reshape(1, 1)

    masked, unit, sent = call(
        functools.partial(head_kernel, norm_w, cl),
        "head",
        (rows,),
        [(marked, blocks(ch), at_blocks), (w_in_d, None, None), (tc, line_table, at_y), (ts, line_table, at_y)],
        [(wide, BF, one_row(ch), at_y), ((rows, width, 256), BF, one_row(256), at_y), ((n, 384), BF, None, None)],
        [vm((n, 256), F32), vm((n, 256), F32)],
        flops=4 * n * pix * 256, bytes_=12 << 20,
    )
    above, below = edges(masked, count)
    got = tie(swap(sent, count), above, below)
    (pre,) = call(
        functools.partial(conv_kernel, cl),
        "conv",
        (rows,),
        [(above, None, None), (masked, None, None), (below, None, None), (wl, None, None), (wc, None, None)],
        [(wide, F32, one_row(ch), at_y)],
        [vm((rows + 2, width, ch), BF)],
        flops=18 * pix * (ch * cl + cl * cg), bytes_=9 << 20,
    )
    stacked, sent = call(
        functools.partial(frequency_kernel, norm_h, tile),
        "frequency",
        (1,),
        [(got, None, None), (hc, None, None), (hs, None, None), (w_freq_p, None, None), (weight, None, None), (sign, None, None)],
        [((n, 384), BF, None, None), ((n, 384), BF, None, None)],
        [vm((n, 384), BF)],
        flops=8 * n * n * 384, bytes_=7 << 20,
    )
    sent, *cots = tied(sent, *cots)
    got = swap(sent, count)
    output, d_out, d_joined, sent, grad_out = call(
        functools.partial(middle_kernel, norm_w, cl, cols),
        "middle",
        (rows,),
        [
            (got, None, None), (tct, back_table, at_y), (tst, back_table, at_y), (tc, line_table, at_y),
            (ts, line_table, at_y), (unit, one_row(256), at_y), (pre, one_row(ch), at_y),
            (w_out_z, None, None), (w_out_t, None, None), (my_col, None, None),
        ]
        + [(c, (1, w, ch), at_y) for c in cots],
        [
            (wide, BF, one_row(ch), at_y), (wide, BF, one_row(ch), at_y), ((rows, width, 256), BF, one_row(256), at_y),
            ((n, 384), BF, None, None), ((cs, cg), BF, None, None),
        ],
        [vm((n, 256), BF), vm((width, ch), BF), vm((n, 256), F32), vm((n, 256), F32), vm((256, cg), F32)],
        flops=8 * n * pix * 256, bytes_=24 << 20,
    )
    got = swap(sent, count)
    d_above, d_below = edges(d_out, count)
    (early,) = call(
        functools.partial(conv_grad_kernel, cl),
        "conv_grad",
        (rows,),
        [(above, None, None), (masked, None, None), (below, None, None), (d_out, one_row(ch), at_y), (grad_out, None, None)],
        [((2, 3 * ch, 384), BF, None, None)],
        [vm((rows + 2, width, ch), BF), vm((3, ch, 3 * cl), F32), vm((3, cl, 3 * cg), F32)],
        flops=18 * pix * (ch * cl + cl * cg), bytes_=7 << 20,
    )
    got, early = tied(got, early)
    got, total, d_above, d_below = tied(got, core_sum(early), d_above, d_below)
    early = scatter_half(total, count)
    sent, grad_freq = call(
        functools.partial(frequency_back_kernel, norm_h, tile),
        "frequency_back",
        (1,),
        [
            (got, None, None), (hc, None, None), (hs, None, None), (w_freq_p, None, None), (w_freq_t, None, None),
            (weight, None, None), (sign, None, None), (stacked, None, None),
        ],
        [((n, 384), BF, None, None), ((384, 384), BF, None, None)],
        [vm((n, 384), BF), vm((256, 384), F32), vm((256, 384), F32)],
        flops=8 * n * n * 384, bytes_=8 << 20,
    )
    sent, early = tied(sent, early)
    got = swap(sent, count)
    (d_conv,) = call(
        functools.partial(conv_back_kernel, cl),
        "conv_back",
        (rows,),
        [(d_above, None, None), (d_out, None, None), (d_below, None, None), (wl_t, None, None), (wc_t, None, None)],
        [(wide, F32, one_row(ch), at_y)],
        [vm((rows + 2, width, 3 * cl), BF), vm((rows + 2, width, 3 * cg), BF)],
        flops=18 * pix * (ch * cl + cl * cg), bytes_=9 << 20,
    )
    got, d_conv, early = tied(got, d_conv, early)
    early = gather_halves(early.astype(F32).sum(0).astype(BF), cols)
    late_rows = -(-(3 * 384 + 3 * cs) // (16 * count)) * 16 * count
    d_unit, late = call(
        functools.partial(tail_kernel, norm_w, cl),
        "tail",
        (rows,),
        [
            (got, None, None), (tct, back_table, at_y), (tst, back_table, at_y), (masked, one_row(ch), at_y),
            (d_joined, one_row(256), at_y), (w_in_d, None, None), (grad_freq, None, None),
        ],
        [((rows, width, 256), BF, one_row(256), at_y), ((late_rows, 128), BF, None, None)],
        [vm((n, 256), BF), vm((256, cg), F32)],
        flops=4 * n * pix * 256, bytes_=16 << 20,
    )
    late = scatter_sum(late, count)
    (grad_features,) = call(
        functools.partial(finish_kernel, cl),
        "finish",
        (rows,),
        [
            (marked, blocks(128), at_blocks), (d_unit, one_row(256), at_y), (d_conv, one_row(ch), at_y),
            (w_in_t, None, None),
        ],
        [(wide, BF, one_row(ch), at_y)],
        flops=2 * pix * 256 * cg, bytes_=7 << 20,
    )
    late, grad_features = tied(late, grad_features)
    grad_local, grad_cross, grad_out = call(
        functools.partial(unpack_kernel, cl),
        "unpack",
        (1,),
        [(early, None, None)],
        [((3, 3, ch, cl), F32, None, None), ((9 * cl, cg), F32, None, None), ((cs, cg), F32, None, None)],
        flops=1, bytes_=7 << 20,
    )
    late = gather(late, count)
    late, grad_local, grad_cross, grad_out = tied(late, grad_local, grad_cross, grad_out)
    grad_freq = jnp.concatenate([late[k * 384 : (k + 1) * 384] for k in range(3)], 1).astype(F32)
    at = 3 * 384
    grad_in = jnp.concatenate([late[at + k * cs : at + (k + 1) * cs] for k in range(3)], 1).astype(F32).T
    grad_cross = grad_cross.reshape(3, 3, cl, cg)
    return output[None], grad_features[None], grad_local, grad_cross, grad_in, grad_freq, grad_out


def solution(mesh):
    return jax.shard_map(
        shards,
        mesh=mesh,
        in_specs=(
            P("dp", "row", "col", None),
            P("dp", "row", "col"),
            P("dp", "row", "col", None),
            P(),
            P(),
            P(),
            P(),
            P(),
        ),
        out_specs=(
            P("dp", ("row", "col"), None, None),
            P("dp", ("row", "col"), None, None),
            P("dp", None, None, None),
            P("dp", None, None, None),
            P("dp", None),
            P("dp", None),
            P("dp", None),
        ),
        check_vma=False,
    )
```

```python
import functools
import math

import jax
import jax.numpy as jnp
import numpy as np
from jax import lax
from jax.experimental import pallas as pl
from jax.experimental.pallas import tpu as pltpu
from jax.sharding import PartitionSpec as P

AXES = ("row", "col")
HOLE = 64.0
BF = jnp.bfloat16
F32 = jnp.float32
ROWS_OF = ((0,), (0,))


def dot(a, b, dims=((1,), (0,))):
    return lax.dot_general(a, b, (dims, ((), ())), preferred_element_type=F32)


def line_tables(rows, width, count, lines, slots):
    cos = np.zeros((rows, count, slots, width), np.float32)
    sin = np.zeros((rows, count, slots, width), np.float32)
    freq = lines * np.arange(count)[:, None] + np.arange(lines)[None]
    angle = 2.0 * np.pi * (freq[..., None] * np.arange(width) % width) / width
    valid = (freq <= width // 2)[..., None]
    for y in range(rows):
        cos[y, :, y * lines : (y + 1) * lines] = np.cos(angle) * valid
        sin[y, :, y * lines : (y + 1) * lines] = np.sin(angle) * valid
    shape = (rows, count * slots, width)
    return cos.reshape(shape).astype(BF), sin.reshape(shape).astype(BF)


def column_tables(rows, count, lines, slots):
    height = rows * count
    cos = np.zeros((count, slots, count, slots), np.float32)
    sin = np.zeros((count, slots, count, slots), np.float32)
    h = np.arange(height).reshape(count, rows)
    angle = 2.0 * np.pi * (h[:, :, None, None] * h[None, None] % height) / height
    for y in range(rows):
        for z in range(rows):
            for j in range(lines):
                cos[:, y * lines + j, :, z * lines + j] = np.cos(angle[:, y, :, z])
                sin[:, y * lines + j, :, z * lines + j] = np.sin(angle[:, y, :, z])
    shape = (count * slots, count * slots)
    return cos.reshape(shape).astype(BF), sin.reshape(shape).astype(BF)


def slope_and_silu(value):
    sigma = 1.0 / (1.0 + jnp.exp(-value))
    return sigma * (1.0 + value * (1.0 - sigma)), value * sigma


def lanes_below(shape, bound):
    return lax.broadcasted_iota(jnp.int32, shape, 1) < bound


def packed(re, im):
    mid = jnp.where(lanes_below(re[:, 128:].shape, 64), re[:, 128:], im[:, 128:])
    return jnp.concatenate([re[:, :128], mid, im[:, :128]], 1)


def turned(p, q, sign):
    mid = pltpu.roll(q[:, 128:256], 64, 1)
    flip = jnp.where(lanes_below(mid.shape, 64), sign, -sign)
    return jnp.concatenate(
        [p[:, :128] + sign * q[:, 256:], p[:, 128:256] + flip * mid, p[:, 256:] - sign * q[:, :128]], 1
    )


def natural_lanes(x):
    mid, im = x[:, 128:256], pltpu.roll(x[:, 256:], 64, 1)
    low = lanes_below(mid.shape, 64)
    return jnp.concatenate([x[:, :128], jnp.where(low, mid, im), jnp.where(low, im, mid)], 1)


def pack_order(cs):
    return [(0, 128), (128, cs), (cs + 128, 2 * cs), (cs, cs + 128)]


def pack_dim(x, dim, cs):
    return jnp.concatenate([lax.slice_in_dim(x, a, b, axis=dim) for a, b in pack_order(cs)], dim)


def call(body, name, grid, ins, outs, scratch=(), flops=0, bytes_=0):
    def spec(shape, block, index):
        if shape == (1, 1):
            return pl.BlockSpec(memory_space=pltpu.SMEM)
        if block is None:
            zeros = (0,) * len(shape)
            return pl.BlockSpec(shape, lambda *_: zeros)
        return pl.BlockSpec(block, index)

    return pl.pallas_call(
        body,
        grid=grid,
        in_specs=[spec(a.shape, block, index) for a, block, index in ins],
        out_specs=[spec(shape, block, index) for shape, _, block, index in outs],
        out_shape=[jax.ShapeDtypeStruct(shape, dtype) for shape, dtype, _, _ in outs],
        scratch_shapes=list(scratch),
        compiler_params=pltpu.CompilerParams(vmem_limit_bytes=56 << 20),
        cost_estimate=pl.CostEstimate(flops=flops, bytes_accessed=bytes_, transcendentals=0),
        name=name,
    )(*[a for a, _, _ in ins])


def head_kernel(norm, cl, marked, w_in, tc, ts, masked, unit, sent, acc_c, acc_s):
    y = pl.program_id(0)
    x = marked[...].reshape(-1, marked.shape[-1])
    keep = x[:, :1].astype(F32) < 0.5 * HOLE
    x = jnp.where(keep, x, jnp.zeros_like(x))
    masked[0] = x
    u = slope_and_silu(dot(x[:, cl:], w_in[...]))[1].astype(BF)
    unit[0] = u
    transform_out(y, norm, u, tc, ts, sent, acc_c, acc_s)


def transform_out(y, norm, u, tc, ts, sent, acc_c, acc_s):
    re, im = dot(tc[0], u), dot(ts[0], u)

    @pl.when(y == 0)
    def _():
        acc_c[...] = re
        acc_s[...] = im

    @pl.when(y > 0)
    def _():
        acc_c[...] += re
        acc_s[...] += im

    @pl.when(y == pl.num_programs(0) - 1)
    def _():
        sent[...] = packed(acc_c[...] * norm, acc_s[...] * -norm).astype(BF)


def frequency_kernel(norm, tile, got, tc, ts, w_freq, weight, sign, stacked, sent, z):
    def first(k, carry):
        rows = pl.ds(pl.multiple_of(k * tile, tile), tile)
        spec = turned(dot(tc[rows, :], got[...]), dot(ts[rows, :], got[...]), 1.0) * norm
        st = spec.astype(BF)
        stacked[rows, :] = st
        pos = slope_and_silu(dot(st, w_freq[...]))[1]
        neg = slope_and_silu(dot((st.astype(F32) * sign[...]).astype(BF), w_freq[...]))[1]
        z[rows, :] = (weight[rows, :] * (pos + sign[...] * neg)).astype(BF)
        return carry

    def second(k, carry):
        rows = pl.ds(pl.multiple_of(k * tile, tile), tile)
        sent[rows, :] = (turned(dot(tc[rows, :], z[...]), dot(ts[rows, :], z[...]), -1.0) * norm).astype(BF)
        return carry

    steps = got.shape[0] // tile
    lax.fori_loop(0, steps, first, 0)
    lax.fori_loop(0, steps, second, 0)


def frequency_back_kernel(
    norm, tile, got, tc, ts, w_freq, w_freq_t, weight, sign, stacked, sent, grad, z, acc_p, acc_m
):
    acc_p[...] = jnp.zeros_like(acc_p)
    acc_m[...] = jnp.zeros_like(acc_m)

    def first(k, carry):
        rows = pl.ds(pl.multiple_of(k * tile, tile), tile)
        dz = turned(dot(tc[rows, :], got[...]), dot(ts[rows, :], got[...]), 1.0) * norm
        st = stacked[rows, :]
        pos = slope_and_silu(dot(st, w_freq[...]))[0]
        neg = slope_and_silu(dot((st.astype(F32) * sign[...]).astype(BF), w_freq[...]))[0]
        pos = (dz * pos).astype(BF).astype(F32)
        neg = (dz * sign[...] * neg).astype(BF).astype(F32)
        total = (weight[rows, :] * (pos + neg)).astype(BF)
        delta = (weight[rows, :] * (pos - neg)).astype(BF)
        acc_p[...] += dot(st[:, :256], total, ROWS_OF)
        acc_m[...] += dot(st[:, 128:], delta, ROWS_OF)
        re = dot(total, w_freq_t[:, :256])
        im = dot(delta, w_freq_t[:, 128:])
        mid = jnp.where(lanes_below((tile, 128), 64), re[:, 128:], im[:, :128])
        z[rows, :] = jnp.concatenate([re[:, :128], mid, im[:, 128:]], 1).astype(BF)
        return carry

    def second(k, carry):
        rows = pl.ds(pl.multiple_of(k * tile, tile), tile)
        sent[rows, :] = (turned(dot(tc[rows, :], z[...]), dot(ts[rows, :], z[...]), -1.0) * norm).astype(BF)
        return carry

    steps = got.shape[0] // tile
    lax.fori_loop(0, steps, first, 0)
    lax.fori_loop(0, steps, second, 0)
    grad[0:192, :] = natural_lanes(acc_p[0:192, :]).astype(BF)
    grad[192:320, :] = natural_lanes(acc_m[128:256, :]).astype(BF)
    grad[320:384, :] = natural_lanes(acc_m[64:128, :]).astype(BF)


def imag_first(got):
    mid = pltpu.roll(got[:, 128:256].astype(F32), 64, 1).astype(BF)
    return jnp.concatenate([got[:, 256:], mid], 1)


def middle_kernel(
    norm, cl, cols, got, tct, tst, tc, ts, unit, pre, w_out, w_out_t, my_col, *refs,
):
    cots = refs[:cols]
    output, d_out, d_joined, sent, grad, got_s, cot, acc_c, acc_s, acc_g = refs[cols:]
    y = pl.program_id(0)
    w = cots[0].shape[1]
    for k in range(cols):
        at = lax.rem(my_col[0, 0] + (cols - k), cols)
        cot[pl.ds(pl.multiple_of(at * w, w), w), :] = cots[k][0]

    @pl.when(y == 0)
    def _():
        got_s[...] = imag_first(got[...])

    back = ((dot(tct[0], got[:, :256]) - dot(tst[0], got_s[...])) * norm).astype(BF)
    joined = (unit[0].astype(F32) + back.astype(F32)).astype(BF)
    pre_all = jnp.concatenate([pre[0, :, :cl], pre[0, :, cl:] + dot(joined, w_out[...])], 1)
    slope, silu = slope_and_silu(pre_all)
    output[0] = silu.astype(BF)
    d = (cot[...].astype(F32) * slope).astype(BF)
    d_out[0] = d
    dj = dot(d[:, cl:], w_out_t[...]).astype(BF)
    d_joined[0] = dj
    g = dot(joined, d[:, cl:], ROWS_OF)

    @pl.when(y == 0)
    def _():
        acc_g[...] = g

    @pl.when(y > 0)
    def _():
        acc_g[...] += g

    transform_out(y, norm, dj, tc, ts, sent, acc_c, acc_s)

    @pl.when(y == pl.num_programs(0) - 1)
    def _():
        grad[...] = acc_g[0 : grad.shape[0], :].astype(BF)


def tail_kernel(
    norm, cl, got, tct, tst, masked, d_joined, w_in, grad_freq, d_unit, late, got_s, acc_g
):
    y = pl.program_id(0)

    @pl.when(y == 0)
    def _():
        got_s[...] = imag_first(got[...])

    back = ((dot(tct[0], got[:, :256]) - dot(tst[0], got_s[...])) * norm).astype(BF)
    x = masked[0, :, cl:]
    slope = slope_and_silu(dot(x, w_in[...]))[0]
    du = ((d_joined[0].astype(F32) + back.astype(F32)) * slope).astype(BF)
    g = dot(du, x, ROWS_OF)

    @pl.when(y == 0)
    def _():
        acc_g[...] = g

    @pl.when(y > 0)
    def _():
        acc_g[...] += g

    d_unit[0] = du

    @pl.when(y == pl.num_programs(0) - 1)
    def _():
        at = 0
        for part, size in ((grad_freq, 384), (acc_g, 192)):
            for k in range(3):
                late[at : at + size, :] = part[0:size, k * 128 : (k + 1) * 128].astype(BF)
                at += size
        late[at:, :] = jnp.zeros((late.shape[0] - at, 128), BF)


def finish_kernel(cl, marked, d_unit, d_conv, w_in_t, grad_features):
    keep = marked[...].reshape(-1, marked.shape[-1])[:, :1].astype(F32) < 0.5 * HOLE
    total = jnp.concatenate([d_conv[0, :, :cl], d_conv[0, :, cl:] + dot(d_unit[0], w_in_t[...])], 1)
    grad_features[0] = jnp.where(keep, total, 0.0).astype(BF)


def shifted(x, step):
    n = x.shape[0]
    at = lax.broadcasted_iota(jnp.int32, x.shape, 0)
    if step == 1:
        return jnp.where(at == 0, 0.0, pltpu.roll(x, 1, 0))
    return jnp.where(at == n - 1, 0.0, pltpu.roll(x, n - 1, 0))


def three(x):
    f = x.astype(F32)
    return jnp.concatenate([shifted(f, -1).astype(BF), x, shifted(f, 1).astype(BF)], 1)


def conv_kernel(cl, above, masked, below, w_local, w_cross, pre, pad):
    y = pl.program_id(0)
    rows = masked.shape[0]

    @pl.when(y == 0)
    def _():
        pad[0] = above[0]
        pad[1 : rows + 1] = masked[...]
        pad[rows + 1] = below[0]

    local = dot(pad[y], w_local[0]) + dot(pad[y + 1], w_local[1]) + dot(pad[y + 2], w_local[2])
    near = jnp.concatenate([pad[y, :, :cl], pad[y + 1, :, :cl], pad[y + 2, :, :cl]], 1)
    cross = dot(near, w_cross[...])
    c, g = cl, w_cross.shape[1] // 3
    pre[0, :, :cl] = shifted(local[:, :c], 1) + local[:, c : 2 * c] + shifted(local[:, 2 * c :], -1)
    pre[0, :, cl:] = shifted(cross[:, :g], 1) + cross[:, g : 2 * g] + shifted(cross[:, 2 * g :], -1)


def conv_grad_kernel(cl, above, masked, below, d_out, g_out, early, pad, acc_l, acc_c):
    y = pl.program_id(0)
    rows = masked.shape[0]

    @pl.when(y == 0)
    def _():
        pad[0] = above[0]
        pad[1 : rows + 1] = masked[...]
        pad[rows + 1] = below[0]
        acc_l[...] = jnp.zeros_like(acc_l)
        acc_c[...] = jnp.zeros_like(acc_c)

    d_local = three(d_out[0, :, :cl])
    d_global = three(d_out[0, :, cl:])
    g = d_global.shape[1] // 3
    for i in range(3):
        x = pad[y + i]
        acc_l[i] += dot(x, d_local, ROWS_OF)
        acc_c[i] += dot(x[:, :cl], d_global, ROWS_OF)

    @pl.when(y == pl.num_programs(0) - 1)
    def _():
        ch = masked.shape[2]
        for i in range(3):
            early[0, i * ch : (i + 1) * ch, :] = acc_l[i].astype(BF)
            for j in range(3):
                at = (3 * i + j) * cl
                early[1, at : at + cl, :] = acc_c[i, :, j * g : (j + 1) * g].astype(BF)
        at, size = 9 * cl, g_out.shape[0]
        early[1, at : at + size, :] = g_out[...]
        early[1, at + size :, :] = jnp.zeros((early.shape[1] - at - size, g), BF)


def unpack_kernel(cl, mine, other, core, g_local, g_cross, g_out):
    ch = g_local.shape[2]

    def write(local, rest):
        for at in range(0, 3 * ch, 64):
            block = local[at : at + 64, :].astype(F32)
            for j in range(3):
                g_local[at // ch, j, at % ch : at % ch + 64, :] = block[:, j * cl : (j + 1) * cl]
        g_cross[...] = rest[0 : 9 * cl, :].astype(F32)
        g_out[...] = rest[9 * cl : 9 * cl + g_out.shape[0], :].astype(F32)

    @pl.when(core[0, 0] == 0)
    def _():
        write(mine, other)

    @pl.when(core[0, 0] == 1)
    def _():
        write(other, mine)


def conv_back_kernel(cl, above, d_out, below, w_local, w_cross, d_conv, pad_l, pad_g):
    y = pl.program_id(0)
    rows = d_out.shape[0]

    @pl.when(y == 0)
    def _():
        for k in range(rows + 2):
            line = above[0] if k == 0 else below[0] if k == rows + 1 else d_out[k - 1]
            pad_l[k] = three(line[:, :cl])
            pad_g[k] = three(line[:, cl:])

    total = dot(pad_l[y + 2], w_local[0]) + dot(pad_l[y + 1], w_local[1]) + dot(pad_l[y], w_local[2])
    cross = dot(pad_g[y + 2], w_cross[0]) + dot(pad_g[y + 1], w_cross[1]) + dot(pad_g[y], w_cross[2])
    d_conv[0, :, :cl] = total[:, :cl] + cross
    d_conv[0, :, cl:] = total[:, cl:]


def swap(x, count):
    return lax.all_to_all(x.reshape(count, -1, x.shape[-1]), AXES, 0, 0, tiled=True).reshape(x.shape)


def to_rows(field, cols):
    h, w, c = field.shape
    return lax.all_to_all(field.reshape(cols, h // cols, w, c), "col", 0, 0, tiled=True)


def turn(field, cols):
    h, w, c = field.shape
    blocks = field.reshape(cols, h // cols, w, c)
    me = lax.axis_index("col")
    out = []
    for k in range(cols):
        part = lax.dynamic_index_in_dim(blocks, (me + k) % cols, 0, keepdims=False)
        out.append(lax.ppermute(part, "col", [(i, (i + k) % cols) for i in range(cols)]) if k else part)
    return out


def core_sum(early):
    pairs = lax.axis_size("row")
    core = lax.axis_index("row") % 2
    mine = lax.dynamic_index_in_dim(early, core, 0, keepdims=False)
    other = lax.dynamic_index_in_dim(early, 1 - core, 0, keepdims=False)
    other = lax.ppermute(other, "row", [(i, i ^ 1) for i in range(pairs)])
    return (mine.astype(F32) + other.astype(F32)).astype(BF)


def core_exchange(x, count):
    pairs = lax.axis_size("row")
    cols = count // pairs
    groups = [[cols * r + c for r in range(k, pairs, 2) for c in range(cols)] for k in range(2)]
    x = x.reshape(count // 2, -1, x.shape[-1])
    return lax.all_to_all(x, AXES, 0, 0, axis_index_groups=groups, tiled=True)


def edges(field, count):
    down = lax.ppermute(field[-1:], AXES, [(i, i + 1) for i in range(count - 1)])
    up = lax.ppermute(field[:1], AXES, [(i + 1, i) for i in range(count - 1)])
    return down, up


def scatter_sum(x, count):
    x = lax.all_to_all(x.reshape(count, -1, x.shape[-1]), AXES, 0, 0, tiled=True)
    return x.astype(F32).sum(0).astype(BF)


def gather(x, count):
    x = lax.all_to_all(jnp.broadcast_to(x[None], (count,) + x.shape), AXES, 0, 0, tiled=True)
    return x.reshape(-1, x.shape[-1])


def tie(value, *after):
    return lax.optimization_barrier((value,) + after)[0]


def tied(*values):
    return lax.optimization_barrier(values)


def shards(features, hole_mask, cotangent, w_local, w_cross, w_in, w_freq, w_out):
    cols = lax.axis_size("col")
    count = lax.axis_size("row") * cols
    me = lax.axis_index(AXES)
    _, h, w, ch = features.shape
    rows, width = h // cols, w * cols
    height = rows * count
    cl, cg, cs = w_local.shape[3], w_cross.shape[3], w_in.shape[1]
    lines = -(-(width // 2 + 1) // count)
    slots = -(-(rows * lines) // 16) * 16
    n = count * slots
    tile = min(256, n)
    tc, ts = line_tables(rows, width, count, lines, slots)
    tct, tst = jnp.asarray(tc.transpose(0, 2, 1)), jnp.asarray(ts.transpose(0, 2, 1))
    tc, ts = jnp.asarray(tc), jnp.asarray(ts)
    hc, hs = (jnp.asarray(t) for t in column_tables(rows, count, lines, slots))
    norm_w, norm_h = 1.0 / math.sqrt(width), 1.0 / math.sqrt(height)
    freq = lines * me + jnp.arange(slots) % lines
    weight = jnp.where((freq == 0) | (freq * 2 == width), 0.5, jnp.where(freq * 2 < width, 1.0, 0.0))
    weight = jnp.tile(weight.astype(F32), count)[:, None]
    sign = np.where((np.arange(384) < 192), 1.0, -1.0).astype(np.float32)
    sign = jnp.asarray(sign[None])

    w_in_d = jnp.concatenate([w_in, w_in[:, 128:]], 1)
    w_in_t = jnp.pad(w_in.T, ((0, 64), (0, 0)))
    w_out_z = jnp.pad(w_out, ((0, 64), (0, 0)))
    w_out_t = jnp.concatenate([w_out, w_out[128:]], 0).T
    w_freq_p = pack_dim(pack_dim(w_freq, 0, cs), 1, cs)
    w_freq_t = w_freq_p.T
    wl = jnp.transpose(w_local, (0, 2, 1, 3)).reshape(3, ch, 3 * cl)
    wc = jnp.transpose(w_cross, (0, 2, 1, 3)).reshape(3 * cl, 3 * cg)
    wl_t = jnp.transpose(w_local, (0, 1, 3, 2)).reshape(3, 3 * cl, ch)
    wc_t = jnp.transpose(w_cross, (0, 1, 3, 2)).reshape(3, 3 * cg, cl)

    at_y = lambda y: (y, 0, 0)
    one_row = lambda c: (1, width, c)
    blocks = lambda c: (cols, 1, w, c)
    at_blocks = lambda y: (0, y, 0, 0)
    line_table = (1, n, width)
    back_table = (1, width, n)
    wide = (rows, width, ch)
    pix = rows * width
    vm = pltpu.VMEM

    marked = jnp.where(hole_mask[0][..., None] == 1, HOLE, features[0]).astype(BF)
    marked = to_rows(marked, cols)
    w_in_d, w_in_t, w_out_z, w_out_t, w_freq_p, w_freq_t, wl, wc, wl_t, wc_t, weight = tied(
        w_in_d, w_in_t, w_out_z, w_out_t, w_freq_p, w_freq_t, wl, wc, wl_t, wc_t, weight
    )
    cots = turn(tie(cotangent[0], marked), cols)
    my_col = lax.axis_index("col").astype(jnp.int32).reshape(1, 1)

    masked, unit, sent = call(
        functools.partial(head_kernel, norm_w, cl),
        "head",
        (rows,),
        [(marked, blocks(ch), at_blocks), (w_in_d, None, None), (tc, line_table, at_y), (ts, line_table, at_y)],
        [(wide, BF, one_row(ch), at_y), ((rows, width, 256), BF, one_row(256), at_y), ((n, 384), BF, None, None)],
        [vm((n, 256), F32), vm((n, 256), F32)],
        flops=4 * n * pix * 256, bytes_=12 << 20,
    )
    above, below = edges(masked, count)
    got = tie(swap(sent, count), above, below)
    (pre,) = call(
        functools.partial(conv_kernel, cl),
        "conv",
        (rows,),
        [(above, None, None), (masked, None, None), (below, None, None), (wl, None, None), (wc, None, None)],
        [(wide, F32, one_row(ch), at_y)],
        [vm((rows + 2, width, ch), BF)],
        flops=18 * pix * (ch * cl + cl * cg), bytes_=9 << 20,
    )
    stacked, sent = call(
        functools.partial(frequency_kernel, norm_h, tile),
        "frequency",
        (1,),
        [(got, None, None), (hc, None, None), (hs, None, None), (w_freq_p, None, None), (weight, None, None), (sign, None, None)],
        [((n, 384), BF, None, None), ((n, 384), BF, None, None)],
        [vm((n, 384), BF)],
        flops=8 * n * n * 384, bytes_=7 << 20,
    )
    sent, *cots = tied(sent, *cots)
    got = swap(sent, count)
    output, d_out, d_joined, sent, grad_out = call(
        functools.partial(middle_kernel, norm_w, cl, cols),
        "middle",
        (rows,),
        [
            (got, None, None), (tct, back_table, at_y), (tst, back_table, at_y), (tc, line_table, at_y),
            (ts, line_table, at_y), (unit, one_row(256), at_y), (pre, one_row(ch), at_y),
            (w_out_z, None, None), (w_out_t, None, None), (my_col, None, None),
        ]
        + [(c, (1, w, ch), at_y) for c in cots],
        [
            (wide, BF, one_row(ch), at_y), (wide, BF, one_row(ch), at_y), ((rows, width, 256), BF, one_row(256), at_y),
            ((n, 384), BF, None, None), ((cs, cg), BF, None, None),
        ],
        [vm((n, 256), BF), vm((width, ch), BF), vm((n, 256), F32), vm((n, 256), F32), vm((256, cg), F32)],
        flops=8 * n * pix * 256, bytes_=24 << 20,
    )
    got = swap(sent, count)
    d_above, d_below = edges(d_out, count)
    (early,) = call(
        functools.partial(conv_grad_kernel, cl),
        "conv_grad",
        (rows,),
        [(above, None, None), (masked, None, None), (below, None, None), (d_out, one_row(ch), at_y), (grad_out, None, None)],
        [((2, 3 * ch, 384), BF, None, None)],
        [vm((rows + 2, width, ch), BF), vm((3, ch, 3 * cl), F32), vm((3, cl, 3 * cg), F32)],
        flops=18 * pix * (ch * cl + cl * cg), bytes_=7 << 20,
    )
    got, early = tied(got, early)
    got, total, d_above, d_below = tied(got, core_sum(early), d_above, d_below)
    early = core_exchange(total, count)
    sent, grad_freq = call(
        functools.partial(frequency_back_kernel, norm_h, tile),
        "frequency_back",
        (1,),
        [
            (got, None, None), (hc, None, None), (hs, None, None), (w_freq_p, None, None), (w_freq_t, None, None),
            (weight, None, None), (sign, None, None), (stacked, None, None),
        ],
        [((n, 384), BF, None, None), ((384, 384), BF, None, None)],
        [vm((n, 384), BF), vm((256, 384), F32), vm((256, 384), F32)],
        flops=8 * n * n * 384, bytes_=8 << 20,
    )
    sent, early = tied(sent, early)
    got = swap(sent, count)
    (d_conv,) = call(
        functools.partial(conv_back_kernel, cl),
        "conv_back",
        (rows,),
        [(d_above, None, None), (d_out, None, None), (d_below, None, None), (wl_t, None, None), (wc_t, None, None)],
        [(wide, F32, one_row(ch), at_y)],
        [vm((rows + 2, width, 3 * cl), BF), vm((rows + 2, width, 3 * cg), BF)],
        flops=18 * pix * (ch * cl + cl * cg), bytes_=9 << 20,
    )
    got, d_conv, early = tied(got, d_conv, early)
    early = early.astype(F32).sum(0).astype(BF)
    early = core_exchange(jnp.tile(early, (count // 2, 1)), count).reshape(-1, 384)
    late_rows = -(-(3 * 384 + 3 * cs) // (16 * count)) * 16 * count
    d_unit, late = call(
        functools.partial(tail_kernel, norm_w, cl),
        "tail",
        (rows,),
        [
            (got, None, None), (tct, back_table, at_y), (tst, back_table, at_y), (masked, one_row(ch), at_y),
            (d_joined, one_row(256), at_y), (w_in_d, None, None), (grad_freq, None, None),
        ],
        [((rows, width, 256), BF, one_row(256), at_y), ((late_rows, 128), BF, None, None)],
        [vm((n, 256), BF), vm((256, cg), F32)],
        flops=4 * n * pix * 256, bytes_=16 << 20,
    )
    late, early = tied(late, early)
    pairs = lax.axis_size("row")
    other = lax.ppermute(early, "row", [(i, i ^ 1) for i in range(pairs)])
    my_core = (lax.axis_index("row") % 2).astype(jnp.int32).reshape(1, 1)
    late = scatter_sum(late, count)
    (grad_features,) = call(
        functools.partial(finish_kernel, cl),
        "finish",
        (rows,),
        [
            (marked, blocks(128), at_blocks), (d_unit, one_row(256), at_y), (d_conv, one_row(ch), at_y),
            (w_in_t, None, None),
        ],
        [(wide, BF, one_row(ch), at_y)],
        flops=2 * pix * 256 * cg, bytes_=7 << 20,
    )
    late, grad_features = tied(late, grad_features)
    grad_local, grad_cross, grad_out = call(
        functools.partial(unpack_kernel, cl),
        "unpack",
        (1,),
        [(early, None, None), (other, None, None), (my_core, None, None)],
        [((3, 3, ch, cl), F32, None, None), ((9 * cl, cg), F32, None, None), ((cs, cg), F32, None, None)],
        flops=1, bytes_=7 << 20,
    )
    late = gather(late, count)
    late, grad_local, grad_cross, grad_out = tied(late, grad_local, grad_cross, grad_out)
    grad_freq = jnp.concatenate([late[k * 384 : (k + 1) * 384] for k in range(3)], 1).astype(F32)
    at = 3 * 384
    grad_in = jnp.concatenate([late[at + k * cs : at + (k + 1) * cs] for k in range(3)], 1).astype(F32).T
    grad_cross = grad_cross.reshape(3, 3, cl, cg)
    return output[None], grad_features[None], grad_local, grad_cross, grad_in, grad_freq, grad_out


def solution(mesh):
    return jax.shard_map(
        shards,
        mesh=mesh,
        in_specs=(
            P("dp", "row", "col", None),
            P("dp", "row", "col"),
            P("dp", "row", "col", None),
            P(),
            P(),
            P(),
            P(),
            P(),
        ),
        out_specs=(
            P("dp", ("row", "col"), None, None),
            P("dp", ("row", "col"), None, None),
            P("dp", None, None, None),
            P("dp", None, None, None),
            P("dp", None),
            P("dp", None),
            P("dp", None),
        ),
        check_vma=False,
    )
```

```python
import functools
import math

import jax
import jax.numpy as jnp
import numpy as np
from jax import lax
from jax.experimental import pallas as pl
from jax.experimental.pallas import tpu as pltpu
from jax.sharding import PartitionSpec as P

AXES = ("row", "col")
HOLE = 64.0
BF = jnp.bfloat16
F32 = jnp.float32
ROWS_OF = ((0,), (0,))


def dot(a, b, dims=((1,), (0,))):
    return lax.dot_general(a, b, (dims, ((), ())), preferred_element_type=F32)


def line_tables(width, count, lines):
    freq = (lines * np.arange(count)[None] + np.arange(lines)[:, None]).reshape(-1, 1)
    angle = 2.0 * np.pi * (freq * np.arange(width) % width) / width
    valid = freq <= width // 2
    return (np.cos(angle) * valid).astype(BF), (np.sin(angle) * valid).astype(BF)


def column_tables(rows, count):
    h = (rows * np.arange(count)[None] + np.arange(rows)[:, None]).reshape(-1)
    angle = 2.0 * np.pi * (h[:, None] * h[None] % (rows * count)) / (rows * count)
    return np.cos(angle).astype(BF), np.sin(angle).astype(BF)


def slope_and_silu(value):
    sigma = 1.0 / (1.0 + jnp.exp(-value))
    return sigma * (1.0 + value * (1.0 - sigma)), value * sigma


def lanes_below(shape, bound):
    return lax.broadcasted_iota(jnp.int32, shape, 1) < bound


def packed(re, im):
    mid = jnp.where(lanes_below(re[:, 128:].shape, 64), re[:, 128:], im[:, 128:])
    return jnp.concatenate([re[:, :128], mid, im[:, :128]], 1)


def turned(p, q, sign):
    mid = pltpu.roll(q[:, 128:256], 64, 1)
    flip = jnp.where(lanes_below(mid.shape, 64), sign, -sign)
    return jnp.concatenate(
        [p[:, :128] + sign * q[:, 256:], p[:, 128:256] + flip * mid, p[:, 256:] - sign * q[:, :128]], 1
    )


def natural_lanes(x):
    mid, im = x[:, 128:256], pltpu.roll(x[:, 256:], 64, 1)
    low = lanes_below(mid.shape, 64)
    return jnp.concatenate([x[:, :128], jnp.where(low, mid, im), jnp.where(low, im, mid)], 1)


def pack_order(cs):
    return [(0, 128), (128, cs), (cs + 128, 2 * cs), (cs, cs + 128)]


def pack_dim(x, dim, cs):
    return jnp.concatenate([lax.slice_in_dim(x, a, b, axis=dim) for a, b in pack_order(cs)], dim)


def call(body, name, grid, ins, outs, scratch=(), flops=0, bytes_=0):
    def spec(shape, block, index):
        if shape[0] == 1 and shape[-1] < 8:
            return pl.BlockSpec(memory_space=pltpu.SMEM)
        if block is None:
            zeros = (0,) * len(shape)
            return pl.BlockSpec(shape, lambda *_: zeros)
        return pl.BlockSpec(block, index)

    return pl.pallas_call(
        body,
        grid=grid,
        in_specs=[spec(a.shape, block, index) for a, block, index in ins],
        out_specs=[spec(shape, block, index) for shape, _, block, index in outs],
        out_shape=[jax.ShapeDtypeStruct(shape, dtype) for shape, dtype, _, _ in outs],
        scratch_shapes=list(scratch),
        compiler_params=pltpu.CompilerParams(vmem_limit_bytes=56 << 20),
        cost_estimate=pl.CostEstimate(flops=flops, bytes_accessed=bytes_, transcendentals=0),
        name=name,
    )(*[a for a, _, _ in ins])


def put_slots(sizes, z, value_of, sent):
    rows, lines, count, slots = sizes
    for q in range(slots):
        value = value_of(q // lines, q % lines) if q < rows * lines else jnp.zeros((count, 384), F32)
        for k in range(3):
            z[k, pl.ds(q, count, stride=slots), :] = value[:, k * 128 : (k + 1) * 128]
    for k in range(3):
        sent[:, k * 128 : (k + 1) * 128] = z[k].astype(BF)


def spread(got, z):
    for k in range(3):
        z[k] = got[:, k * 128 : (k + 1) * 128].astype(F32)


def slot(sizes, z, q):
    _, _, count, slots = sizes
    return jnp.concatenate([z[k, pl.ds(q, count, stride=slots), :] for k in range(3)], 1)


def take_slots(sizes, got, z, x):
    rows, lines, count, slots = sizes
    spread(got, z)
    for q in range(rows * lines):
        x[q * count : (q + 1) * count, :] = slot(sizes, z, q).astype(BF)


def head_kernel(norm, sizes, cl, marked, w_in, tc, ts, masked, unit, sent, v, z):
    y = pl.program_id(0)
    x = marked[...].reshape(-1, marked.shape[-1])
    keep = x[:, :1].astype(F32) < 0.5 * HOLE
    x = jnp.where(keep, x, jnp.zeros_like(x))
    masked[0] = x
    u = slope_and_silu(dot(x[:, cl:], w_in[...]))[1].astype(BF)
    unit[0] = u
    transform_out(y, norm, sizes, u, tc, ts, sent, v, z)


def transform_out(y, norm, sizes, u, tc, ts, sent, v, z):
    count = sizes[2]
    v[y] = packed(dot(tc[...], u) * norm, dot(ts[...], u) * -norm)

    @pl.when(y == pl.num_programs(0) - 1)
    def _():
        put_slots(sizes, z, lambda row, j: v[row, j * count : (j + 1) * count, :], sent)


def column_line(sizes, z, j):
    rows, lines, count, slots = sizes
    parts = [slot(sizes, z, row * lines + j) for row in range(rows)]
    return jnp.concatenate(parts, 0).astype(BF)


def frequency_kernel(norm, sizes, got, hc, hs, w_freq, weight, sign, stacked, sent, z, v):
    count = sizes[2]
    spread(got, z)
    for j in range(sizes[1]):
        x = column_line(sizes, z, j)
        st = (turned(dot(hc[...], x), dot(hs[...], x), 1.0) * norm).astype(BF)
        stacked[j] = st
        pos = slope_and_silu(dot(st, w_freq[...]))[1]
        neg = slope_and_silu(dot((st.astype(F32) * sign[...]).astype(BF), w_freq[...]))[1]
        x = (weight[0, j] * (pos + sign[...] * neg)).astype(BF)
        v[j] = turned(dot(hc[...], x), dot(hs[...], x), -1.0) * norm
    put_slots(sizes, z, lambda row, j: v[j, row * count : (row + 1) * count, :], sent)


def frequency_back_kernel(
    norm, sizes, got, hc, hs, w_freq, w_freq_t, weight, sign, stacked, sent, grad, z, v, acc_p, acc_m
):
    count = sizes[2]
    spread(got, z)
    for j in range(sizes[1]):
        x = column_line(sizes, z, j)
        dz = turned(dot(hc[...], x), dot(hs[...], x), 1.0) * norm
        st = stacked[j]
        pos = slope_and_silu(dot(st, w_freq[...]))[0]
        neg = slope_and_silu(dot((st.astype(F32) * sign[...]).astype(BF), w_freq[...]))[0]
        pos = (dz * pos).astype(BF).astype(F32)
        neg = (dz * sign[...] * neg).astype(BF).astype(F32)
        total = (weight[0, j] * (pos + neg)).astype(BF)
        delta = (weight[0, j] * (pos - neg)).astype(BF)
        g_p = dot(st[:, :256], total, ROWS_OF)
        g_m = dot(st[:, 128:], delta, ROWS_OF)
        acc_p[...] = g_p if j == 0 else acc_p[...] + g_p
        acc_m[...] = g_m if j == 0 else acc_m[...] + g_m
        re = dot(total, w_freq_t[:, :256])
        im = dot(delta, w_freq_t[:, 128:])
        mid = jnp.where(lanes_below((re.shape[0], 128), 64), re[:, 128:], im[:, :128])
        x = jnp.concatenate([re[:, :128], mid, im[:, 128:]], 1).astype(BF)
        v[j] = turned(dot(hc[...], x), dot(hs[...], x), -1.0) * norm
    put_slots(sizes, z, lambda row, j: v[j, row * count : (row + 1) * count, :], sent)
    grad[0:192, :] = natural_lanes(acc_p[0:192, :]).astype(BF)
    grad[192:320, :] = natural_lanes(acc_m[128:256, :]).astype(BF)
    grad[320:384, :] = natural_lanes(acc_m[64:128, :]).astype(BF)


def imag_first(got):
    mid = pltpu.roll(got[:, 128:256].astype(F32), 64, 1).astype(BF)
    return jnp.concatenate([got[:, 256:], mid], 1)


def line_back(y, norm, sizes, got, tct, tst, z, got_x, got_s):
    @pl.when(y == 0)
    def _():
        take_slots(sizes, got, z, got_x)
        got_s[...] = imag_first(got_x[...])

    size = sizes[1] * sizes[2]
    at = pl.ds(pl.multiple_of(y * size, size), size)
    return ((dot(tct[...], got_x[at, :256]) - dot(tst[...], got_s[at, :])) * norm).astype(BF)


def middle_kernel(
    norm, sizes, cl, cols, got, tct, tst, tc, ts, unit, pre, w_out, w_out_t, my_col, *refs,
):
    cots = refs[:cols]
    output, d_out, d_joined, sent, grad, got_x, got_s, cot, v, z, acc_g = refs[cols:]
    y = pl.program_id(0)
    w = cots[0].shape[1]
    for k in range(cols):
        at = lax.rem(my_col[0, 0] + (cols - k), cols)
        cot[pl.ds(pl.multiple_of(at * w, w), w), :] = cots[k][0]

    back = line_back(y, norm, sizes, got, tct, tst, z, got_x, got_s)
    joined = (unit[0].astype(F32) + back.astype(F32)).astype(BF)
    pre_all = jnp.concatenate([pre[0, :, :cl], pre[0, :, cl:] + dot(joined, w_out[...])], 1)
    slope, silu = slope_and_silu(pre_all)
    output[0] = silu.astype(BF)
    d = (cot[...].astype(F32) * slope).astype(BF)
    d_out[0] = d
    dj = dot(d[:, cl:], w_out_t[...]).astype(BF)
    d_joined[0] = dj
    g = dot(joined, d[:, cl:], ROWS_OF)

    @pl.when(y == 0)
    def _():
        acc_g[...] = g

    @pl.when(y > 0)
    def _():
        acc_g[...] += g

    transform_out(y, norm, sizes, dj, tc, ts, sent, v, z)

    @pl.when(y == pl.num_programs(0) - 1)
    def _():
        grad[...] = acc_g[0 : grad.shape[0], :].astype(BF)


def tail_kernel(
    norm, sizes, cl, got, tct, tst, masked, d_joined, w_in, grad_freq, d_unit, late, got_x, got_s, z, acc_g
):
    y = pl.program_id(0)

    back = line_back(y, norm, sizes, got, tct, tst, z, got_x, got_s)
    x = masked[0, :, cl:]
    slope = slope_and_silu(dot(x, w_in[...]))[0]
    du = ((d_joined[0].astype(F32) + back.astype(F32)) * slope).astype(BF)
    g = dot(du, x, ROWS_OF)

    @pl.when(y == 0)
    def _():
        acc_g[...] = g

    @pl.when(y > 0)
    def _():
        acc_g[...] += g

    d_unit[0] = du

    @pl.when(y == pl.num_programs(0) - 1)
    def _():
        at = 0
        for part, size in ((grad_freq, 384), (acc_g, 192)):
            for k in range(3):
                late[at : at + size, :] = part[0:size, k * 128 : (k + 1) * 128].astype(BF)
                at += size
        late[at:, :] = jnp.zeros((late.shape[0] - at, 128), BF)


def finish_kernel(cl, marked, d_unit, d_conv, w_in_t, grad_features):
    keep = marked[...].reshape(-1, marked.shape[-1])[:, :1].astype(F32) < 0.5 * HOLE
    total = jnp.concatenate([d_conv[0, :, :cl], d_conv[0, :, cl:] + dot(d_unit[0], w_in_t[...])], 1)
    grad_features[0] = jnp.where(keep, total, 0.0).astype(BF)


def shifted(x, step):
    n = x.shape[0]
    at = lax.broadcasted_iota(jnp.int32, x.shape, 0)
    if step == 1:
        return jnp.where(at == 0, 0.0, pltpu.roll(x, 1, 0))
    return jnp.where(at == n - 1, 0.0, pltpu.roll(x, n - 1, 0))


def three(x):
    f = x.astype(F32)
    return jnp.concatenate([shifted(f, -1).astype(BF), x, shifted(f, 1).astype(BF)], 1)


def conv_kernel(cl, above, masked, below, w_local, w_cross, pre, pad):
    y = pl.program_id(0)
    rows = masked.shape[0]

    @pl.when(y == 0)
    def _():
        pad[0] = above[0]
        pad[1 : rows + 1] = masked[...]
        pad[rows + 1] = below[0]

    local = dot(pad[y], w_local[0]) + dot(pad[y + 1], w_local[1]) + dot(pad[y + 2], w_local[2])
    near = jnp.concatenate([pad[y, :, :cl], pad[y + 1, :, :cl], pad[y + 2, :, :cl]], 1)
    cross = dot(near, w_cross[...])
    c, g = cl, w_cross.shape[1] // 3
    pre[0, :, :cl] = shifted(local[:, :c], 1) + local[:, c : 2 * c] + shifted(local[:, 2 * c :], -1)
    pre[0, :, cl:] = shifted(cross[:, :g], 1) + cross[:, g : 2 * g] + shifted(cross[:, 2 * g :], -1)


def conv_grad_kernel(cl, above, masked, below, d_out, g_out, early, pad, acc_l, acc_c):
    y = pl.program_id(0)
    rows = masked.shape[0]

    @pl.when(y == 0)
    def _():
        pad[0] = above[0]
        pad[1 : rows + 1] = masked[...]
        pad[rows + 1] = below[0]
        acc_l[...] = jnp.zeros_like(acc_l)
        acc_c[...] = jnp.zeros_like(acc_c)

    d_local = three(d_out[0, :, :cl])
    d_global = three(d_out[0, :, cl:])
    g = d_global.shape[1] // 3
    for i in range(3):
        x = pad[y + i]
        acc_l[i] += dot(x, d_local, ROWS_OF)
        acc_c[i] += dot(x[:, :cl], d_global, ROWS_OF)

    @pl.when(y == pl.num_programs(0) - 1)
    def _():
        ch = masked.shape[2]
        for i in range(3):
            early[0, i * ch : (i + 1) * ch, :] = acc_l[i].astype(BF)
            for j in range(3):
                at = (3 * i + j) * cl
                early[1, at : at + cl, :] = acc_c[i, :, j * g : (j + 1) * g].astype(BF)
        at, size = 9 * cl, g_out.shape[0]
        early[1, at : at + size, :] = g_out[...]
        early[1, at + size :, :] = jnp.zeros((early.shape[1] - at - size, g), BF)


def unpack_kernel(cl, mine, other, core, g_local, g_cross, g_out):
    ch = g_local.shape[2]

    def write(local, rest):
        for at in range(0, 3 * ch, 64):
            block = local[at : at + 64, :].astype(F32)
            for j in range(3):
                g_local[at // ch, j, at % ch : at % ch + 64, :] = block[:, j * cl : (j + 1) * cl]
        g_cross[...] = rest[0 : 9 * cl, :].astype(F32)
        g_out[...] = rest[9 * cl : 9 * cl + g_out.shape[0], :].astype(F32)

    @pl.when(core[0, 0] == 0)
    def _():
        write(mine, other)

    @pl.when(core[0, 0] == 1)
    def _():
        write(other, mine)


def conv_back_kernel(cl, above, d_out, below, w_local, w_cross, d_conv, pad_l, pad_g):
    y = pl.program_id(0)
    rows = d_out.shape[0]

    @pl.when(y == 0)
    def _():
        for k in range(rows + 2):
            line = above[0] if k == 0 else below[0] if k == rows + 1 else d_out[k - 1]
            pad_l[k] = three(line[:, :cl])
            pad_g[k] = three(line[:, cl:])

    total = dot(pad_l[y + 2], w_local[0]) + dot(pad_l[y + 1], w_local[1]) + dot(pad_l[y], w_local[2])
    cross = dot(pad_g[y + 2], w_cross[0]) + dot(pad_g[y + 1], w_cross[1]) + dot(pad_g[y], w_cross[2])
    d_conv[0, :, :cl] = total[:, :cl] + cross
    d_conv[0, :, cl:] = total[:, cl:]


def swap(x, count):
    return lax.all_to_all(x.reshape(count, -1, x.shape[-1]), AXES, 0, 0, tiled=True).reshape(x.shape)


def to_rows(field, cols):
    h, w, c = field.shape
    return lax.all_to_all(field.reshape(cols, h // cols, w, c), "col", 0, 0, tiled=True)


def turn(field, cols):
    h, w, c = field.shape
    blocks = field.reshape(cols, h // cols, w, c)
    me = lax.axis_index("col")
    out = []
    for k in range(cols):
        part = lax.dynamic_index_in_dim(blocks, (me + k) % cols, 0, keepdims=False)
        out.append(lax.ppermute(part, "col", [(i, (i + k) % cols) for i in range(cols)]) if k else part)
    return out


def core_sum(early):
    pairs = lax.axis_size("row")
    core = lax.axis_index("row") % 2
    mine = lax.dynamic_index_in_dim(early, core, 0, keepdims=False)
    other = lax.dynamic_index_in_dim(early, 1 - core, 0, keepdims=False)
    other = lax.ppermute(other, "row", [(i, i ^ 1) for i in range(pairs)])
    return (mine.astype(F32) + other.astype(F32)).astype(BF)


def core_exchange(x, count):
    pairs = lax.axis_size("row")
    cols = count // pairs
    groups = [[cols * r + c for r in range(k, pairs, 2) for c in range(cols)] for k in range(2)]
    x = x.reshape(count // 2, -1, x.shape[-1])
    return lax.all_to_all(x, AXES, 0, 0, axis_index_groups=groups, tiled=True)


def edges(field, count):
    down = lax.ppermute(field[-1:], AXES, [(i, i + 1) for i in range(count - 1)])
    up = lax.ppermute(field[:1], AXES, [(i + 1, i) for i in range(count - 1)])
    return down, up


def scatter_sum(x, count):
    x = lax.all_to_all(x.reshape(count, -1, x.shape[-1]), AXES, 0, 0, tiled=True)
    return x.astype(F32).sum(0).astype(BF)


def gather(x, count):
    x = lax.all_to_all(jnp.broadcast_to(x[None], (count,) + x.shape), AXES, 0, 0, tiled=True)
    return x.reshape(-1, x.shape[-1])


def tie(value, *after):
    return lax.optimization_barrier((value,) + after)[0]


def tied(*values):
    return lax.optimization_barrier(values)


def shards(features, hole_mask, cotangent, w_local, w_cross, w_in, w_freq, w_out):
    cols = lax.axis_size("col")
    count = lax.axis_size("row") * cols
    me = lax.axis_index(AXES)
    _, h, w, ch = features.shape
    rows, width = h // cols, w * cols
    height = rows * count
    cl, cg, cs = w_local.shape[3], w_cross.shape[3], w_in.shape[1]
    lines = -(-(width // 2 + 1) // count)
    slots = -(-(rows * lines) // 16) * 16
    n = count * slots
    sizes = (rows, lines, count, slots)
    tc, ts = line_tables(width, count, lines)
    tct, tst = jnp.asarray(tc.T), jnp.asarray(ts.T)
    tc, ts = jnp.asarray(tc), jnp.asarray(ts)
    hc, hs = (jnp.asarray(t) for t in column_tables(rows, count))
    norm_w, norm_h = 1.0 / math.sqrt(width), 1.0 / math.sqrt(height)
    freq = lines * me + jnp.arange(lines)
    weight = jnp.where((freq == 0) | (freq * 2 == width), 0.5, jnp.where(freq * 2 < width, 1.0, 0.0))
    weight = weight.astype(F32)[None]
    sign = np.where((np.arange(384) < 192), 1.0, -1.0).astype(np.float32)
    sign = jnp.asarray(sign[None])

    w_in_d = jnp.concatenate([w_in, w_in[:, 128:]], 1)
    w_in_t = jnp.pad(w_in.T, ((0, 64), (0, 0)))
    w_out_z = jnp.pad(w_out, ((0, 64), (0, 0)))
    w_out_t = jnp.concatenate([w_out, w_out[128:]], 0).T
    w_freq_p = pack_dim(pack_dim(w_freq, 0, cs), 1, cs)
    w_freq_t = w_freq_p.T
    wl = jnp.transpose(w_local, (0, 2, 1, 3)).reshape(3, ch, 3 * cl)
    wc = jnp.transpose(w_cross, (0, 2, 1, 3)).reshape(3 * cl, 3 * cg)
    wl_t = jnp.transpose(w_local, (0, 1, 3, 2)).reshape(3, 3 * cl, ch)
    wc_t = jnp.transpose(w_cross, (0, 1, 3, 2)).reshape(3, 3 * cg, cl)

    at_y = lambda y: (y, 0, 0)
    one_row = lambda c: (1, width, c)
    blocks = lambda c: (cols, 1, w, c)
    at_blocks = lambda y: (0, y, 0, 0)
    wide = (rows, width, ch)
    pix = rows * width
    vm = pltpu.VMEM
    lined = (rows, lines * count, 384)
    spectral = (lines, height, 384)
    used = rows * lines * count

    marked = jnp.where(hole_mask[0][..., None] == 1, HOLE, features[0]).astype(BF)
    marked = to_rows(marked, cols)
    w_in_d, w_in_t, w_out_z, w_out_t, w_freq_p, w_freq_t, wl, wc, wl_t, wc_t, weight = tied(
        w_in_d, w_in_t, w_out_z, w_out_t, w_freq_p, w_freq_t, wl, wc, wl_t, wc_t, weight
    )
    cots = turn(tie(cotangent[0], marked), cols)
    my_col = lax.axis_index("col").astype(jnp.int32).reshape(1, 1)

    masked, unit, sent = call(
        functools.partial(head_kernel, norm_w, sizes, cl),
        "head",
        (rows,),
        [(marked, blocks(ch), at_blocks), (w_in_d, None, None), (tc, None, None), (ts, None, None)],
        [(wide, BF, one_row(ch), at_y), ((rows, width, 256), BF, one_row(256), at_y), ((n, 384), BF, None, None)],
        [vm(lined, F32), vm((3, n, 128), F32)],
        flops=1 << 30, bytes_=6 << 20,
    )
    above, below = edges(masked, count)
    got = tie(swap(sent, count), above, below)
    (pre,) = call(
        functools.partial(conv_kernel, cl),
        "conv",
        (rows,),
        [(above, None, None), (masked, None, None), (below, None, None), (wl, None, None), (wc, None, None)],
        [(wide, F32, one_row(ch), at_y)],
        [vm((rows + 2, width, ch), BF)],
        flops=18 * pix * (ch * cl + cl * cg), bytes_=9 << 20,
    )
    stacked, sent = call(
        functools.partial(frequency_kernel, norm_h, sizes),
        "frequency",
        (1,),
        [(got, None, None), (hc, None, None), (hs, None, None), (w_freq_p, None, None), (weight, None, None), (sign, None, None)],
        [(spectral, BF, None, None), ((n, 384), BF, None, None)],
        [vm((3, n, 128), F32), vm(spectral, F32)],
        flops=3 << 30, bytes_=7 << 20,
    )
    sent, *cots = tied(sent, *cots)
    got = swap(sent, count)
    output, d_out, d_joined, sent, grad_out = call(
        functools.partial(middle_kernel, norm_w, sizes, cl, cols),
        "middle",
        (rows,),
        [
            (got, None, None), (tct, None, None), (tst, None, None), (tc, None, None),
            (ts, None, None), (unit, one_row(256), at_y), (pre, one_row(ch), at_y),
            (w_out_z, None, None), (w_out_t, None, None), (my_col, None, None),
        ]
        + [(c, (1, w, ch), at_y) for c in cots],
        [
            (wide, BF, one_row(ch), at_y), (wide, BF, one_row(ch), at_y), ((rows, width, 256), BF, one_row(256), at_y),
            ((n, 384), BF, None, None), ((cs, cg), BF, None, None),
        ],
        [vm((used, 384), BF), vm((used, 256), BF), vm((width, ch), BF), vm(lined, F32), vm((3, n, 128), F32), vm((256, cg), F32)],
        flops=3 << 30, bytes_=12 << 20,
    )
    got = swap(sent, count)
    d_above, d_below = edges(d_out, count)
    (early,) = call(
        functools.partial(conv_grad_kernel, cl),
        "conv_grad",
        (rows,),
        [(above, None, None), (masked, None, None), (below, None, None), (d_out, one_row(ch), at_y), (grad_out, None, None)],
        [((2, 3 * ch, 384), BF, None, None)],
        [vm((rows + 2, width, ch), BF), vm((3, ch, 3 * cl), F32), vm((3, cl, 3 * cg), F32)],
        flops=18 * pix * (ch * cl + cl * cg), bytes_=7 << 20,
    )
    got, early, d_above, d_below = tied(got, early, d_above, d_below)
    got, total = tied(got, core_sum(early))
    early = core_exchange(total, count)
    sent, grad_freq = call(
        functools.partial(frequency_back_kernel, norm_h, sizes),
        "frequency_back",
        (1,),
        [
            (got, None, None), (hc, None, None), (hs, None, None), (w_freq_p, None, None), (w_freq_t, None, None),
            (weight, None, None), (sign, None, None), (stacked, None, None),
        ],
        [((n, 384), BF, None, None), ((384, 384), BF, None, None)],
        [vm((3, n, 128), F32), vm(spectral, F32), vm((256, 384), F32), vm((256, 384), F32)],
        flops=3 << 30, bytes_=8 << 20,
    )
    sent, early = tied(sent, early)
    got = swap(sent, count)
    (d_conv,) = call(
        functools.partial(conv_back_kernel, cl),
        "conv_back",
        (rows,),
        [(d_above, None, None), (d_out, None, None), (d_below, None, None), (wl_t, None, None), (wc_t, None, None)],
        [(wide, F32, one_row(ch), at_y)],
        [vm((rows + 2, width, 3 * cl), BF), vm((rows + 2, width, 3 * cg), BF)],
        flops=18 * pix * (ch * cl + cl * cg), bytes_=9 << 20,
    )
    got, d_conv, early = tied(got, d_conv, early)
    early = early.astype(F32).sum(0).astype(BF)
    early = core_exchange(jnp.tile(early, (count // 2, 1)), count).reshape(-1, 384)
    late_rows = -(-(3 * 384 + 3 * cs) // (16 * count)) * 16 * count
    d_unit, late = call(
        functools.partial(tail_kernel, norm_w, sizes, cl),
        "tail",
        (rows,),
        [
            (got, None, None), (tct, None, None), (tst, None, None), (masked, one_row(ch), at_y),
            (d_joined, one_row(256), at_y), (w_in_d, None, None), (grad_freq, None, None),
        ],
        [((rows, width, 256), BF, one_row(256), at_y), ((late_rows, 128), BF, None, None)],
        [vm((used, 384), BF), vm((used, 256), BF), vm((3, n, 128), F32), vm((256, cg), F32)],
        flops=1 << 30, bytes_=5 << 20,
    )
    late, early = tied(late, early)
    pairs = lax.axis_size("row")
    other = lax.ppermute(early, "row", [(i, i ^ 1) for i in range(pairs)])
    my_core = (lax.axis_index("row") % 2).astype(jnp.int32).reshape(1, 1)
    late = scatter_sum(late, count)
    (grad_features,) = call(
        functools.partial(finish_kernel, cl),
        "finish",
        (rows,),
        [
            (marked, blocks(128), at_blocks), (d_unit, one_row(256), at_y), (d_conv, one_row(ch), at_y),
            (w_in_t, None, None),
        ],
        [(wide, BF, one_row(ch), at_y)],
        flops=2 * pix * 256 * cg, bytes_=7 << 20,
    )
    late, grad_features = tied(late, grad_features)
    grad_local, grad_cross, grad_out = call(
        functools.partial(unpack_kernel, cl),
        "unpack",
        (1,),
        [(early, None, None), (other, None, None), (my_core, None, None)],
        [((3, 3, ch, cl), F32, None, None), ((9 * cl, cg), F32, None, None), ((cs, cg), F32, None, None)],
        flops=1, bytes_=7 << 20,
    )
    late = gather(late, count)
    late, grad_local, grad_cross, grad_out = tied(late, grad_local, grad_cross, grad_out)
    grad_freq = jnp.concatenate([late[k * 384 : (k + 1) * 384] for k in range(3)], 1).astype(F32)
    at = 3 * 384
    grad_in = jnp.concatenate([late[at + k * cs : at + (k + 1) * cs] for k in range(3)], 1).astype(F32).T
    grad_cross = grad_cross.reshape(3, 3, cl, cg)
    return output[None], grad_features[None], grad_local, grad_cross, grad_in, grad_freq, grad_out


def solution(mesh):
    return jax.shard_map(
        shards,
        mesh=mesh,
        in_specs=(
            P("dp", "row", "col", None),
            P("dp", "row", "col"),
            P("dp", "row", "col", None),
            P(),
            P(),
            P(),
            P(),
            P(),
        ),
        out_specs=(
            P("dp", ("row", "col"), None, None),
            P("dp", ("row", "col"), None, None),
            P("dp", None, None, None),
            P("dp", None, None, None),
            P("dp", None),
            P("dp", None),
            P("dp", None),
        ),
        check_vma=False,
    )
```

```python
import functools
import math

import jax
import jax.numpy as jnp
import numpy as np
from jax import lax
from jax.experimental import pallas as pl
from jax.experimental.pallas import tpu as pltpu
from jax.sharding import PartitionSpec as P

AXES = ("row", "col")
HOLE = 64.0
BF = jnp.bfloat16
F32 = jnp.float32
ROWS_OF = ((0,), (0,))


def dot(a, b, dims=((1,), (0,))):
    return lax.dot_general(a, b, (dims, ((), ())), preferred_element_type=F32)


def line_tables(width, count, lines):
    freq = (lines * np.arange(count)[None] + np.arange(lines)[:, None]).reshape(-1, 1)
    angle = 2.0 * np.pi * (freq * np.arange(width) % width) / width
    valid = freq <= width // 2
    return (np.cos(angle) * valid).astype(BF), (np.sin(angle) * valid).astype(BF)


def column_tables(rows, count):
    h = (rows * np.arange(count)[None] + np.arange(rows)[:, None]).reshape(-1)
    angle = 2.0 * np.pi * (h[:, None] * h[None] % (rows * count)) / (rows * count)
    return np.cos(angle).astype(BF), np.sin(angle).astype(BF)


def slope_and_silu(value):
    sigma = 1.0 / (1.0 + jnp.exp(-value))
    return sigma * (1.0 + value * (1.0 - sigma)), value * sigma


def lanes_below(shape, bound):
    return lax.broadcasted_iota(jnp.int32, shape, 1) < bound


def packed(re, im):
    mid = jnp.where(lanes_below(re[:, 128:].shape, 64), re[:, 128:], im[:, 128:])
    return jnp.concatenate([re[:, :128], mid, im[:, :128]], 1)


def turned(p, q, sign):
    mid = pltpu.roll(q[:, 128:256], 64, 1)
    flip = jnp.where(lanes_below(mid.shape, 64), sign, -sign)
    return jnp.concatenate(
        [p[:, :128] + sign * q[:, 256:], p[:, 128:256] + flip * mid, p[:, 256:] - sign * q[:, :128]], 1
    )


def natural_lanes(x):
    mid, im = x[:, 128:256], pltpu.roll(x[:, 256:], 64, 1)
    low = lanes_below(mid.shape, 64)
    return jnp.concatenate([x[:, :128], jnp.where(low, mid, im), jnp.where(low, im, mid)], 1)


def pack_order(cs):
    return [(0, 128), (128, cs), (cs + 128, 2 * cs), (cs, cs + 128)]


def pack_dim(x, dim, cs):
    return jnp.concatenate([lax.slice_in_dim(x, a, b, axis=dim) for a, b in pack_order(cs)], dim)


def call(body, name, grid, ins, outs, scratch=(), flops=0, bytes_=0):
    def spec(shape, block, index):
        if shape[0] == 1 and shape[-1] < 8:
            return pl.BlockSpec(memory_space=pltpu.SMEM)
        if block is None:
            zeros = (0,) * len(shape)
            return pl.BlockSpec(shape, lambda *_: zeros)
        return pl.BlockSpec(block, index)

    return pl.pallas_call(
        body,
        grid=grid,
        in_specs=[spec(a.shape, block, index) for a, block, index in ins],
        out_specs=[spec(shape, block, index) for shape, _, block, index in outs],
        out_shape=[jax.ShapeDtypeStruct(shape, dtype) for shape, dtype, _, _ in outs],
        scratch_shapes=list(scratch),
        compiler_params=pltpu.CompilerParams(vmem_limit_bytes=56 << 20),
        cost_estimate=pl.CostEstimate(flops=flops, bytes_accessed=bytes_, transcendentals=0),
        name=name,
    )(*[a for a, _, _ in ins])


def put_slots(sizes, z, value_of, sent):
    rows, lines, count, slots = sizes
    for q in range(slots):
        value = value_of(q // lines, q % lines) if q < rows * lines else jnp.zeros((count, 384), F32)
        for k in range(3):
            z[k, pl.ds(q, count, stride=slots), :] = value[:, k * 128 : (k + 1) * 128]
    for k in range(3):
        sent[:, k * 128 : (k + 1) * 128] = z[k].astype(BF)


def spread(got, z):
    for k in range(3):
        z[k] = got[:, k * 128 : (k + 1) * 128].astype(F32)


def slot(sizes, z, q):
    _, _, count, slots = sizes
    return jnp.concatenate([z[k, pl.ds(q, count, stride=slots), :] for k in range(3)], 1)


def take_slots(sizes, got, z, x):
    rows, lines, count, slots = sizes
    spread(got, z)
    for q in range(rows * lines):
        x[q * count : (q + 1) * count, :] = slot(sizes, z, q).astype(BF)


def kept(x):
    keep = x[:, :1].astype(F32) < 0.5 * HOLE
    return jnp.where(keep, x, jnp.zeros_like(x)), keep


def unit_kernel(cl, marked, w_in, unit):
    x = kept(marked[...].reshape(-1, marked.shape[-1]))[0]
    u = slope_and_silu(dot(x[:, cl:], w_in[...]))[1].astype(BF)
    unit[...] = u.reshape(unit.shape)


def front_kernel(norm, sizes, unit, tc, ts, sent, v, z):
    u = unit[...].reshape(-1, unit.shape[-1])
    transform_out(pl.program_id(0), norm, sizes, u, tc, ts, sent, v, z)


def place(parts, my_col, line):
    w = parts[0].shape[1]
    for k, part in enumerate(parts):
        at = lax.rem(my_col[0, 0] + (len(parts) - k), len(parts))
        line[pl.ds(pl.multiple_of(at * w, w), w), :] = part[0]


def rows_kernel(cols, my_col, *refs):
    masked, marks, line = refs[cols:]
    place(refs[:cols], my_col, line)
    x = line[...]
    marks[0] = x[:, :128]
    masked[0] = kept(x)[0]


def transform_out(y, norm, sizes, u, tc, ts, sent, v, z):
    count = sizes[2]
    v[y] = packed(dot(tc[...], u) * norm, dot(ts[...], u) * -norm)

    @pl.when(y == pl.num_programs(0) - 1)
    def _():
        put_slots(sizes, z, lambda row, j: v[row, j * count : (j + 1) * count, :], sent)


def column_line(sizes, z, j):
    rows, lines, count, slots = sizes
    parts = [slot(sizes, z, row * lines + j) for row in range(rows)]
    return jnp.concatenate(parts, 0).astype(BF)


def frequency_kernel(norm, sizes, got, hc, hs, w_freq, weight, sign, stacked, sent, z, v):
    count = sizes[2]
    spread(got, z)
    for j in range(sizes[1]):
        x = column_line(sizes, z, j)
        st = (turned(dot(hc[...], x), dot(hs[...], x), 1.0) * norm).astype(BF)
        stacked[j] = st
        pos = slope_and_silu(dot(st, w_freq[...]))[1]
        neg = slope_and_silu(dot((st.astype(F32) * sign[...]).astype(BF), w_freq[...]))[1]
        x = (weight[0, j] * (pos + sign[...] * neg)).astype(BF)
        v[j] = turned(dot(hc[...], x), dot(hs[...], x), -1.0) * norm
    put_slots(sizes, z, lambda row, j: v[j, row * count : (row + 1) * count, :], sent)


def frequency_back_kernel(
    norm, sizes, got, hc, hs, w_freq, w_freq_t, weight, sign, stacked, sent, grad, z, v, acc_p, acc_m
):
    count = sizes[2]
    spread(got, z)
    for j in range(sizes[1]):
        x = column_line(sizes, z, j)
        dz = turned(dot(hc[...], x), dot(hs[...], x), 1.0) * norm
        st = stacked[j]
        pos = slope_and_silu(dot(st, w_freq[...]))[0]
        neg = slope_and_silu(dot((st.astype(F32) * sign[...]).astype(BF), w_freq[...]))[0]
        pos = (dz * pos).astype(BF).astype(F32)
        neg = (dz * sign[...] * neg).astype(BF).astype(F32)
        total = (weight[0, j] * (pos + neg)).astype(BF)
        delta = (weight[0, j] * (pos - neg)).astype(BF)
        g_p = dot(st[:, :256], total, ROWS_OF)
        g_m = dot(st[:, 128:], delta, ROWS_OF)
        acc_p[...] = g_p if j == 0 else acc_p[...] + g_p
        acc_m[...] = g_m if j == 0 else acc_m[...] + g_m
        re = dot(total, w_freq_t[:, :256])
        im = dot(delta, w_freq_t[:, 128:])
        mid = jnp.where(lanes_below((re.shape[0], 128), 64), re[:, 128:], im[:, :128])
        x = jnp.concatenate([re[:, :128], mid, im[:, 128:]], 1).astype(BF)
        v[j] = turned(dot(hc[...], x), dot(hs[...], x), -1.0) * norm
    put_slots(sizes, z, lambda row, j: v[j, row * count : (row + 1) * count, :], sent)
    grad[0:192, :] = natural_lanes(acc_p[0:192, :]).astype(BF)
    grad[192:320, :] = natural_lanes(acc_m[128:256, :]).astype(BF)
    grad[320:384, :] = natural_lanes(acc_m[64:128, :]).astype(BF)


def imag_first(got):
    mid = pltpu.roll(got[:, 128:256].astype(F32), 64, 1).astype(BF)
    return jnp.concatenate([got[:, 256:], mid], 1)


def line_back(y, norm, sizes, got, tct, tst, z, got_x, got_s):
    @pl.when(y == 0)
    def _():
        take_slots(sizes, got, z, got_x)
        got_s[...] = imag_first(got_x[...])

    size = sizes[1] * sizes[2]
    at = pl.ds(pl.multiple_of(y * size, size), size)
    return ((dot(tct[...], got_x[at, :256]) - dot(tst[...], got_s[at, :])) * norm).astype(BF)


def middle_kernel(
    norm, sizes, cl, cols, got, tct, tst, tc, ts, unit, pre, w_out, w_out_t, my_col, *refs,
):
    cots = refs[:cols]
    output, d_out, d_joined, sent, grad, got_x, got_s, cot, v, z, acc_g = refs[cols:]
    y = pl.program_id(0)
    place(cots, my_col, cot)

    back = line_back(y, norm, sizes, got, tct, tst, z, got_x, got_s)
    joined = (unit[...].reshape(back.shape).astype(F32) + back.astype(F32)).astype(BF)
    pre_all = jnp.concatenate([pre[0, :, :cl], pre[0, :, cl:] + dot(joined, w_out[...])], 1)
    slope, silu = slope_and_silu(pre_all)
    output[0] = silu.astype(BF)
    d = (cot[...].astype(F32) * slope).astype(BF)
    d_out[0] = d
    dj = dot(d[:, cl:], w_out_t[...]).astype(BF)
    d_joined[0] = dj
    g = dot(joined, d[:, cl:], ROWS_OF)

    @pl.when(y == 0)
    def _():
        acc_g[...] = g

    @pl.when(y > 0)
    def _():
        acc_g[...] += g

    transform_out(y, norm, sizes, dj, tc, ts, sent, v, z)

    @pl.when(y == pl.num_programs(0) - 1)
    def _():
        grad[...] = acc_g[0 : grad.shape[0], :].astype(BF)


def tail_kernel(
    norm, sizes, cl, got, tct, tst, masked, d_joined, w_in, grad_freq, d_unit, late, got_x, got_s, z, acc_g
):
    y = pl.program_id(0)

    back = line_back(y, norm, sizes, got, tct, tst, z, got_x, got_s)
    x = masked[0, :, cl:]
    slope = slope_and_silu(dot(x, w_in[...]))[0]
    du = ((d_joined[0].astype(F32) + back.astype(F32)) * slope).astype(BF)
    g = dot(du, x, ROWS_OF)

    @pl.when(y == 0)
    def _():
        acc_g[...] = g

    @pl.when(y > 0)
    def _():
        acc_g[...] += g

    d_unit[0] = du

    @pl.when(y == pl.num_programs(0) - 1)
    def _():
        at = 0
        for part, size in ((grad_freq, 384), (acc_g, 192)):
            for k in range(3):
                late[at : at + size, :] = part[0:size, k * 128 : (k + 1) * 128].astype(BF)
                at += size
        late[at:, :] = jnp.zeros((late.shape[0] - at, 128), BF)


def finish_kernel(cl, marked, d_unit, d_conv, w_in_t, grad_features):
    keep = kept(marked[0])[1]
    total = jnp.concatenate([d_conv[0, :, :cl], d_conv[0, :, cl:] + dot(d_unit[0], w_in_t[...])], 1)
    grad_features[0] = jnp.where(keep, total, 0.0).astype(BF)


def shifted(x, step):
    n = x.shape[0]
    at = lax.broadcasted_iota(jnp.int32, x.shape, 0)
    if step == 1:
        return jnp.where(at == 0, 0.0, pltpu.roll(x, 1, 0))
    return jnp.where(at == n - 1, 0.0, pltpu.roll(x, n - 1, 0))


def three(x):
    f = x.astype(F32)
    return jnp.concatenate([shifted(f, -1).astype(BF), x, shifted(f, 1).astype(BF)], 1)


def conv_kernel(cl, above, masked, below, w_local, w_cross, pre, pad):
    y = pl.program_id(0)
    rows = masked.shape[0]

    @pl.when(y == 0)
    def _():
        pad[0] = above[0]
        pad[1 : rows + 1] = masked[...]
        pad[rows + 1] = below[0]

    local = dot(pad[y], w_local[0]) + dot(pad[y + 1], w_local[1]) + dot(pad[y + 2], w_local[2])
    near = jnp.concatenate([pad[y, :, :cl], pad[y + 1, :, :cl], pad[y + 2, :, :cl]], 1)
    cross = dot(near, w_cross[...])
    c, g = cl, w_cross.shape[1] // 3
    pre[0, :, :cl] = shifted(local[:, :c], 1) + local[:, c : 2 * c] + shifted(local[:, 2 * c :], -1)
    pre[0, :, cl:] = shifted(cross[:, :g], 1) + cross[:, g : 2 * g] + shifted(cross[:, 2 * g :], -1)


def conv_grad_kernel(cl, above, masked, below, d_out, g_out, early, pad, acc_l, acc_c):
    y = pl.program_id(0)
    rows = masked.shape[0]

    @pl.when(y == 0)
    def _():
        pad[0] = above[0]
        pad[1 : rows + 1] = masked[...]
        pad[rows + 1] = below[0]
        acc_l[...] = jnp.zeros_like(acc_l)
        acc_c[...] = jnp.zeros_like(acc_c)

    d_local = three(d_out[0, :, :cl])
    d_global = three(d_out[0, :, cl:])
    g = d_global.shape[1] // 3
    for i in range(3):
        x = pad[y + i]
        acc_l[i] += dot(x, d_local, ROWS_OF)
        acc_c[i] += dot(x[:, :cl], d_global, ROWS_OF)

    @pl.when(y == pl.num_programs(0) - 1)
    def _():
        ch = masked.shape[2]
        for i in range(3):
            early[0, i * ch : (i + 1) * ch, :] = acc_l[i].astype(BF)
            for j in range(3):
                at = (3 * i + j) * cl
                early[1, at : at + cl, :] = acc_c[i, :, j * g : (j + 1) * g].astype(BF)
        at, size = 9 * cl, g_out.shape[0]
        early[1, at : at + size, :] = g_out[...]
        early[1, at + size :, :] = jnp.zeros((early.shape[1] - at - size, g), BF)


def unpack_kernel(cl, mine, other, core, g_local, g_cross, g_out):
    ch = g_local.shape[2]

    def write(local, rest):
        for at in range(0, 3 * ch, 64):
            block = local[at : at + 64, :].astype(F32)
            for j in range(3):
                g_local[at // ch, j, at % ch : at % ch + 64, :] = block[:, j * cl : (j + 1) * cl]
        g_cross[...] = rest[0 : 9 * cl, :].astype(F32)
        g_out[...] = rest[9 * cl : 9 * cl + g_out.shape[0], :].astype(F32)

    @pl.when(core[0, 0] == 0)
    def _():
        write(mine, other)

    @pl.when(core[0, 0] == 1)
    def _():
        write(other, mine)


def conv_back_kernel(cl, above, d_out, below, w_local, w_cross, d_conv, pad_l, pad_g):
    y = pl.program_id(0)
    rows = d_out.shape[0]

    @pl.when(y == 0)
    def _():
        for k in range(rows + 2):
            line = above[0] if k == 0 else below[0] if k == rows + 1 else d_out[k - 1]
            pad_l[k] = three(line[:, :cl])
            pad_g[k] = three(line[:, cl:])

    total = dot(pad_l[y + 2], w_local[0]) + dot(pad_l[y + 1], w_local[1]) + dot(pad_l[y], w_local[2])
    cross = dot(pad_g[y + 2], w_cross[0]) + dot(pad_g[y + 1], w_cross[1]) + dot(pad_g[y], w_cross[2])
    d_conv[0, :, :cl] = total[:, :cl] + cross
    d_conv[0, :, cl:] = total[:, cl:]


def swap(x, count):
    return lax.all_to_all(x.reshape(count, -1, x.shape[-1]), AXES, 0, 0, tiled=True).reshape(x.shape)


def turned(p, q, sign):
    mid = pltpu.roll(q[:, 128:256], 64, 1)
    flip = jnp.where(lanes_below(mid.shape, 64), sign, -sign)
    return jnp.concatenate(
        [p[:, :128] + sign * q[:, 256:], p[:, 128:256] + flip * mid, p[:, 256:] - sign * q[:, :128]], 1
    )


def natural_lanes(x):
    mid, im = x[:, 128:256], pltpu.roll(x[:, 256:], 64, 1)
    low = lanes_below(mid.shape, 64)
    return jnp.concatenate([x[:, :128], jnp.where(low, mid, im), jnp.where(low, im, mid)], 1)


def pack_order(cs):
    return [(0, 128), (128, cs), (cs + 128, 2 * cs), (cs, cs + 128)]


def pack_dim(x, dim, cs):
    return jnp.concatenate([lax.slice_in_dim(x, a, b, axis=dim) for a, b in pack_order(cs)], dim)


def call(body, name, grid, ins, outs, scratch=(), flops=0, bytes_=0):
    def spec(shape, block, index):
        if shape[0] == 1 and shape[-1] < 8:
            return pl.BlockSpec(memory_space=pltpu.SMEM)
        if block is None:
            zeros = (0,) * len(shape)
            return pl.BlockSpec(shape, lambda *_: zeros)
        return pl.BlockSpec(block, index)

    return pl.pallas_call(
        body,
        grid=grid,
        in_specs=[spec(a.shape, block, index) for a, block, index in ins],
        out_specs=[spec(shape, block, index) for shape, _, block, index in outs],
        out_shape=[jax.ShapeDtypeStruct(shape, dtype) for shape, dtype, _, _ in outs],
        scratch_shapes=list(scratch),
        compiler_params=pltpu.CompilerParams(vmem_limit_bytes=56 << 20),
        cost_estimate=pl.CostEstimate(flops=flops, bytes_accessed=bytes_, transcendentals=0),
        name=name,
    )(*[a for a, _, _ in ins])


def put_slots(sizes, z, value_of, sent):
    rows, lines, count, slots = sizes
    for q in range(slots):
        value = value_of(q // lines, q % lines) if q < rows * lines else jnp.zeros((count, 384), F32)
        for k in range(3):
            z[k, pl.ds(q, count, stride=slots), :] = value[:, k * 128 : (k + 1) * 128]
    for k in range(3):
        sent[:, k * 128 : (k + 1) * 128] = z[k].astype(BF)


def spread(got, z):
    for k in range(3):
        z[k] = got[:, k * 128 : (k + 1) * 128].astype(F32)


def slot(sizes, z, q):
    _, _, count, slots = sizes
    return jnp.concatenate([z[k, pl.ds(q, count, stride=slots), :] for k in range(3)], 1)


def take_slots(sizes, got, z, x):
    rows, lines, count, slots = sizes
    spread(got, z)
    for q in range(rows * lines):
        x[q * count : (q + 1) * count, :] = slot(sizes, z, q).astype(BF)


def kept(x):
    keep = x[:, :1].astype(F32) < 0.5 * HOLE
    return jnp.where(keep, x, jnp.zeros_like(x)), keep


def unit_kernel(cl, marked, w_in, unit):
    x = kept(marked[...].reshape(-1, marked.shape[-1]))[0]
    u = slope_and_silu(dot(x[:, cl:], w_in[...]))[1].astype(BF)
    unit[...] = u.reshape(unit.shape)


def front_kernel(norm, sizes, unit, tc, ts, sent, v, z):
    u = unit[...].reshape(-1, unit.shape[-1])
    transform_out(pl.program_id(0), norm, sizes, u, tc, ts, sent, v, z)


def place(parts, my_col, line):
    w = parts[0].shape[1]
    for k, part in enumerate(parts):
        at = lax.rem(my_col[0, 0] + (len(parts) - k), len(parts))
        line[pl.ds(pl.multiple_of(at * w, w), w), :] = part[0]


def rows_kernel(cols, my_col, *refs):
    masked, marks, line = refs[cols:]
    place(refs[:cols], my_col, line)
    x = line[...]
    marks[0] = x[:, :128]
    masked[0] = kept(x)[0]


def transform_out(y, norm, sizes, u, tc, ts, sent, v, z):
    count = sizes[2]
    v[y] = packed(dot(tc[...], u) * norm, dot(ts[...], u) * -norm)

    @pl.when(y == pl.num_programs(0) - 1)
    def _():
        put_slots(sizes, z, lambda row, j: v[row, j * count : (j + 1) * count, :], sent)


def column_line(sizes, z, j):
    rows, lines, count, slots = sizes
    parts = [slot(sizes, z, row * lines + j) for row in range(rows)]
    return jnp.concatenate(parts, 0).astype(BF)


def frequency_kernel(norm, sizes, got, hc, hs, w_freq, weight, sign, stacked, sent, z, v):
    count = sizes[2]
    spread(got, z)
    for j in range(sizes[1]):
        x = column_line(sizes, z, j)
        st = (turned(dot(hc[...], x), dot(hs[...], x), 1.0) * norm).astype(BF)
        stacked[j] = st
        pos = slope_and_silu(dot(st, w_freq[...]))[1]
        neg = slope_and_silu(dot((st.astype(F32) * sign[...]).astype(BF), w_freq[...]))[1]
        x = (weight[0, j] * (pos + sign[...] * neg)).astype(BF)
        v[j] = turned(dot(hc[...], x), dot(hs[...], x), -1.0) * norm
    put_slots(sizes, z, lambda row, j: v[j, row * count : (row + 1) * count, :], sent)


def frequency_back_kernel(
    norm, sizes, got, hc, hs, w_freq, w_freq_t, weight, sign, stacked, sent, grad, z, v, acc_p, acc_m
):
    count = sizes[2]
    spread(got, z)
    for j in range(sizes[1]):
        x = column_line(sizes, z, j)
        dz = turned(dot(hc[...], x), dot(hs[...], x), 1.0) * norm
        st = stacked[j]
        pos = slope_and_silu(dot(st, w_freq[...]))[0]
        neg = slope_and_silu(dot((st.astype(F32) * sign[...]).astype(BF), w_freq[...]))[0]
        pos = (dz * pos).astype(BF).astype(F32)
        neg = (dz * sign[...] * neg).astype(BF).astype(F32)
        total = (weight[0, j] * (pos + neg)).astype(BF)
        delta = (weight[0, j] * (pos - neg)).astype(BF)
        g_p = dot(st[:, :256], total, ROWS_OF)
        g_m = dot(st[:, 128:], delta, ROWS_OF)
        acc_p[...] = g_p if j == 0 else acc_p[...] + g_p
        acc_m[...] = g_m if j == 0 else acc_m[...] + g_m
        re = dot(total, w_freq_t[:, :256])
        im = dot(delta, w_freq_t[:, 128:])
        mid = jnp.where(lanes_below((re.shape[0], 128), 64), re[:, 128:], im[:, :128])
        x = jnp.concatenate([re[:, :128], mid, im[:, 128:]], 1).astype(BF)
        v[j] = turned(dot(hc[...], x), dot(hs[...], x), -1.0) * norm
    put_slots(sizes, z, lambda row, j: v[j, row * count : (row + 1) * count, :], sent)
    grad[0:192, :] = natural_lanes(acc_p[0:192, :]).astype(BF)
    grad[192:320, :] = natural_lanes(acc_m[128:256, :]).astype(BF)
    grad[320:384, :] = natural_lanes(acc_m[64:128, :]).astype(BF)


def imag_first(got):
    mid = pltpu.roll(got[:, 128:256].astype(F32), 64, 1).astype(BF)
    return jnp.concatenate([got[:, 256:], mid], 1)


def line_back(y, norm, sizes, got, tct, tst, z, got_x, got_s):
    @pl.when(y == 0)
    def _():
        take_slots(sizes, got, z, got_x)
        got_s[...] = imag_first(got_x[...])

    size = sizes[1] * sizes[2]
    at = pl.ds(pl.multiple_of(y * size, size), size)
    return ((dot(tct[...], got_x[at, :256]) - dot(tst[...], got_s[at, :])) * norm).astype(BF)


def middle_kernel(
    norm, sizes, cl, cols, got, tct, tst, tc, ts, unit, pre, w_out, w_out_t, my_col, *refs,
):
    cots = refs[:cols]
    output, d_out, d_joined, sent, grad, got_x, got_s, cot, v, z, acc_g = refs[cols:]
    y = pl.program_id(0)
    place(cots, my_col, cot)

    back = line_back(y, norm, sizes, got, tct, tst, z, got_x, got_s)
    joined = (unit[...].reshape(back.shape).astype(F32) + back.astype(F32)).astype(BF)
    pre_all = jnp.concatenate([pre[0, :, :cl], pre[0, :, cl:] + dot(joined, w_out[...])], 1)
    slope, silu = slope_and_silu(pre_all)
    output[0] = silu.astype(BF)
    d = (cot[...].astype(F32) * slope).astype(BF)
    d_out[0] = d
    dj = dot(d[:, cl:], w_out_t[...]).astype(BF)
    d_joined[0] = dj
    g = dot(joined, d[:, cl:], ROWS_OF)

    @pl.when(y == 0)
    def _():
        acc_g[...] = g

    @pl.when(y > 0)
    def _():
        acc_g[...] += g

    transform_out(y, norm, sizes, dj, tc, ts, sent, v, z)

    @pl.when(y == pl.num_programs(0) - 1)
    def _():
        grad[...] = acc_g[0 : grad.shape[0], :].astype(BF)


def tail_kernel(
    norm, sizes, cl, got, tct, tst, masked, d_joined, w_in, grad_freq, d_unit, late, got_x, got_s, z, acc_g
):
    y = pl.program_id(0)

    back = line_back(y, norm, sizes, got, tct, tst, z, got_x, got_s)
    x = masked[0, :, cl:]
    slope = slope_and_silu(dot(x, w_in[...]))[0]
    du = ((d_joined[0].astype(F32) + back.astype(F32)) * slope).astype(BF)
    g = dot(du, x, ROWS_OF)

    @pl.when(y == 0)
    def _():
        acc_g[...] = g

    @pl.when(y > 0)
    def _():
        acc_g[...] += g

    d_unit[0] = du

    @pl.when(y == pl.num_programs(0) - 1)
    def _():
        at = 0
        for part, size in ((grad_freq, 384), (acc_g, 192)):
            for k in range(3):
                late[at : at + size, :] = part[0:size, k * 128 : (k + 1) * 128].astype(BF)
                at += size
        late[at:, :] = jnp.zeros((late.shape[0] - at, 128), BF)


def finish_kernel(cl, marked, d_unit, d_conv, w_in_t, grad_features):
    keep = kept(marked[0])[1]
    total = jnp.concatenate([d_conv[0, :, :cl], d_conv[0, :, cl:] + dot(d_unit[0], w_in_t[...])], 1)
    grad_features[0] = jnp.where(keep, total, 0.0).astype(BF)


def shifted(x, step):
    n = x.shape[0]
    at = lax.broadcasted_iota(jnp.int32, x.shape, 0)
    if step == 1:
        return jnp.where(at == 0, 0.0, pltpu.roll(x, 1, 0))
    return jnp.where(at == n - 1, 0.0, pltpu.roll(x, n - 1, 0))


def three(x):
    f = x.astype(F32)
    return jnp.concatenate([shifted(f, -1).astype(BF), x, shifted(f, 1).astype(BF)], 1)


def conv_kernel(cl, above, masked, below, w_local, w_cross, pre, pad):
    y = pl.program_id(0)
    rows = masked.shape[0]

    @pl.when(y == 0)
    def _():
        pad[0] = above[0]
        pad[1 : rows + 1] = masked[...]
        pad[rows + 1] = below[0]

    local = dot(pad[y], w_local[0]) + dot(pad[y + 1], w_local[1]) + dot(pad[y + 2], w_local[2])
    near = jnp.concatenate([pad[y, :, :cl], pad[y + 1, :, :cl], pad[y + 2, :, :cl]], 1)
    cross = dot(near, w_cross[...])
    c, g = cl, w_cross.shape[1] // 3
    pre[0, :, :cl] = shifted(local[:, :c], 1) + local[:, c : 2 * c] + shifted(local[:, 2 * c :], -1)
    pre[0, :, cl:] = shifted(cross[:, :g], 1) + cross[:, g : 2 * g] + shifted(cross[:, 2 * g :], -1)


def conv_grad_kernel(cl, above, masked, below, d_out, g_out, early, pad, acc_l, acc_c):
    y = pl.program_id(0)
    rows = masked.shape[0]

    @pl.when(y == 0)
    def _():
        pad[0] = above[0]
        pad[1 : rows + 1] = masked[...]
        pad[rows + 1] = below[0]
        acc_l[...] = jnp.zeros_like(acc_l)
        acc_c[...] = jnp.zeros_like(acc_c)

    d_local = three(d_out[0, :, :cl])
    d_global = three(d_out[0, :, cl:])
    g = d_global.shape[1] // 3
    for i in range(3):
        x = pad[y + i]
        acc_l[i] += dot(x, d_local, ROWS_OF)
        acc_c[i] += dot(x[:, :cl], d_global, ROWS_OF)

    @pl.when(y == pl.num_programs(0) - 1)
    def _():
        ch = masked.shape[2]
        for i in range(3):
            early[0, i * ch : (i + 1) * ch, :] = acc_l[i].astype(BF)
            for j in range(3):
                at = (3 * i + j) * cl
                early[1, at : at + cl, :] = acc_c[i, :, j * g : (j + 1) * g].astype(BF)
        at, size = 9 * cl, g_out.shape[0]
        early[1, at : at + size, :] = g_out[...]
        early[1, at + size :, :] = jnp.zeros((early.shape[1] - at - size, g), BF)


def unpack_kernel(cl, mine, other, core, g_local, g_cross, g_out):
    ch = g_local.shape[2]

    def write(local, rest):
        for at in range(0, 3 * ch, 64):
            block = local[at : at + 64, :].astype(F32)
            for j in range(3):
                g_local[at // ch, j, at % ch : at % ch + 64, :] = block[:, j * cl : (j + 1) * cl]
        g_cross[...] = rest[0 : 9 * cl, :].astype(F32)
        g_out[...] = rest[9 * cl : 9 * cl + g_out.shape[0], :].astype(F32)

    @pl.when(core[0, 0] == 0)
    def _():
        write(mine, other)

    @pl.when(core[0, 0] == 1)
    def _():
        write(other, mine)


def conv_back_kernel(cl, above, d_out, below, w_local, w_cross, d_conv, pad_l, pad_g):
    y = pl.program_id(0)
    rows = d_out.shape[0]

    @pl.when(y == 0)
    def _():
        for k in range(rows + 2):
            line = above[0] if k == 0 else below[0] if k == rows + 1 else d_out[k - 1]
            pad_l[k] = three(line[:, :cl])
            pad_g[k] = three(line[:, cl:])

    total = dot(pad_l[y + 2], w_local[0]) + dot(pad_l[y + 1], w_local[1]) + dot(pad_l[y], w_local[2])
    cross = dot(pad_g[y + 2], w_cross[0]) + dot(pad_g[y + 1], w_cross[1]) + dot(pad_g[y], w_cross[2])
    d_conv[0, :, :cl] = total[:, :cl] + cross
    d_conv[0, :, cl:] = total[:, cl:]


def swap(x, count):
    return lax.all_to_all(x.reshape(count, -1, x.shape[-1]), AXES, 0, 0, tiled=True).reshape(x.shape)


def to_rows(field, cols):
    h, w, c = field.shape
    return lax.all_to_all(field.reshape(cols, h // cols, w, c), "col", 0, 0, tiled=True)


def turn(field, cols):
    h, w, c = field.shape
    blocks = field.reshape(cols, h // cols, w, c)
    me = lax.axis_index("col")
    out = []
    for k in range(cols):
        part = lax.dynamic_index_in_dim(blocks, (me + k) % cols, 0, keepdims=False)
        out.append(lax.ppermute(part, "col", [(i, (i + k) % cols) for i in range(cols)]) if k else part)
    return out


def core_sum(early):
    pairs = lax.axis_size("row")
    core = lax.axis_index("row") % 2
    mine = lax.dynamic_index_in_dim(early, core, 0, keepdims=False)
    other = lax.dynamic_index_in_dim(early, 1 - core, 0, keepdims=False)
    other = lax.ppermute(other, "row", [(i, i ^ 1) for i in range(pairs)])
    return (mine.astype(F32) + other.astype(F32)).astype(BF)


def core_exchange(x, count):
    pairs = lax.axis_size("row")
    cols = count // pairs
    groups = [[cols * r + c for r in range(k, pairs, 2) for c in range(cols)] for k in range(2)]
    x = x.reshape(count // 2, -1, x.shape[-1])
    return lax.all_to_all(x, AXES, 0, 0, axis_index_groups=groups, tiled=True)


def edges(field, count):
    down = lax.ppermute(field[-1:], AXES, [(i, i + 1) for i in range(count - 1)])
    up = lax.ppermute(field[:1], AXES, [(i + 1, i) for i in range(count - 1)])
    return down, up


def scatter_sum(x, count):
    x = lax.all_to_all(x.reshape(count, -1, x.shape[-1]), AXES, 0, 0, tiled=True)
    return x.astype(F32).sum(0).astype(BF)


def gather(x, count):
    x = lax.all_to_all(jnp.broadcast_to(x[None], (count,) + x.shape), AXES, 0, 0, tiled=True)
    return x.reshape(-1, x.shape[-1])


def tie(value, *after):
    return lax.optimization_barrier((value,) + after)[0]


def tied(*values):
    return lax.optimization_barrier(values)


def shards(features, hole_mask, cotangent, w_local, w_cross, w_in, w_freq, w_out):
    cols = lax.axis_size("col")
    count = lax.axis_size("row") * cols
    me = lax.axis_index(AXES)
    _, h, w, ch = features.shape
    rows, width = h // cols, w * cols
    height = rows * count
    cl, cg, cs = w_local.shape[3], w_cross.shape[3], w_in.shape[1]
    lines = -(-(width // 2 + 1) // count)
    slots = -(-(rows * lines) // 16) * 16
    n = count * slots
    sizes = (rows, lines, count, slots)
    tc, ts = line_tables(width, count, lines)
    tct, tst = jnp.asarray(tc.T), jnp.asarray(ts.T)
    tc, ts = jnp.asarray(tc), jnp.asarray(ts)
    hc, hs = (jnp.asarray(t) for t in column_tables(rows, count))
    norm_w, norm_h = 1.0 / math.sqrt(width), 1.0 / math.sqrt(height)
    freq = lines * me + jnp.arange(lines)
    weight = jnp.where((freq == 0) | (freq * 2 == width), 0.5, jnp.where(freq * 2 < width, 1.0, 0.0))
    weight = weight.astype(F32)[None]
    sign = np.where((np.arange(384) < 192), 1.0, -1.0).astype(np.float32)
    sign = jnp.asarray(sign[None])

    w_in_d = jnp.concatenate([w_in, w_in[:, 128:]], 1)
    w_in_t = jnp.pad(w_in.T, ((0, 64), (0, 0)))
    w_out_z = jnp.pad(w_out, ((0, 64), (0, 0)))
    w_out_t = jnp.concatenate([w_out, w_out[128:]], 0).T
    w_freq_p = pack_dim(pack_dim(w_freq, 0, cs), 1, cs)
    w_freq_t = w_freq_p.T
    wl = jnp.transpose(w_local, (0, 2, 1, 3)).reshape(3, ch, 3 * cl)
    wc = jnp.transpose(w_cross, (0, 2, 1, 3)).reshape(3 * cl, 3 * cg)
    wl_t = jnp.transpose(w_local, (0, 1, 3, 2)).reshape(3, 3 * cl, ch)
    wc_t = jnp.transpose(w_cross, (0, 1, 3, 2)).reshape(3, 3 * cg, cl)

    at_y = lambda y: (y, 0, 0)
    one_row = lambda c: (1, width, c)
    blocks = lambda c: (cols, 1, w, c)
    at_blocks = lambda y: (0, y, 0, 0)
    wide = (rows, width, ch)
    pix = rows * width
    vm = pltpu.VMEM
    lined = (rows, lines * count, 384)
    spectral = (lines, height, 384)
    used = rows * lines * count

    marked = jnp.where(hole_mask[0][..., None] == 1, HOLE, features[0]).astype(BF)
    (unit,) = call(
        functools.partial(unit_kernel, cl),
        "unit",
        (cols,),
        [(marked.reshape(cols, rows, w, ch), (1, rows, w, ch), lambda k: (k, 0, 0, 0)), (w_in_d, None, None)],
        [((cols, rows, w, 256), BF, (1, rows, w, 256), lambda k: (k, 0, 0, 0))],
        flops=2 * pix * cg * 256, bytes_=3 << 20,
    )
    unit = lax.all_to_all(unit, "col", 0, 0, tiled=True)
    unit, w_in_t, w_out_z, w_out_t, w_freq_p, w_freq_t, wl, wc, wl_t, wc_t, weight, marked = tied(
        unit, w_in_t, w_out_z, w_out_t, w_freq_p, w_freq_t, wl, wc, wl_t, wc_t, weight, marked
    )
    my_col = lax.axis_index("col").astype(jnp.int32).reshape(1, 1)
    (sent,) = call(
        functools.partial(front_kernel, norm_w, sizes),
        "front",
        (rows,),
        [(unit, blocks(256), at_blocks), (tc, None, None), (ts, None, None)],
        [((n, 384), BF, None, None)],
        [vm(lined, F32), vm((3, n, 128), F32)],
        flops=1 << 30, bytes_=3 << 20,
    )
    parts = turn(marked, cols)
    got = swap(sent, count)
    got, cot = tied(got, cotangent[0])
    cots = turn(cot, cols)
    stacked, sent = call(
        functools.partial(frequency_kernel, norm_h, sizes),
        "frequency",
        (1,),
        [(got, None, None), (hc, None, None), (hs, None, None), (w_freq_p, None, None), (weight, None, None), (sign, None, None)],
        [(spectral, BF, None, None), ((n, 384), BF, None, None)],
        [vm((3, n, 128), F32), vm(spectral, F32)],
        flops=3 << 30, bytes_=7 << 20,
    )
    sent, *parts = tied(sent, *parts)
    masked, marks = call(
        functools.partial(rows_kernel, cols),
        "rows",
        (rows,),
        [(my_col, None, None)] + [(p, (1, w, ch), at_y) for p in parts],
        [(wide, BF, one_row(ch), at_y), ((rows, width, 128), BF, one_row(128), at_y)],
        [vm((width, ch), BF)],
        flops=1, bytes_=4 << 20,
    )
    above, below = edges(masked, count)
    got = swap(sent, count)
    (pre,) = call(
        functools.partial(conv_kernel, cl),
        "conv",
        (rows,),
        [(above, None, None), (masked, None, None), (below, None, None), (wl, None, None), (wc, None, None)],
        [(wide, F32, one_row(ch), at_y)],
        [vm((rows + 2, width, ch), BF)],
        flops=18 * pix * (ch * cl + cl * cg), bytes_=9 << 20,
    )
    output, d_out, d_joined, sent, grad_out = call(
        functools.partial(middle_kernel, norm_w, sizes, cl, cols),
        "middle",
        (rows,),
        [
            (got, None, None), (tct, None, None), (tst, None, None), (tc, None, None),
            (ts, None, None), (unit, blocks(256), at_blocks), (pre, one_row(ch), at_y),
            (w_out_z, None, None), (w_out_t, None, None), (my_col, None, None),
        ]
        + [(c, (1, w, ch), at_y) for c in cots],
        [
            (wide, BF, one_row(ch), at_y), (wide, BF, one_row(ch), at_y), ((rows, width, 256), BF, one_row(256), at_y),
            ((n, 384), BF, None, None), ((cs, cg), BF, None, None),
        ],
        [vm((used, 384), BF), vm((used, 256), BF), vm((width, ch), BF), vm(lined, F32), vm((3, n, 128), F32), vm((256, cg), F32)],
        flops=3 << 30, bytes_=12 << 20,
    )
    got = swap(sent, count)
    d_above, d_below = edges(d_out, count)
    (early,) = call(
        functools.partial(conv_grad_kernel, cl),
        "conv_grad",
        (rows,),
        [(above, None, None), (masked, None, None), (below, None, None), (d_out, one_row(ch), at_y), (grad_out, None, None)],
        [((2, 3 * ch, 384), BF, None, None)],
        [vm((rows + 2, width, ch), BF), vm((3, ch, 3 * cl), F32), vm((3, cl, 3 * cg), F32)],
        flops=18 * pix * (ch * cl + cl * cg), bytes_=7 << 20,
    )
    got, early, d_above, d_below = tied(got, early, d_above, d_below)
    got, total = tied(got, core_sum(early))
    early = core_exchange(total, count)
    sent, grad_freq = call(
        functools.partial(frequency_back_kernel, norm_h, sizes),
        "frequency_back",
        (1,),
        [
            (got, None, None), (hc, None, None), (hs, None, None), (w_freq_p, None, None), (w_freq_t, None, None),
            (weight, None, None), (sign, None, None), (stacked, None, None),
        ],
        [((n, 384), BF, None, None), ((384, 384), BF, None, None)],
        [vm((3, n, 128), F32), vm(spectral, F32), vm((256, 384), F32), vm((256, 384), F32)],
        flops=3 << 30, bytes_=8 << 20,
    )
    sent, early = tied(sent, early)
    got = swap(sent, count)
    (d_conv,) = call(
        functools.partial(conv_back_kernel, cl),
        "conv_back",
        (rows,),
        [(d_above, None, None), (d_out, None, None), (d_below, None, None), (wl_t, None, None), (wc_t, None, None)],
        [(wide, F32, one_row(ch), at_y)],
        [vm((rows + 2, width, 3 * cl), BF), vm((rows + 2, width, 3 * cg), BF)],
        flops=18 * pix * (ch * cl + cl * cg), bytes_=9 << 20,
    )
    got, d_conv, early = tied(got, d_conv, early)
    early = early.astype(F32).sum(0).astype(BF)
    early = core_exchange(jnp.tile(early, (count // 2, 1)), count).reshape(-1, 384)
    late_rows = -(-(3 * 384 + 3 * cs) // (16 * count)) * 16 * count
    d_unit, late = call(
        functools.partial(tail_kernel, norm_w, sizes, cl),
        "tail",
        (rows,),
        [
            (got, None, None), (tct, None, None), (tst, None, None), (masked, one_row(ch), at_y),
            (d_joined, one_row(256), at_y), (w_in_d, None, None), (grad_freq, None, None),
        ],
        [((rows, width, 256), BF, one_row(256), at_y), ((late_rows, 128), BF, None, None)],
        [vm((used, 384), BF), vm((used, 256), BF), vm((3, n, 128), F32), vm((256, cg), F32)],
        flops=1 << 30, bytes_=5 << 20,
    )
    late, early = tied(late, early)
    pairs = lax.axis_size("row")
    other = lax.ppermute(early, "row", [(i, i ^ 1) for i in range(pairs)])
    my_core = (lax.axis_index("row") % 2).astype(jnp.int32).reshape(1, 1)
    late = scatter_sum(late, count)
    (grad_features,) = call(
        functools.partial(finish_kernel, cl),
        "finish",
        (rows,),
        [
            (marks, one_row(128), at_y), (d_unit, one_row(256), at_y), (d_conv, one_row(ch), at_y),
            (w_in_t, None, None),
        ],
        [(wide, BF, one_row(ch), at_y)],
        flops=2 * pix * 256 * cg, bytes_=7 << 20,
    )
    late, grad_features = tied(late, grad_features)
    grad_local, grad_cross, grad_out = call(
        functools.partial(unpack_kernel, cl),
        "unpack",
        (1,),
        [(early, None, None), (other, None, None), (my_core, None, None)],
        [((3, 3, ch, cl), F32, None, None), ((9 * cl, cg), F32, None, None), ((cs, cg), F32, None, None)],
        flops=1, bytes_=7 << 20,
    )
    late = gather(late, count)
    late, grad_local, grad_cross, grad_out = tied(late, grad_local, grad_cross, grad_out)
    grad_freq = jnp.concatenate([late[k * 384 : (k + 1) * 384] for k in range(3)], 1).astype(F32)
    at = 3 * 384
    grad_in = jnp.concatenate([late[at + k * cs : at + (k + 1) * cs] for k in range(3)], 1).astype(F32).T
    grad_cross = grad_cross.reshape(3, 3, cl, cg)
    return output[None], grad_features[None], grad_local, grad_cross, grad_in, grad_freq, grad_out


def solution(mesh):
    return jax.shard_map(
        shards,
        mesh=mesh,
        in_specs=(
            P("dp", "row", "col", None),
            P("dp", "row", "col"),
            P("dp", "row", "col", None),
            P(),
            P(),
            P(),
            P(),
            P(),
        ),
        out_specs=(
            P("dp", ("row", "col"), None, None),
            P("dp", ("row", "col"), None, None),
            P("dp", None, None, None),
            P("dp", None, None, None),
            P("dp", None),
            P("dp", None),
            P("dp", None),
        ),
        check_vma=False,
    )
```

```python
import functools
import math

import jax
import jax.numpy as jnp
import numpy as np
from jax import lax
from jax.experimental import pallas as pl
from jax.experimental.pallas import tpu as pltpu
from jax.sharding import PartitionSpec as P

AXES = ("row", "col")
HOLE = 64.0
BF = jnp.bfloat16
F32 = jnp.float32
ROWS_OF = ((0,), (0,))


def dot(a, b, dims=((1,), (0,))):
    return lax.dot_general(a, b, (dims, ((), ())), preferred_element_type=F32)


def line_tables(width, count, lines):
    freq = (lines * np.arange(count)[None] + np.arange(lines)[:, None]).reshape(-1, 1)
    angle = 2.0 * np.pi * (freq * np.arange(width) % width) / width
    valid = freq <= width // 2
    return (np.cos(angle) * valid).astype(BF), (np.sin(angle) * valid).astype(BF)


def column_tables(rows, count):
    h = (rows * np.arange(count)[None] + np.arange(rows)[:, None]).reshape(-1)
    angle = 2.0 * np.pi * (h[:, None] * h[None] % (rows * count)) / (rows * count)
    return np.cos(angle).astype(BF), np.sin(angle).astype(BF)


def slope_and_silu(value):
    sigma = 1.0 / (1.0 + jnp.exp(-value))
    return sigma * (1.0 + value * (1.0 - sigma)), value * sigma


def lanes_below(shape, bound):
    return lax.broadcasted_iota(jnp.int32, shape, 1) < bound


def packed(re, im):
    mid = jnp.where(lanes_below(re[:, 128:].shape, 64), re[:, 128:], im[:, 128:])
    return jnp.concatenate([re[:, :128], mid, im[:, :128]], 1)


def turned(p, q, sign):
    mid = pltpu.roll(q[:, 128:256], 64, 1)
    flip = jnp.where(lanes_below(mid.shape, 64), sign, -sign)
    return jnp.concatenate(
        [p[:, :128] + sign * q[:, 256:], p[:, 128:256] + flip * mid, p[:, 256:] - sign * q[:, :128]], 1
    )


def natural_lanes(x):
    mid, im = x[:, 128:256], pltpu.roll(x[:, 256:], 64, 1)
    low = lanes_below(mid.shape, 64)
    return jnp.concatenate([x[:, :128], jnp.where(low, mid, im), jnp.where(low, im, mid)], 1)


def pack_order(cs):
    return [(0, 128), (128, cs), (cs + 128, 2 * cs), (cs, cs + 128)]


def pack_dim(x, dim, cs):
    return jnp.concatenate([lax.slice_in_dim(x, a, b, axis=dim) for a, b in pack_order(cs)], dim)


def call(body, name, grid, ins, outs, scratch=(), flops=0, bytes_=0):
    def spec(shape, block, index):
        if shape[0] == 1 and shape[-1] < 8:
            return pl.BlockSpec(memory_space=pltpu.SMEM)
        if block is None:
            zeros = (0,) * len(shape)
            return pl.BlockSpec(shape, lambda *_: zeros)
        return pl.BlockSpec(block, index)

    return pl.pallas_call(
        body,
        grid=grid,
        in_specs=[spec(a.shape, block, index) for a, block, index in ins],
        out_specs=[spec(shape, block, index) for shape, _, block, index in outs],
        out_shape=[jax.ShapeDtypeStruct(shape, dtype) for shape, dtype, _, _ in outs],
        scratch_shapes=list(scratch),
        compiler_params=pltpu.CompilerParams(vmem_limit_bytes=56 << 20),
        cost_estimate=pl.CostEstimate(flops=flops, bytes_accessed=bytes_, transcendentals=0),
        name=name,
    )(*[a for a, _, _ in ins])


def put_slots(sizes, z, value_of, sent):
    rows, lines, count, slots = sizes
    for q in range(slots):
        value = value_of(q // lines, q % lines) if q < rows * lines else jnp.zeros((count, 384), F32)
        for k in range(3):
            z[k, pl.ds(q, count, stride=slots), :] = value[:, k * 128 : (k + 1) * 128]
    for k in range(3):
        sent[:, k * 128 : (k + 1) * 128] = z[k].astype(BF)


def spread(got, z):
    for k in range(3):
        z[k] = got[:, k * 128 : (k + 1) * 128].astype(F32)


def slot(sizes, z, q):
    _, _, count, slots = sizes
    return jnp.concatenate([z[k, pl.ds(q, count, stride=slots), :] for k in range(3)], 1)


def take_slots(sizes, got, z, x):
    rows, lines, count, slots = sizes
    spread(got, z)
    for q in range(rows * lines):
        x[q * count : (q + 1) * count, :] = slot(sizes, z, q).astype(BF)


def head_kernel(norm, sizes, cl, marked, w_in, tc, ts, masked, unit, sent, v, z):
    y = pl.program_id(0)
    x = marked[...].reshape(-1, marked.shape[-1])
    keep = x[:, :1].astype(F32) < 0.5 * HOLE
    x = jnp.where(keep, x, jnp.zeros_like(x))
    masked[0] = x
    u = slope_and_silu(dot(x[:, cl:], w_in[...]))[1].astype(BF)
    unit[0] = u
    transform_out(y, norm, sizes, u, tc, ts, sent, v, z)


def transform_out(y, norm, sizes, u, tc, ts, sent, v, z):
    count = sizes[2]
    v[y] = packed(dot(tc[...], u) * norm, dot(ts[...], u) * -norm)

    @pl.when(y == pl.num_programs(0) - 1)
    def _():
        put_slots(sizes, z, lambda row, j: v[row, j * count : (j + 1) * count, :], sent)


def column_line(sizes, z, j):
    rows, lines, count, slots = sizes
    parts = [slot(sizes, z, row * lines + j) for row in range(rows)]
    return jnp.concatenate(parts, 0).astype(BF)


def frequency_kernel(norm, sizes, got, hc, hs, w_freq, weight, sign, stacked, sent, z, v):
    count = sizes[2]
    spread(got, z)
    for j in range(sizes[1]):
        x = column_line(sizes, z, j)
        st = (turned(dot(hc[...], x), dot(hs[...], x), 1.0) * norm).astype(BF)
        stacked[j] = st
        pos = slope_and_silu(dot(st, w_freq[...]))[1]
        neg = slope_and_silu(dot((st.astype(F32) * sign[...]).astype(BF), w_freq[...]))[1]
        x = (weight[0, j] * (pos + sign[...] * neg)).astype(BF)
        v[j] = turned(dot(hc[...], x), dot(hs[...], x), -1.0) * norm
    put_slots(sizes, z, lambda row, j: v[j, row * count : (row + 1) * count, :], sent)


def frequency_back_kernel(
    norm, sizes, got, hc, hs, w_freq, w_freq_t, weight, sign, stacked, sent, grad, z, v, acc_p, acc_m
):
    count = sizes[2]
    spread(got, z)
    for j in range(sizes[1]):
        x = column_line(sizes, z, j)
        dz = turned(dot(hc[...], x), dot(hs[...], x), 1.0) * norm
        st = stacked[j]
        pos = slope_and_silu(dot(st, w_freq[...]))[0]
        neg = slope_and_silu(dot((st.astype(F32) * sign[...]).astype(BF), w_freq[...]))[0]
        pos = (dz * pos).astype(BF).astype(F32)
        neg = (dz * sign[...] * neg).astype(BF).astype(F32)
        total = (weight[0, j] * (pos + neg)).astype(BF)
        delta = (weight[0, j] * (pos - neg)).astype(BF)
        g_p = dot(st[:, :256], total, ROWS_OF)
        g_m = dot(st[:, 128:], delta, ROWS_OF)
        acc_p[...] = g_p if j == 0 else acc_p[...] + g_p
        acc_m[...] = g_m if j == 0 else acc_m[...] + g_m
        re = dot(total, w_freq_t[:, :256])
        im = dot(delta, w_freq_t[:, 128:])
        mid = jnp.where(lanes_below((re.shape[0], 128), 64), re[:, 128:], im[:, :128])
        x = jnp.concatenate([re[:, :128], mid, im[:, 128:]], 1).astype(BF)
        v[j] = turned(dot(hc[...], x), dot(hs[...], x), -1.0) * norm
    put_slots(sizes, z, lambda row, j: v[j, row * count : (row + 1) * count, :], sent)
    grad[0:192, :] = natural_lanes(acc_p[0:192, :]).astype(BF)
    grad[192:320, :] = natural_lanes(acc_m[128:256, :]).astype(BF)
    grad[320:384, :] = natural_lanes(acc_m[64:128, :]).astype(BF)


def imag_first(got):
    mid = pltpu.roll(got[:, 128:256].astype(F32), 64, 1).astype(BF)
    return jnp.concatenate([got[:, 256:], mid], 1)


def line_back(y, norm, sizes, got, tct, tst, z, got_x, got_s):
    @pl.when(y == 0)
    def _():
        take_slots(sizes, got, z, got_x)
        got_s[...] = imag_first(got_x[...])

    size = sizes[1] * sizes[2]
    at = pl.ds(pl.multiple_of(y * size, size), size)
    return ((dot(tct[...], got_x[at, :256]) - dot(tst[...], got_s[at, :])) * norm).astype(BF)


def middle_kernel(
    norm, sizes, cl, cols, got, tct, tst, tc, ts, unit, pre, w_out, w_out_t, my_col, *refs,
):
    cots = refs[:cols]
    output, d_out, d_joined, sent, grad, got_x, got_s, cot, v, z, acc_g = refs[cols:]
    y = pl.program_id(0)
    w = cots[0].shape[1]
    for k in range(cols):
        at = lax.rem(my_col[0, 0] + (cols - k), cols)
        cot[pl.ds(pl.multiple_of(at * w, w), w), :] = cots[k][0]

    back = line_back(y, norm, sizes, got, tct, tst, z, got_x, got_s)
    joined = (unit[0].astype(F32) + back.astype(F32)).astype(BF)
    pre_all = jnp.concatenate([pre[0, :, :cl], pre[0, :, cl:] + dot(joined, w_out[...])], 1)
    slope, silu = slope_and_silu(pre_all)
    output[0] = silu.astype(BF)
    d = (cot[...].astype(F32) * slope).astype(BF)
    d_out[0] = d
    dj = dot(d[:, cl:], w_out_t[...]).astype(BF)
    d_joined[0] = dj
    g = dot(joined, d[:, cl:], ROWS_OF)

    @pl.when(y == 0)
    def _():
        acc_g[...] = g

    @pl.when(y > 0)
    def _():
        acc_g[...] += g

    transform_out(y, norm, sizes, dj, tc, ts, sent, v, z)

    @pl.when(y == pl.num_programs(0) - 1)
    def _():
        grad[...] = acc_g[0 : grad.shape[0], :].astype(BF)


def tail_kernel(
    norm, sizes, cl, got, tct, tst, masked, d_joined, w_in, grad_freq, d_unit, late, got_x, got_s, z, acc_g
):
    y = pl.program_id(0)

    back = line_back(y, norm, sizes, got, tct, tst, z, got_x, got_s)
    x = masked[0, :, cl:]
    slope = slope_and_silu(dot(x, w_in[...]))[0]
    du = ((d_joined[0].astype(F32) + back.astype(F32)) * slope).astype(BF)
    g = dot(du, x, ROWS_OF)

    @pl.when(y == 0)
    def _():
        acc_g[...] = g

    @pl.when(y > 0)
    def _():
        acc_g[...] += g

    d_unit[0] = du

    @pl.when(y == pl.num_programs(0) - 1)
    def _():
        at = 0
        for part, size in ((grad_freq, 384), (acc_g, 192)):
            for k in range(3):
                late[at : at + size, :] = part[0:size, k * 128 : (k + 1) * 128].astype(BF)
                at += size
        late[at:, :] = jnp.zeros((late.shape[0] - at, 128), BF)


def finish_kernel(cl, marked, d_unit, d_conv, w_in_t, grad_features):
    keep = marked[...].reshape(-1, marked.shape[-1])[:, :1].astype(F32) < 0.5 * HOLE
    total = jnp.concatenate([d_conv[0, :, :cl], d_conv[0, :, cl:] + dot(d_unit[0], w_in_t[...])], 1)
    grad_features[0] = jnp.where(keep, total, 0.0).astype(BF)


def shifted(x, step):
    n = x.shape[0]
    at = lax.broadcasted_iota(jnp.int32, x.shape, 0)
    if step == 1:
        return jnp.where(at == 0, 0.0, pltpu.roll(x, 1, 0))
    return jnp.where(at == n - 1, 0.0, pltpu.roll(x, n - 1, 0))


def three(x):
    f = x.astype(F32)
    return jnp.concatenate([shifted(f, -1).astype(BF), x, shifted(f, 1).astype(BF)], 1)


def conv_kernel(cl, above, masked, below, w_local, w_cross, pre, pad):
    y = pl.program_id(0)
    rows = masked.shape[0]

    @pl.when(y == 0)
    def _():
        pad[0] = above[0]
        pad[1 : rows + 1] = masked[...]
        pad[rows + 1] = below[0]

    local = dot(pad[y], w_local[0]) + dot(pad[y + 1], w_local[1]) + dot(pad[y + 2], w_local[2])
    near = jnp.concatenate([pad[y, :, :cl], pad[y + 1, :, :cl], pad[y + 2, :, :cl]], 1)
    cross = dot(near, w_cross[...])
    c, g = cl, w_cross.shape[1] // 3
    pre[0, :, :cl] = shifted(local[:, :c], 1) + local[:, c : 2 * c] + shifted(local[:, 2 * c :], -1)
    pre[0, :, cl:] = shifted(cross[:, :g], 1) + cross[:, g : 2 * g] + shifted(cross[:, 2 * g :], -1)


def conv_grad_kernel(cl, above, masked, below, d_out, g_out, early, pad, acc_l, acc_c):
    y = pl.program_id(0)
    rows = masked.shape[0]

    @pl.when(y == 0)
    def _():
        pad[0] = above[0]
        pad[1 : rows + 1] = masked[...]
        pad[rows + 1] = below[0]
        acc_l[...] = jnp.zeros_like(acc_l)
        acc_c[...] = jnp.zeros_like(acc_c)

    d_local = three(d_out[0, :, :cl])
    d_global = three(d_out[0, :, cl:])
    g = d_global.shape[1] // 3
    for i in range(3):
        x = pad[y + i]
        acc_l[i] += dot(x, d_local, ROWS_OF)
        acc_c[i] += dot(x[:, :cl], d_global, ROWS_OF)

    @pl.when(y == pl.num_programs(0) - 1)
    def _():
        ch = masked.shape[2]
        for i in range(3):
            early[0, i * ch : (i + 1) * ch, :] = acc_l[i].astype(BF)
            for j in range(3):
                at = (3 * i + j) * cl
                early[1, at : at + cl, :] = acc_c[i, :, j * g : (j + 1) * g].astype(BF)
        at, size = 9 * cl, g_out.shape[0]
        early[1, at : at + size, :] = g_out[...]
        early[1, at + size :, :] = jnp.zeros((early.shape[1] - at - size, g), BF)


def unpack_kernel(cl, mine, other, core, g_local, g_cross, g_out):
    ch = g_local.shape[2]

    def write(local, rest):
        for at in range(0, 3 * ch, 64):
            block = local[at : at + 64, :].astype(F32)
            for j in range(3):
                g_local[at // ch, j, at % ch : at % ch + 64, :] = block[:, j * cl : (j + 1) * cl]
        g_cross[...] = rest[0 : 9 * cl, :].astype(F32)
        g_out[...] = rest[9 * cl : 9 * cl + g_out.shape[0], :].astype(F32)

    @pl.when(core[0, 0] == 0)
    def _():
        write(mine, other)

    @pl.when(core[0, 0] == 1)
    def _():
        write(other, mine)


def conv_back_kernel(cl, above, d_out, below, w_local, w_cross, d_conv, pad_l, pad_g):
    y = pl.program_id(0)
    rows = d_out.shape[0]

    @pl.when(y == 0)
    def _():
        for k in range(rows + 2):
            line = above[0] if k == 0 else below[0] if k == rows + 1 else d_out[k - 1]
            pad_l[k] = three(line[:, :cl])
            pad_g[k] = three(line[:, cl:])

    total = dot(pad_l[y + 2], w_local[0]) + dot(pad_l[y + 1], w_local[1]) + dot(pad_l[y], w_local[2])
    cross = dot(pad_g[y + 2], w_cross[0]) + dot(pad_g[y + 1], w_cross[1]) + dot(pad_g[y], w_cross[2])
    d_conv[0, :, :cl] = total[:, :cl] + cross
    d_conv[0, :, cl:] = total[:, cl:]


def swap(x, count):
    return lax.all_to_all(x.reshape(count, -1, x.shape[-1]), AXES, 0, 0, tiled=True).reshape(x.shape)


def to_rows(field, cols):
    h, w, c = field.shape
    return lax.all_to_all(field.reshape(cols, h // cols, w, c), "col", 0, 0, tiled=True)


def turn(field, cols):
    h, w, c = field.shape
    blocks = field.reshape(cols, h // cols, w, c)
    me = lax.axis_index("col")
    out = []
    for k in range(cols):
        part = lax.dynamic_index_in_dim(blocks, (me + k) % cols, 0, keepdims=False)
        out.append(lax.ppermute(part, "col", [(i, (i + k) % cols) for i in range(cols)]) if k else part)
    return out


def core_sum(early):
    pairs = lax.axis_size("row")
    core = lax.axis_index("row") % 2
    mine = lax.dynamic_index_in_dim(early, core, 0, keepdims=False)
    other = lax.dynamic_index_in_dim(early, 1 - core, 0, keepdims=False)
    other = lax.ppermute(other, "row", [(i, i ^ 1) for i in range(pairs)])
    return (mine.astype(F32) + other.astype(F32)).astype(BF)


def core_exchange(x, count):
    pairs = lax.axis_size("row")
    cols = count // pairs
    groups = [[cols * r + c for r in range(k, pairs, 2) for c in range(cols)] for k in range(2)]
    x = x.reshape(count // 2, -1, x.shape[-1])
    return lax.all_to_all(x, AXES, 0, 0, axis_index_groups=groups, tiled=True)


def edges(field, count):
    down = lax.ppermute(field[-1:], AXES, [(i, i + 1) for i in range(count - 1)])
    up = lax.ppermute(field[:1], AXES, [(i + 1, i) for i in range(count - 1)])
    return down, up


def scatter_sum(x, count):
    x = lax.all_to_all(x.reshape(count, -1, x.shape[-1]), AXES, 0, 0, tiled=True)
    return x.astype(F32).sum(0).astype(BF)


def gather(x, count):
    x = lax.all_to_all(jnp.broadcast_to(x[None], (count,) + x.shape), AXES, 0, 0, tiled=True)
    return x.reshape(-1, x.shape[-1])


def tie(value, *after):
    return lax.optimization_barrier((value,) + after)[0]


def tied(*values):
    return lax.optimization_barrier(values)


def shards(features, hole_mask, cotangent, w_local, w_cross, w_in, w_freq, w_out):
    cols = lax.axis_size("col")
    count = lax.axis_size("row") * cols
    me = lax.axis_index(AXES)
    _, h, w, ch = features.shape
    rows, width = h // cols, w * cols
    height = rows * count
    cl, cg, cs = w_local.shape[3], w_cross.shape[3], w_in.shape[1]
    lines = -(-(width // 2 + 1) // count)
    slots = -(-(rows * lines) // 16) * 16
    n = count * slots
    sizes = (rows, lines, count, slots)
    tc, ts = line_tables(width, count, lines)
    tct, tst = jnp.asarray(tc.T), jnp.asarray(ts.T)
    tc, ts = jnp.asarray(tc), jnp.asarray(ts)
    hc, hs = (jnp.asarray(t) for t in column_tables(rows, count))
    norm_w, norm_h = 1.0 / math.sqrt(width), 1.0 / math.sqrt(height)
    freq = lines * me + jnp.arange(lines)
    weight = jnp.where((freq == 0) | (freq * 2 == width), 0.5, jnp.where(freq * 2 < width, 1.0, 0.0))
    weight = weight.astype(F32)[None]
    sign = np.where((np.arange(384) < 192), 1.0, -1.0).astype(np.float32)
    sign = jnp.asarray(sign[None])

    w_in_d = jnp.concatenate([w_in, w_in[:, 128:]], 1)
    w_in_t = jnp.pad(w_in.T, ((0, 64), (0, 0)))
    w_out_z = jnp.pad(w_out, ((0, 64), (0, 0)))
    w_out_t = jnp.concatenate([w_out, w_out[128:]], 0).T
    w_freq_p = pack_dim(pack_dim(w_freq, 0, cs), 1, cs)
    w_freq_t = w_freq_p.T
    wl = jnp.transpose(w_local, (0, 2, 1, 3)).reshape(3, ch, 3 * cl)
    wc = jnp.transpose(w_cross, (0, 2, 1, 3)).reshape(3 * cl, 3 * cg)
    wl_t = jnp.transpose(w_local, (0, 1, 3, 2)).reshape(3, 3 * cl, ch)
    wc_t = jnp.transpose(w_cross, (0, 1, 3, 2)).reshape(3, 3 * cg, cl)

    at_y = lambda y: (y, 0, 0)
    one_row = lambda c: (1, width, c)
    blocks = lambda c: (cols, 1, w, c)
    at_blocks = lambda y: (0, y, 0, 0)
    wide = (rows, width, ch)
    pix = rows * width
    vm = pltpu.VMEM
    lined = (rows, lines * count, 384)
    spectral = (lines, height, 384)
    used = rows * lines * count

    marked = jnp.where(hole_mask[0][..., None] == 1, HOLE, features[0]).astype(BF)
    marked = to_rows(marked, cols)
    w_in_d, w_in_t, w_out_z, w_out_t, w_freq_p, w_freq_t, wl, wc, wl_t, wc_t, weight = tied(
        w_in_d, w_in_t, w_out_z, w_out_t, w_freq_p, w_freq_t, wl, wc, wl_t, wc_t, weight
    )
    cots = turn(tie(cotangent[0], marked), cols)
    my_col = lax.axis_index("col").astype(jnp.int32).reshape(1, 1)

    masked, unit, sent = call(
        functools.partial(head_kernel, norm_w, sizes, cl),
        "head",
        (rows,),
        [(marked, blocks(ch), at_blocks), (w_in_d, None, None), (tc, None, None), (ts, None, None)],
        [(wide, BF, one_row(ch), at_y), ((rows, width, 256), BF, one_row(256), at_y), ((n, 384), BF, None, None)],
        [vm(lined, F32), vm((3, n, 128), F32)],
        flops=1 << 30, bytes_=6 << 20,
    )
    near = [k for k in range(cols) if k in (0, 1, cols - 1)]
    sent, *moved = tied(sent, *[cots[k] for k in near])
    for k, c in zip(near, moved):
        cots[k] = c
    above, below = edges(masked, count)
    got = swap(sent, count)
    stacked, sent = call(
        functools.partial(frequency_kernel, norm_h, sizes),
        "frequency",
        (1,),
        [(got, None, None), (hc, None, None), (hs, None, None), (w_freq_p, None, None), (weight, None, None), (sign, None, None)],
        [(spectral, BF, None, None), ((n, 384), BF, None, None)],
        [vm((3, n, 128), F32), vm(spectral, F32)],
        flops=3 << 30, bytes_=7 << 20,
    )
    sent, above, below, *cots = tied(sent, above, below, *cots)
    got = swap(sent, count)
    (pre,) = call(
        functools.partial(conv_kernel, cl),
        "conv",
        (rows,),
        [(above, None, None), (masked, None, None), (below, None, None), (wl, None, None), (wc, None, None)],
        [(wide, F32, one_row(ch), at_y)],
        [vm((rows + 2, width, ch), BF)],
        flops=18 * pix * (ch * cl + cl * cg), bytes_=9 << 20,
    )
    output, d_out, d_joined, sent, grad_out = call(
        functools.partial(middle_kernel, norm_w, sizes, cl, cols),
        "middle",
        (rows,),
        [
            (got, None, None), (tct, None, None), (tst, None, None), (tc, None, None),
            (ts, None, None), (unit, one_row(256), at_y), (pre, one_row(ch), at_y),
            (w_out_z, None, None), (w_out_t, None, None), (my_col, None, None),
        ]
        + [(c, (1, w, ch), at_y) for c in cots],
        [
            (wide, BF, one_row(ch), at_y), (wide, BF, one_row(ch), at_y), ((rows, width, 256), BF, one_row(256), at_y),
            ((n, 384), BF, None, None), ((cs, cg), BF, None, None),
        ],
        [vm((used, 384), BF), vm((used, 256), BF), vm((width, ch), BF), vm(lined, F32), vm((3, n, 128), F32), vm((256, cg), F32)],
        flops=3 << 30, bytes_=12 << 20,
    )
    got = swap(sent, count)
    d_above, d_below = edges(d_out, count)
    (early,) = call(
        functools.partial(conv_grad_kernel, cl),
        "conv_grad",
        (rows,),
        [(above, None, None), (masked, None, None), (below, None, None), (d_out, one_row(ch), at_y), (grad_out, None, None)],
        [((2, 3 * ch, 384), BF, None, None)],
        [vm((rows + 2, width, ch), BF), vm((3, ch, 3 * cl), F32), vm((3, cl, 3 * cg), F32)],
        flops=18 * pix * (ch * cl + cl * cg), bytes_=7 << 20,
    )
    got, early = tied(got, early)
    got, total = tied(got, core_sum(early))
    early = core_exchange(total, count)
    sent, grad_freq = call(
        functools.partial(frequency_back_kernel, norm_h, sizes),
        "frequency_back",
        (1,),
        [
            (got, None, None), (hc, None, None), (hs, None, None), (w_freq_p, None, None), (w_freq_t, None, None),
            (weight, None, None), (sign, None, None), (stacked, None, None),
        ],
        [((n, 384), BF, None, None), ((384, 384), BF, None, None)],
        [vm((3, n, 128), F32), vm(spectral, F32), vm((256, 384), F32), vm((256, 384), F32)],
        flops=3 << 30, bytes_=8 << 20,
    )
    sent, early, d_above, d_below = tied(sent, early, d_above, d_below)
    got = swap(sent, count)
    (d_conv,) = call(
        functools.partial(conv_back_kernel, cl),
        "conv_back",
        (rows,),
        [(d_above, None, None), (d_out, None, None), (d_below, None, None), (wl_t, None, None), (wc_t, None, None)],
        [(wide, F32, one_row(ch), at_y)],
        [vm((rows + 2, width, 3 * cl), BF), vm((rows + 2, width, 3 * cg), BF)],
        flops=18 * pix * (ch * cl + cl * cg), bytes_=9 << 20,
    )
    got, d_conv, early = tied(got, d_conv, early)
    early = early.astype(F32).sum(0).astype(BF)
    early = core_exchange(jnp.tile(early, (count // 2, 1)), count).reshape(-1, 384)
    late_rows = -(-(3 * 384 + 3 * cs) // (16 * count)) * 16 * count
    d_unit, late = call(
        functools.partial(tail_kernel, norm_w, sizes, cl),
        "tail",
        (rows,),
        [
            (got, None, None), (tct, None, None), (tst, None, None), (masked, one_row(ch), at_y),
            (d_joined, one_row(256), at_y), (w_in_d, None, None), (grad_freq, None, None),
        ],
        [((rows, width, 256), BF, one_row(256), at_y), ((late_rows, 128), BF, None, None)],
        [vm((used, 384), BF), vm((used, 256), BF), vm((3, n, 128), F32), vm((256, cg), F32)],
        flops=1 << 30, bytes_=5 << 20,
    )
    late, early = tied(late, early)
    pairs = lax.axis_size("row")
    other = lax.ppermute(early, "row", [(i, i ^ 1) for i in range(pairs)])
    my_core = (lax.axis_index("row") % 2).astype(jnp.int32).reshape(1, 1)
    late = scatter_sum(late, count)
    (grad_features,) = call(
        functools.partial(finish_kernel, cl),
        "finish",
        (rows,),
        [
            (marked, blocks(128), at_blocks), (d_unit, one_row(256), at_y), (d_conv, one_row(ch), at_y),
            (w_in_t, None, None),
        ],
        [(wide, BF, one_row(ch), at_y)],
        flops=2 * pix * 256 * cg, bytes_=7 << 20,
    )
    late, grad_features = tied(late, grad_features)
    grad_local, grad_cross, grad_out = call(
        functools.partial(unpack_kernel, cl),
        "unpack",
        (1,),
        [(early, None, None), (other, None, None), (my_core, None, None)],
        [((3, 3, ch, cl), F32, None, None), ((9 * cl, cg), F32, None, None), ((cs, cg), F32, None, None)],
        flops=1, bytes_=7 << 20,
    )
    late = gather(late, count)
    late, grad_local, grad_cross, grad_out = tied(late, grad_local, grad_cross, grad_out)
    grad_freq = jnp.concatenate([late[k * 384 : (k + 1) * 384] for k in range(3)], 1).astype(F32)
    at = 3 * 384
    grad_in = jnp.concatenate([late[at + k * cs : at + (k + 1) * cs] for k in range(3)], 1).astype(F32).T
    grad_cross = grad_cross.reshape(3, 3, cl, cg)
    return output[None], grad_features[None], grad_local, grad_cross, grad_in, grad_freq, grad_out


def solution(mesh):
    return jax.shard_map(
        shards,
        mesh=mesh,
        in_specs=(
            P("dp", "row", "col", None),
            P("dp", "row", "col"),
            P("dp", "row", "col", None),
            P(),
            P(),
            P(),
            P(),
            P(),
        ),
        out_specs=(
            P("dp", ("row", "col"), None, None),
            P("dp", ("row", "col"), None, None),
            P("dp", None, None, None),
            P("dp", None, None, None),
            P("dp", None),
            P("dp", None),
            P("dp", None),
        ),
        check_vma=False,
    )
```

```python
import functools
import math

import jax
import jax.numpy as jnp
import numpy as np
from jax import lax
from jax.experimental import pallas as pl
from jax.experimental.pallas import tpu as pltpu
from jax.sharding import PartitionSpec as P

AXES = ("row", "col")
HOLE = 64.0
BF = jnp.bfloat16
F32 = jnp.float32
ROWS_OF = ((0,), (0,))


def dot(a, b, dims=((1,), (0,))):
    return lax.dot_general(a, b, (dims, ((), ())), preferred_element_type=F32)


def line_tables(width, count, lines):
    freq = (lines * np.arange(count)[None] + np.arange(lines)[:, None]).reshape(-1, 1)
    angle = 2.0 * np.pi * (freq * np.arange(width) % width) / width
    valid = freq <= width // 2
    return (np.cos(angle) * valid).astype(BF), (np.sin(angle) * valid).astype(BF)


def column_tables(rows, count):
    h = (rows * np.arange(count)[None] + np.arange(rows)[:, None]).reshape(-1)
    angle = 2.0 * np.pi * (h[:, None] * h[None] % (rows * count)) / (rows * count)
    return np.cos(angle).astype(BF), np.sin(angle).astype(BF)


def slope_and_silu(value):
    sigma = 1.0 / (1.0 + jnp.exp(-value))
    return sigma * (1.0 + value * (1.0 - sigma)), value * sigma


def lanes_below(shape, bound):
    return lax.broadcasted_iota(jnp.int32, shape, 1) < bound


def packed(re, im):
    mid = jnp.where(lanes_below(re[:, 128:].shape, 64), re[:, 128:], im[:, 128:])
    return jnp.concatenate([re[:, :128], mid, im[:, :128]], 1)


def turned(p, q, sign):
    mid = pltpu.roll(q[:, 128:256], 64, 1)
    flip = jnp.where(lanes_below(mid.shape, 64), sign, -sign)
    return jnp.concatenate(
        [p[:, :128] + sign * q[:, 256:], p[:, 128:256] + flip * mid, p[:, 256:] - sign * q[:, :128]], 1
    )


def natural_lanes(x):
    mid, im = x[:, 128:256], pltpu.roll(x[:, 256:], 64, 1)
    low = lanes_below(mid.shape, 64)
    return jnp.concatenate([x[:, :128], jnp.where(low, mid, im), jnp.where(low, im, mid)], 1)


def pack_order(cs):
    return [(0, 128), (128, cs), (cs + 128, 2 * cs), (cs, cs + 128)]


def pack_dim(x, dim, cs):
    return jnp.concatenate([lax.slice_in_dim(x, a, b, axis=dim) for a, b in pack_order(cs)], dim)


def call(body, name, grid, ins, outs, scratch=(), flops=0, bytes_=0):
    def spec(shape, block, index):
        if shape[0] == 1 and shape[-1] < 8:
            return pl.BlockSpec(memory_space=pltpu.SMEM)
        if block is None:
            zeros = (0,) * len(shape)
            return pl.BlockSpec(shape, lambda *_: zeros)
        return pl.BlockSpec(block, index)

    return pl.pallas_call(
        body,
        grid=grid,
        in_specs=[spec(a.shape, block, index) for a, block, index in ins],
        out_specs=[spec(shape, block, index) for shape, _, block, index in outs],
        out_shape=[jax.ShapeDtypeStruct(shape, dtype) for shape, dtype, _, _ in outs],
        scratch_shapes=list(scratch),
        compiler_params=pltpu.CompilerParams(vmem_limit_bytes=56 << 20),
        cost_estimate=pl.CostEstimate(flops=flops, bytes_accessed=bytes_, transcendentals=0),
        name=name,
    )(*[a for a, _, _ in ins])


def put_slots(sizes, z, value_of, sent):
    rows, lines, count, slots = sizes
    for q in range(slots):
        value = value_of(q // lines, q % lines) if q < rows * lines else jnp.zeros((count, 384), F32)
        for k in range(3):
            z[k, pl.ds(q, count, stride=slots), :] = value[:, k * 128 : (k + 1) * 128]
    for k in range(3):
        sent[:, k * 128 : (k + 1) * 128] = z[k].astype(BF)


def spread(got, z):
    for k in range(3):
        z[k] = got[:, k * 128 : (k + 1) * 128].astype(F32)


def slot(sizes, z, q):
    _, _, count, slots = sizes
    return jnp.concatenate([z[k, pl.ds(q, count, stride=slots), :] for k in range(3)], 1)


def take_slots(sizes, got, z, x):
    rows, lines, count, slots = sizes
    spread(got, z)
    for q in range(rows * lines):
        x[q * count : (q + 1) * count, :] = slot(sizes, z, q).astype(BF)


def head_kernel(norm, sizes, cl, marked, w_in, tc, ts, masked, unit, sent, v, z):
    y = pl.program_id(0)
    x = marked[...].reshape(-1, marked.shape[-1])
    keep = x[:, :1].astype(F32) < 0.5 * HOLE
    x = jnp.where(keep, x, jnp.zeros_like(x))
    masked[0] = x
    u = slope_and_silu(dot(x[:, cl:], w_in[...]))[1].astype(BF)
    unit[0] = u
    transform_out(y, norm, sizes, u, tc, ts, sent, v, z)


def transform_out(y, norm, sizes, u, tc, ts, sent, v, z):
    count = sizes[2]
    v[y] = packed(dot(tc[...], u) * norm, dot(ts[...], u) * -norm)

    @pl.when(y == pl.num_programs(0) - 1)
    def _():
        put_slots(sizes, z, lambda row, j: v[row, j * count : (j + 1) * count, :], sent)


def column_line(sizes, z, j):
    rows, lines, count, slots = sizes
    parts = [slot(sizes, z, row * lines + j) for row in range(rows)]
    return jnp.concatenate(parts, 0).astype(BF)


def frequency_kernel(norm, sizes, got, hc, hs, w_freq, weight, sign, stacked, sent, z, v):
    count = sizes[2]
    spread(got, z)
    for j in range(sizes[1]):
        x = column_line(sizes, z, j)
        st = (turned(dot(hc[...], x), dot(hs[...], x), 1.0) * norm).astype(BF)
        stacked[j] = st
        pos = slope_and_silu(dot(st, w_freq[...]))[1]
        neg = slope_and_silu(dot((st.astype(F32) * sign[...]).astype(BF), w_freq[...]))[1]
        x = (weight[0, j] * (pos + sign[...] * neg)).astype(BF)
        v[j] = turned(dot(hc[...], x), dot(hs[...], x), -1.0) * norm
    put_slots(sizes, z, lambda row, j: v[j, row * count : (row + 1) * count, :], sent)


def frequency_back_kernel(
    norm, sizes, got, hc, hs, w_freq, w_freq_t, weight, sign, stacked, sent, grad, z, v, acc_p, acc_m
):
    count = sizes[2]
    spread(got, z)
    for j in range(sizes[1]):
        x = column_line(sizes, z, j)
        dz = turned(dot(hc[...], x), dot(hs[...], x), 1.0) * norm
        st = stacked[j]
        pos = slope_and_silu(dot(st, w_freq[...]))[0]
        neg = slope_and_silu(dot((st.astype(F32) * sign[...]).astype(BF), w_freq[...]))[0]
        pos = (dz * pos).astype(BF).astype(F32)
        neg = (dz * sign[...] * neg).astype(BF).astype(F32)
        total = (weight[0, j] * (pos + neg)).astype(BF)
        delta = (weight[0, j] * (pos - neg)).astype(BF)
        g_p = dot(st[:, :256], total, ROWS_OF)
        g_m = dot(st[:, 128:], delta, ROWS_OF)
        acc_p[...] = g_p if j == 0 else acc_p[...] + g_p
        acc_m[...] = g_m if j == 0 else acc_m[...] + g_m
        re = dot(total, w_freq_t[:, :256])
        im = dot(delta, w_freq_t[:, 128:])
        mid = jnp.where(lanes_below((re.shape[0], 128), 64), re[:, 128:], im[:, :128])
        x = jnp.concatenate([re[:, :128], mid, im[:, 128:]], 1).astype(BF)
        v[j] = turned(dot(hc[...], x), dot(hs[...], x), -1.0) * norm
    put_slots(sizes, z, lambda row, j: v[j, row * count : (row + 1) * count, :], sent)
    grad[0:192, :] = natural_lanes(acc_p[0:192, :]).astype(BF)
    grad[192:320, :] = natural_lanes(acc_m[128:256, :]).astype(BF)
    grad[320:384, :] = natural_lanes(acc_m[64:128, :]).astype(BF)


def imag_first(got):
    mid = pltpu.roll(got[:, 128:256].astype(F32), 64, 1).astype(BF)
    return jnp.concatenate([got[:, 256:], mid], 1)


def line_back(y, norm, sizes, got, tct, tst, z, got_x, got_s):
    @pl.when(y == 0)
    def _():
        take_slots(sizes, got, z, got_x)
        got_s[...] = imag_first(got_x[...])

    size = sizes[1] * sizes[2]
    at = pl.ds(pl.multiple_of(y * size, size), size)
    return ((dot(tct[...], got_x[at, :256]) - dot(tst[...], got_s[at, :])) * norm).astype(BF)


def middle_kernel(
    norm, sizes, cl, cols, got, tct, tst, tc, ts, unit, pre, w_out, w_out_t, my_col, *refs,
):
    cots = refs[:cols]
    output, d_out, d_joined, sent, grad, got_x, got_s, cot, v, z, acc_g = refs[cols:]
    y = pl.program_id(0)
    w = cots[0].shape[1]
    for k in range(cols):
        at = lax.rem(my_col[0, 0] + (cols - k), cols)
        cot[pl.ds(pl.multiple_of(at * w, w), w), :] = cots[k][0]

    back = line_back(y, norm, sizes, got, tct, tst, z, got_x, got_s)
    joined = (unit[0].astype(F32) + back.astype(F32)).astype(BF)
    pre_all = jnp.concatenate([pre[0, :, :cl], pre[0, :, cl:] + dot(joined, w_out[...])], 1)
    slope, silu = slope_and_silu(pre_all)
    output[0] = silu.astype(BF)
    d = (cot[...].astype(F32) * slope).astype(BF)
    d_out[0] = d
    dj = dot(d[:, cl:], w_out_t[...]).astype(BF)
    d_joined[0] = dj
    g = dot(joined, d[:, cl:], ROWS_OF)

    @pl.when(y == 0)
    def _():
        acc_g[...] = g

    @pl.when(y > 0)
    def _():
        acc_g[...] += g

    transform_out(y, norm, sizes, dj, tc, ts, sent, v, z)

    @pl.when(y == pl.num_programs(0) - 1)
    def _():
        grad[...] = acc_g[0 : grad.shape[0], :].astype(BF)


def tail_kernel(
    norm, sizes, cl, got, tct, tst, masked, d_joined, w_in, grad_freq, d_unit, late, got_x, got_s, z, acc_g
):
    y = pl.program_id(0)

    back = line_back(y, norm, sizes, got, tct, tst, z, got_x, got_s)
    x = masked[0, :, cl:]
    slope = slope_and_silu(dot(x, w_in[...]))[0]
    du = ((d_joined[0].astype(F32) + back.astype(F32)) * slope).astype(BF)
    g = dot(du, x, ROWS_OF)

    @pl.when(y == 0)
    def _():
        acc_g[...] = g

    @pl.when(y > 0)
    def _():
        acc_g[...] += g

    d_unit[0] = du

    @pl.when(y == pl.num_programs(0) - 1)
    def _():
        at = 0
        for part, size in ((grad_freq, 384), (acc_g, 192)):
            for k in range(3):
                late[at : at + size, :] = part[0:size, k * 128 : (k + 1) * 128].astype(BF)
                at += size
        late[at:, :] = jnp.zeros((late.shape[0] - at, 128), BF)


def finish_kernel(cl, marked, d_unit, d_conv, w_in_t, grad_features):
    keep = marked[...].reshape(-1, marked.shape[-1])[:, :1].astype(F32) < 0.5 * HOLE
    total = jnp.concatenate([d_conv[0, :, :cl], d_conv[0, :, cl:] + dot(d_unit[0], w_in_t[...])], 1)
    grad_features[0] = jnp.where(keep, total, 0.0).astype(BF)


def shifted(x, step):
    n = x.shape[0]
    at = lax.broadcasted_iota(jnp.int32, x.shape, 0)
    if step == 1:
        return jnp.where(at == 0, 0.0, pltpu.roll(x, 1, 0))
    return jnp.where(at == n - 1, 0.0, pltpu.roll(x, n - 1, 0))


def three(x):
    f = x.astype(F32)
    return jnp.concatenate([shifted(f, -1).astype(BF), x, shifted(f, 1).astype(BF)], 1)


def conv_kernel(cl, above, masked, below, w_local, w_cross, pre, pad):
    y = pl.program_id(0)
    rows = masked.shape[0]

    @pl.when(y == 0)
    def _():
        pad[0] = above[0]
        pad[1 : rows + 1] = masked[...]
        pad[rows + 1] = below[0]

    local = dot(pad[y], w_local[0]) + dot(pad[y + 1], w_local[1]) + dot(pad[y + 2], w_local[2])
    near = jnp.concatenate([pad[y, :, :cl], pad[y + 1, :, :cl], pad[y + 2, :, :cl]], 1)
    cross = dot(near, w_cross[...])
    c, g = cl, w_cross.shape[1] // 3
    pre[0, :, :cl] = shifted(local[:, :c], 1) + local[:, c : 2 * c] + shifted(local[:, 2 * c :], -1)
    pre[0, :, cl:] = shifted(cross[:, :g], 1) + cross[:, g : 2 * g] + shifted(cross[:, 2 * g :], -1)


def conv_grad_kernel(cl, above, masked, below, d_out, g_out, core, mine, other, pad, acc_l, acc_c):
    y = pl.program_id(0)
    rows = masked.shape[0]

    @pl.when(y == 0)
    def _():
        pad[0] = above[0]
        pad[1 : rows + 1] = masked[...]
        pad[rows + 1] = below[0]
        acc_l[...] = jnp.zeros_like(acc_l)
        acc_c[...] = jnp.zeros_like(acc_c)

    d_local = three(d_out[0, :, :cl])
    d_global = three(d_out[0, :, cl:])
    g = d_global.shape[1] // 3
    for i in range(3):
        x = pad[y + i]
        acc_l[i] += dot(x, d_local, ROWS_OF)
        acc_c[i] += dot(x[:, :cl], d_global, ROWS_OF)

    def write(local, rest):
        ch = masked.shape[2]
        for i in range(3):
            local[i * ch : (i + 1) * ch, :] = acc_l[i].astype(BF)
            for j in range(3):
                at = (3 * i + j) * cl
                rest[at : at + cl, :] = acc_c[i, :, j * g : (j + 1) * g].astype(BF)
        at, size = 9 * cl, g_out.shape[0]
        rest[at : at + size, :] = g_out[...]
        rest[at + size :, :] = jnp.zeros((rest.shape[0] - at - size, g), BF)

    last = y == pl.num_programs(0) - 1

    @pl.when(last & (core[0, 0] == 0))
    def _():
        write(mine, other)

    @pl.when(last & (core[0, 0] == 1))
    def _():
        write(other, mine)


def unpack_kernel(cl, mine, other, core, g_local, g_cross, g_out):
    ch = g_local.shape[2]

    def write(local, rest):
        for at in range(0, 3 * ch, 64):
            block = local[at : at + 64, :].astype(F32)
            for j in range(3):
                g_local[at // ch, j, at % ch : at % ch + 64, :] = block[:, j * cl : (j + 1) * cl]
        g_cross[...] = rest[0 : 9 * cl, :].astype(F32)
        g_out[...] = rest[9 * cl : 9 * cl + g_out.shape[0], :].astype(F32)

    @pl.when(core[0, 0] == 0)
    def _():
        write(mine, other)

    @pl.when(core[0, 0] == 1)
    def _():
        write(other, mine)


def conv_back_kernel(cl, above, d_out, below, w_local, w_cross, d_conv, pad_l, pad_g):
    y = pl.program_id(0)
    rows = d_out.shape[0]

    @pl.when(y == 0)
    def _():
        for k in range(rows + 2):
            line = above[0] if k == 0 else below[0] if k == rows + 1 else d_out[k - 1]
            pad_l[k] = three(line[:, :cl])
            pad_g[k] = three(line[:, cl:])

    total = dot(pad_l[y + 2], w_local[0]) + dot(pad_l[y + 1], w_local[1]) + dot(pad_l[y], w_local[2])
    cross = dot(pad_g[y + 2], w_cross[0]) + dot(pad_g[y + 1], w_cross[1]) + dot(pad_g[y], w_cross[2])
    d_conv[0, :, :cl] = total[:, :cl] + cross
    d_conv[0, :, cl:] = total[:, cl:]


def swap(x, count):
    return lax.all_to_all(x.reshape(count, -1, x.shape[-1]), AXES, 0, 0, tiled=True).reshape(x.shape)


def to_rows(field, cols):
    h, w, c = field.shape
    return lax.all_to_all(field.reshape(cols, h // cols, w, c), "col", 0, 0, tiled=True)


def turn(field, cols, after):
    h, w, c = field.shape
    blocks = field.reshape(cols, h // cols, w, c)
    me = lax.axis_index("col")
    parts = [lax.dynamic_index_in_dim(blocks, (me + k) % cols, 0, keepdims=False) for k in range(cols)]
    parts = tied(*parts, after)[:-1]
    moves = [[(i, (i + k) % cols) for i in range(cols)] for k in range(cols)]
    return [lax.ppermute(part, "col", move) if k else part for k, (part, move) in enumerate(zip(parts, moves))]


def core_swap(x):
    return lax.ppermute(x, "row", [(i, i ^ 1) for i in range(lax.axis_size("row"))])


def core_exchange(x, count):
    pairs = lax.axis_size("row")
    cols = count // pairs
    groups = [[cols * r + c for r in range(k, pairs, 2) for c in range(cols)] for k in range(2)]
    x = x.reshape(count // 2, -1, x.shape[-1])
    return lax.all_to_all(x, AXES, 0, 0, axis_index_groups=groups, tiled=True)


def edges(field, count):
    down = lax.ppermute(field[-1:], AXES, [(i, i + 1) for i in range(count - 1)])
    up = lax.ppermute(field[:1], AXES, [(i + 1, i) for i in range(count - 1)])
    return down, up


def scatter_sum(x, count):
    x = lax.all_to_all(x.reshape(count, -1, x.shape[-1]), AXES, 0, 0, tiled=True)
    return x.astype(F32).sum(0).astype(BF)


def gather(x, count):
    x = lax.all_to_all(jnp.broadcast_to(x[None], (count,) + x.shape), AXES, 0, 0, tiled=True)
    return x.reshape(-1, x.shape[-1])


def tie(value, *after):
    return lax.optimization_barrier((value,) + after)[0]


def tied(*values):
    return lax.optimization_barrier(values)


def shards(features, hole_mask, cotangent, w_local, w_cross, w_in, w_freq, w_out):
    cols = lax.axis_size("col")
    count = lax.axis_size("row") * cols
    me = lax.axis_index(AXES)
    _, h, w, ch = features.shape
    rows, width = h // cols, w * cols
    height = rows * count
    cl, cg, cs = w_local.shape[3], w_cross.shape[3], w_in.shape[1]
    lines = -(-(width // 2 + 1) // count)
    slots = -(-(rows * lines) // 16) * 16
    n = count * slots
    sizes = (rows, lines, count, slots)
    tc, ts = line_tables(width, count, lines)
    tct, tst = jnp.asarray(tc.T), jnp.asarray(ts.T)
    tc, ts = jnp.asarray(tc), jnp.asarray(ts)
    hc, hs = (jnp.asarray(t) for t in column_tables(rows, count))
    norm_w, norm_h = 1.0 / math.sqrt(width), 1.0 / math.sqrt(height)
    freq = lines * me + jnp.arange(lines)
    weight = jnp.where((freq == 0) | (freq * 2 == width), 0.5, jnp.where(freq * 2 < width, 1.0, 0.0))
    weight = weight.astype(F32)[None]
    sign = np.where((np.arange(384) < 192), 1.0, -1.0).astype(np.float32)
    sign = jnp.asarray(sign[None])

    w_in_d = jnp.concatenate([w_in, w_in[:, 128:]], 1)
    w_in_t = jnp.pad(w_in.T, ((0, 64), (0, 0)))
    w_out_z = jnp.pad(w_out, ((0, 64), (0, 0)))
    w_out_t = jnp.concatenate([w_out, w_out[128:]], 0).T
    w_freq_p = pack_dim(pack_dim(w_freq, 0, cs), 1, cs)
    w_freq_t = w_freq_p.T
    wl = jnp.transpose(w_local, (0, 2, 1, 3)).reshape(3, ch, 3 * cl)
    wc = jnp.transpose(w_cross, (0, 2, 1, 3)).reshape(3 * cl, 3 * cg)
    wl_t = jnp.transpose(w_local, (0, 1, 3, 2)).reshape(3, 3 * cl, ch)
    wc_t = jnp.transpose(w_cross, (0, 1, 3, 2)).reshape(3, 3 * cg, cl)

    at_y = lambda y: (y, 0, 0)
    one_row = lambda c: (1, width, c)
    blocks = lambda c: (cols, 1, w, c)
    at_blocks = lambda y: (0, y, 0, 0)
    wide = (rows, width, ch)
    pix = rows * width
    vm = pltpu.VMEM
    lined = (rows, lines * count, 384)
    spectral = (lines, height, 384)
    used = rows * lines * count

    marked = jnp.where(hole_mask[0][..., None] == 1, HOLE, features[0]).astype(BF)
    marked = to_rows(marked, cols)
    w_in_d, w_in_t, w_out_z, w_out_t, w_freq_p, w_freq_t, wl, wc, wl_t, wc_t, weight = tied(
        w_in_d, w_in_t, w_out_z, w_out_t, w_freq_p, w_freq_t, wl, wc, wl_t, wc_t, weight
    )
    cots = turn(cotangent[0], cols, marked)
    my_col = lax.axis_index("col").astype(jnp.int32).reshape(1, 1)

    masked, unit, sent = call(
        functools.partial(head_kernel, norm_w, sizes, cl),
        "head",
        (rows,),
        [(marked, blocks(ch), at_blocks), (w_in_d, None, None), (tc, None, None), (ts, None, None)],
        [(wide, BF, one_row(ch), at_y), ((rows, width, 256), BF, one_row(256), at_y), ((n, 384), BF, None, None)],
        [vm(lined, F32), vm((3, n, 128), F32)],
        flops=1 << 30, bytes_=6 << 20,
    )
    near = [k for k in range(cols) if k in (0, 1, cols - 1)]
    sent, *moved = tied(sent, *[cots[k] for k in near])
    for k, c in zip(near, moved):
        cots[k] = c
    above, below = edges(masked, count)
    got = swap(sent, count)
    stacked, sent = call(
        functools.partial(frequency_kernel, norm_h, sizes),
        "frequency",
        (1,),
        [(got, None, None), (hc, None, None), (hs, None, None), (w_freq_p, None, None), (weight, None, None), (sign, None, None)],
        [(spectral, BF, None, None), ((n, 384), BF, None, None)],
        [vm((3, n, 128), F32), vm(spectral, F32)],
        flops=3 << 30, bytes_=7 << 20,
    )
    sent, above, below, *cots = tied(sent, above, below, *cots)
    got = swap(sent, count)
    (pre,) = call(
        functools.partial(conv_kernel, cl),
        "conv",
        (rows,),
        [(above, None, None), (masked, None, None), (below, None, None), (wl, None, None), (wc, None, None)],
        [(wide, F32, one_row(ch), at_y)],
        [vm((rows + 2, width, ch), BF)],
        flops=18 * pix * (ch * cl + cl * cg), bytes_=9 << 20,
    )
    output, d_out, d_joined, sent, grad_out = call(
        functools.partial(middle_kernel, norm_w, sizes, cl, cols),
        "middle",
        (rows,),
        [
            (got, None, None), (tct, None, None), (tst, None, None), (tc, None, None),
            (ts, None, None), (unit, one_row(256), at_y), (pre, one_row(ch), at_y),
            (w_out_z, None, None), (w_out_t, None, None), (my_col, None, None),
        ]
        + [(c, (1, w, ch), at_y) for c in cots],
        [
            (wide, BF, one_row(ch), at_y), (wide, BF, one_row(ch), at_y), ((rows, width, 256), BF, one_row(256), at_y),
            ((n, 384), BF, None, None), ((cs, cg), BF, None, None),
        ],
        [vm((used, 384), BF), vm((used, 256), BF), vm((width, ch), BF), vm(lined, F32), vm((3, n, 128), F32), vm((256, cg), F32)],
        flops=3 << 30, bytes_=12 << 20,
    )
    got = swap(sent, count)
    d_above, d_below = edges(d_out, count)
    my_core = (lax.axis_index("row") % 2).astype(jnp.int32).reshape(1, 1)
    mine, other = call(
        functools.partial(conv_grad_kernel, cl),
        "conv_grad",
        (rows,),
        [(above, None, None), (masked, None, None), (below, None, None), (d_out, one_row(ch), at_y), (grad_out, None, None), (my_core, None, None)],
        [((3 * ch, 384), BF, None, None), ((3 * ch, 384), BF, None, None)],
        [vm((rows + 2, width, ch), BF), vm((3, ch, 3 * cl), F32), vm((3, cl, 3 * cg), F32)],
        flops=18 * pix * (ch * cl + cl * cg), bytes_=7 << 20,
    )
    got, other = tied(got, other)
    got, total = tied(got, (mine.astype(F32) + core_swap(other).astype(F32)).astype(BF))
    early = core_exchange(total, count)
    sent, grad_freq = call(
        functools.partial(frequency_back_kernel, norm_h, sizes),
        "frequency_back",
        (1,),
        [
            (got, None, None), (hc, None, None), (hs, None, None), (w_freq_p, None, None), (w_freq_t, None, None),
            (weight, None, None), (sign, None, None), (stacked, None, None),
        ],
        [((n, 384), BF, None, None), ((384, 384), BF, None, None)],
        [vm((3, n, 128), F32), vm(spectral, F32), vm((256, 384), F32), vm((256, 384), F32)],
        flops=3 << 30, bytes_=8 << 20,
    )
    sent, early, d_above, d_below = tied(sent, early, d_above, d_below)
    got = swap(sent, count)
    (d_conv,) = call(
        functools.partial(conv_back_kernel, cl),
        "conv_back",
        (rows,),
        [(d_above, None, None), (d_out, None, None), (d_below, None, None), (wl_t, None, None), (wc_t, None, None)],
        [(wide, F32, one_row(ch), at_y)],
        [vm((rows + 2, width, 3 * cl), BF), vm((rows + 2, width, 3 * cg), BF)],
        flops=18 * pix * (ch * cl + cl * cg), bytes_=9 << 20,
    )
    got, d_conv, early = tied(got, d_conv, early)
    early = early.astype(F32).sum(0).astype(BF)
    early = core_exchange(jnp.tile(early, (count // 2, 1)), count).reshape(-1, 384)
    late_rows = -(-(3 * 384 + 3 * cs) // (16 * count)) * 16 * count
    d_unit, late = call(
        functools.partial(tail_kernel, norm_w, sizes, cl),
        "tail",
        (rows,),
        [
            (got, None, None), (tct, None, None), (tst, None, None), (masked, one_row(ch), at_y),
            (d_joined, one_row(256), at_y), (w_in_d, None, None), (grad_freq, None, None),
        ],
        [((rows, width, 256), BF, one_row(256), at_y), ((late_rows, 128), BF, None, None)],
        [vm((used, 384), BF), vm((used, 256), BF), vm((3, n, 128), F32), vm((256, cg), F32)],
        flops=1 << 30, bytes_=5 << 20,
    )
    late, early = tied(late, early)
    other = core_swap(early)
    late = scatter_sum(late, count)
    (grad_features,) = call(
        functools.partial(finish_kernel, cl),
        "finish",
        (rows,),
        [
            (marked, blocks(128), at_blocks), (d_unit, one_row(256), at_y), (d_conv, one_row(ch), at_y),
            (w_in_t, None, None),
        ],
        [(wide, BF, one_row(ch), at_y)],
        flops=2 * pix * 256 * cg, bytes_=7 << 20,
    )
    late, grad_features = tied(late, grad_features)
    grad_local, grad_cross, grad_out = call(
        functools.partial(unpack_kernel, cl),
        "unpack",
        (1,),
        [(early, None, None), (other, None, None), (my_core, None, None)],
        [((3, 3, ch, cl), F32, None, None), ((9 * cl, cg), F32, None, None), ((cs, cg), F32, None, None)],
        flops=1, bytes_=7 << 20,
    )
    late = gather(late, count)
    late, grad_local, grad_cross, grad_out = tied(late, grad_local, grad_cross, grad_out)
    grad_freq = jnp.concatenate([late[k * 384 : (k + 1) * 384] for k in range(3)], 1).astype(F32)
    at = 3 * 384
    grad_in = jnp.concatenate([late[at + k * cs : at + (k + 1) * cs] for k in range(3)], 1).astype(F32).T
    grad_cross = grad_cross.reshape(3, 3, cl, cg)
    return output[None], grad_features[None], grad_local, grad_cross, grad_in, grad_freq, grad_out


def solution(mesh):
    return jax.shard_map(
        shards,
        mesh=mesh,
        in_specs=(
            P("dp", "row", "col", None),
            P("dp", "row", "col"),
            P("dp", "row", "col", None),
            P(),
            P(),
            P(),
            P(),
            P(),
        ),
        out_specs=(
            P("dp", ("row", "col"), None, None),
            P("dp", ("row", "col"), None, None),
            P("dp", None, None, None),
            P("dp", None, None, None),
            P("dp", None),
            P("dp", None),
            P("dp", None),
        ),
        check_vma=False,
    )
```

```python
import functools
import math

import jax
import jax.numpy as jnp
import numpy as np
from jax import lax
from jax.experimental import pallas as pl
from jax.experimental.pallas import tpu as pltpu
from jax.sharding import PartitionSpec as P

AXES = ("row", "col")
HOLE = 64.0
BF = jnp.bfloat16
F32 = jnp.float32
ROWS_OF = ((0,), (0,))


def dot(a, b, dims=((1,), (0,))):
    return lax.dot_general(a, b, (dims, ((), ())), preferred_element_type=F32)


def line_tables(width, count, lines):
    freq = (lines * np.arange(count)[None] + np.arange(lines)[:, None]).reshape(-1, 1)
    angle = 2.0 * np.pi * (freq * np.arange(width) % width) / width
    valid = freq <= width // 2
    return (np.cos(angle) * valid).astype(BF), (np.sin(angle) * valid).astype(BF)


def column_tables(rows, count):
    h = (rows * np.arange(count)[None] + np.arange(rows)[:, None]).reshape(-1)
    angle = 2.0 * np.pi * (h[:, None] * h[None] % (rows * count)) / (rows * count)
    return np.cos(angle).astype(BF), np.sin(angle).astype(BF)


def slope_and_silu(value):
    sigma = 0.5 + 0.5 * jnp.tanh(0.5 * value)
    return sigma * (1.0 + value * (1.0 - sigma)), value * sigma


def lanes_below(shape, bound):
    return lax.broadcasted_iota(jnp.int32, shape, 1) < bound


def packed(re, im):
    mid = jnp.where(lanes_below(re[:, 128:].shape, 64), re[:, 128:], im[:, 128:])
    return jnp.concatenate([re[:, :128], mid, im[:, :128]], 1)


def turned(p, q, sign):
    mid = pltpu.roll(q[:, 128:256], 64, 1)
    flip = jnp.where(lanes_below(mid.shape, 64), sign, -sign)
    return jnp.concatenate(
        [p[:, :128] + sign * q[:, 256:], p[:, 128:256] + flip * mid, p[:, 256:] - sign * q[:, :128]], 1
    )


def natural_lanes(x):
    mid, im = x[:, 128:256], pltpu.roll(x[:, 256:], 64, 1)
    low = lanes_below(mid.shape, 64)
    return jnp.concatenate([x[:, :128], jnp.where(low, mid, im), jnp.where(low, im, mid)], 1)


def pack_order(cs):
    return [(0, 128), (128, cs), (cs + 128, 2 * cs), (cs, cs + 128)]


def pack_dim(x, dim, cs):
    return jnp.concatenate([lax.slice_in_dim(x, a, b, axis=dim) for a, b in pack_order(cs)], dim)


def call(body, name, grid, ins, outs, scratch=(), flops=0, bytes_=0):
    def spec(shape, block, index):
        if shape[0] == 1 and shape[-1] < 8:
            return pl.BlockSpec(memory_space=pltpu.SMEM)
        if block is None:
            zeros = (0,) * len(shape)
            return pl.BlockSpec(shape, lambda *_: zeros)
        return pl.BlockSpec(block, index)

    return pl.pallas_call(
        body,
        grid=grid,
        in_specs=[spec(a.shape, block, index) for a, block, index in ins],
        out_specs=[spec(shape, block, index) for shape, _, block, index in outs],
        out_shape=[jax.ShapeDtypeStruct(shape, dtype) for shape, dtype, _, _ in outs],
        scratch_shapes=list(scratch),
        compiler_params=pltpu.CompilerParams(vmem_limit_bytes=56 << 20),
        cost_estimate=pl.CostEstimate(flops=flops, bytes_accessed=bytes_, transcendentals=0),
        name=name,
    )(*[a for a, _, _ in ins])


def put_slots(sizes, z, value_of, sent):
    rows, lines, count, slots = sizes
    for q in range(slots):
        value = value_of(q // lines, q % lines) if q < rows * lines else jnp.zeros((count, 384), F32)
        for k in range(3):
            z[k, pl.ds(q, count, stride=slots), :] = value[:, k * 128 : (k + 1) * 128]
    for k in range(3):
        sent[:, k * 128 : (k + 1) * 128] = z[k].astype(BF)


def spread(got, z):
    for k in range(3):
        z[k] = got[:, k * 128 : (k + 1) * 128].astype(F32)


def slot(sizes, z, q):
    _, _, count, slots = sizes
    return jnp.concatenate([z[k, pl.ds(q, count, stride=slots), :] for k in range(3)], 1)


def take_slots(sizes, got, z, x):
    rows, lines, count, slots = sizes
    spread(got, z)
    for q in range(rows * lines):
        x[q * count : (q + 1) * count, :] = slot(sizes, z, q).astype(BF)


def head_kernel(norm, sizes, cl, marked, w_in, tc, ts, masked, unit, sent, v, z):
    y = pl.program_id(0)
    x = marked[...].reshape(-1, marked.shape[-1])
    keep = x[:, :1].astype(F32) < 0.5 * HOLE
    x = jnp.where(keep, x, jnp.zeros_like(x))
    masked[0] = x
    u = slope_and_silu(dot(x[:, cl:], w_in[...]))[1].astype(BF)
    unit[0] = u
    transform_out(y, norm, sizes, u, tc, ts, sent, v, z)


def transform_out(y, norm, sizes, u, tc, ts, sent, v, z):
    count = sizes[2]
    v[y] = packed(dot(tc[...], u) * norm, dot(ts[...], u) * -norm)

    @pl.when(y == pl.num_programs(0) - 1)
    def _():
        put_slots(sizes, z, lambda row, j: v[row, j * count : (j + 1) * count, :], sent)


def column_line(sizes, z, j):
    rows, lines, count, slots = sizes
    parts = [slot(sizes, z, row * lines + j) for row in range(rows)]
    return jnp.concatenate(parts, 0).astype(BF)


def frequency_kernel(norm, sizes, got, hc, hs, w_freq, weight, sign, stacked, sent, z, v):
    count = sizes[2]
    spread(got, z)
    for j in range(sizes[1]):
        x = column_line(sizes, z, j)
        st = (turned(dot(hc[...], x), dot(hs[...], x), 1.0) * norm).astype(BF)
        stacked[j] = st
        pos = slope_and_silu(dot(st, w_freq[...]))[1]
        neg = slope_and_silu(dot((st.astype(F32) * sign[...]).astype(BF), w_freq[...]))[1]
        x = (weight[0, j] * (pos + sign[...] * neg)).astype(BF)
        v[j] = turned(dot(hc[...], x), dot(hs[...], x), -1.0) * norm
    put_slots(sizes, z, lambda row, j: v[j, row * count : (row + 1) * count, :], sent)


def frequency_back_kernel(
    norm, sizes, got, hc, hs, w_freq, w_freq_t, weight, sign, stacked, sent, grad, z, v, acc_p, acc_m
):
    count = sizes[2]
    spread(got, z)
    for j in range(sizes[1]):
        x = column_line(sizes, z, j)
        dz = turned(dot(hc[...], x), dot(hs[...], x), 1.0) * norm
        st = stacked[j]
        pos = slope_and_silu(dot(st, w_freq[...]))[0]
        neg = slope_and_silu(dot((st.astype(F32) * sign[...]).astype(BF), w_freq[...]))[0]
        pos = (dz * pos).astype(BF).astype(F32)
        neg = (dz * sign[...] * neg).astype(BF).astype(F32)
        total = (weight[0, j] * (pos + neg)).astype(BF)
        delta = (weight[0, j] * (pos - neg)).astype(BF)
        g_p = dot(st[:, :256], total, ROWS_OF)
        g_m = dot(st[:, 128:], delta, ROWS_OF)
        acc_p[...] = g_p if j == 0 else acc_p[...] + g_p
        acc_m[...] = g_m if j == 0 else acc_m[...] + g_m
        re = dot(total, w_freq_t[:, :256])
        im = dot(delta, w_freq_t[:, 128:])
        mid = jnp.where(lanes_below((re.shape[0], 128), 64), re[:, 128:], im[:, :128])
        x = jnp.concatenate([re[:, :128], mid, im[:, 128:]], 1).astype(BF)
        v[j] = turned(dot(hc[...], x), dot(hs[...], x), -1.0) * norm
    put_slots(sizes, z, lambda row, j: v[j, row * count : (row + 1) * count, :], sent)
    grad[0:192, :] = natural_lanes(acc_p[0:192, :]).astype(BF)
    grad[192:320, :] = natural_lanes(acc_m[128:256, :]).astype(BF)
    grad[320:384, :] = natural_lanes(acc_m[64:128, :]).astype(BF)


def imag_first(got):
    mid = pltpu.roll(got[:, 128:256].astype(F32), 64, 1).astype(BF)
    return jnp.concatenate([got[:, 256:], mid], 1)


def line_back(y, norm, sizes, got, tct, tst, z, got_x, got_s):
    @pl.when(y == 0)
    def _():
        take_slots(sizes, got, z, got_x)
        got_s[...] = imag_first(got_x[...])

    size = sizes[1] * sizes[2]
    at = pl.ds(pl.multiple_of(y * size, size), size)
    return ((dot(tct[...], got_x[at, :256]) - dot(tst[...], got_s[at, :])) * norm).astype(BF)


def middle_kernel(
    norm, sizes, cl, cols, got, tct, tst, tc, ts, unit, pre, w_out, w_out_t, my_col, *refs,
):
    cots = refs[:cols]
    output, d_out, d_joined, sent, joined_out, got_x, got_s, cot, v, z = refs[cols:]
    y = pl.program_id(0)
    w = cots[0].shape[1]
    for k in range(cols):
        at = lax.rem(my_col[0, 0] + (cols - k), cols)
        cot[pl.ds(pl.multiple_of(at * w, w), w), :] = cots[k][0]

    back = line_back(y, norm, sizes, got, tct, tst, z, got_x, got_s)
    joined = (unit[0].astype(F32) + back.astype(F32)).astype(BF)
    joined_out[0] = joined
    pre_all = jnp.concatenate([pre[0, :, :cl], pre[0, :, cl:] + dot(joined, w_out[...])], 1)
    slope, silu = slope_and_silu(pre_all)
    output[0] = silu.astype(BF)
    d = (cot[...].astype(F32) * slope).astype(BF)
    d_out[0] = d
    dj = dot(d[:, cl:], w_out_t[...]).astype(BF)
    d_joined[0] = dj
    transform_out(y, norm, sizes, dj, tc, ts, sent, v, z)


def tail_kernel(
    norm, sizes, cl, got, tct, tst, masked, d_joined, w_in, grad_freq, d_unit, late, got_x, got_s, z, acc_g
):
    y = pl.program_id(0)

    back = line_back(y, norm, sizes, got, tct, tst, z, got_x, got_s)
    x = masked[0, :, cl:]
    slope = slope_and_silu(dot(x, w_in[...]))[0]
    du = ((d_joined[0].astype(F32) + back.astype(F32)) * slope).astype(BF)
    g = dot(du, x, ROWS_OF)

    @pl.when(y == 0)
    def _():
        acc_g[...] = g

    @pl.when(y > 0)
    def _():
        acc_g[...] += g

    d_unit[0] = du

    @pl.when(y == pl.num_programs(0) - 1)
    def _():
        at = 0
        for part, size in ((grad_freq, 384), (acc_g, 192)):
            for k in range(3):
                late[at : at + size, :] = part[0:size, k * 128 : (k + 1) * 128].astype(BF)
                at += size
        late[at:, :] = jnp.zeros((late.shape[0] - at, 128), BF)


def finish_kernel(cl, marked, d_unit, d_conv, w_in_t, grad_features):
    keep = marked[...].reshape(-1, marked.shape[-1])[:, :1].astype(F32) < 0.5 * HOLE
    total = jnp.concatenate([d_conv[0, :, :cl], d_conv[0, :, cl:] + dot(d_unit[0], w_in_t[...])], 1)
    grad_features[0] = jnp.where(keep, total, 0.0).astype(BF)


def shifted(x, step):
    n = x.shape[0]
    at = lax.broadcasted_iota(jnp.int32, x.shape, 0)
    if step == 1:
        return jnp.where(at == 0, 0.0, pltpu.roll(x, 1, 0))
    return jnp.where(at == n - 1, 0.0, pltpu.roll(x, n - 1, 0))


def three(x):
    f = x.astype(F32)
    return jnp.concatenate([shifted(f, -1).astype(BF), x, shifted(f, 1).astype(BF)], 1)


def conv_kernel(cl, above, masked, below, w_local, w_cross, pre, pad):
    y = pl.program_id(0)
    rows = masked.shape[0]

    @pl.when(y == 0)
    def _():
        pad[0] = above[0]
        pad[1 : rows + 1] = masked[...]
        pad[rows + 1] = below[0]

    local = dot(pad[y], w_local[0]) + dot(pad[y + 1], w_local[1]) + dot(pad[y + 2], w_local[2])
    near = jnp.concatenate([pad[y, :, :cl], pad[y + 1, :, :cl], pad[y + 2, :, :cl]], 1)
    cross = dot(near, w_cross[...])
    c, g = cl, w_cross.shape[1] // 3
    pre[0, :, :cl] = shifted(local[:, :c], 1) + local[:, c : 2 * c] + shifted(local[:, 2 * c :], -1)
    pre[0, :, cl:] = shifted(cross[:, :g], 1) + cross[:, g : 2 * g] + shifted(cross[:, 2 * g :], -1)


def conv_grad_kernel(cl, above, masked, below, d_out, joined, core, mine, other, pad, acc_l, acc_c, acc_g):
    y = pl.program_id(0)
    rows = masked.shape[0]

    @pl.when(y == 0)
    def _():
        pad[0] = above[0]
        pad[1 : rows + 1] = masked[...]
        pad[rows + 1] = below[0]
        acc_l[...] = jnp.zeros_like(acc_l)
        acc_c[...] = jnp.zeros_like(acc_c)
        acc_g[...] = jnp.zeros_like(acc_g)

    d_local = three(d_out[0, :, :cl])
    d_global = three(d_out[0, :, cl:])
    g = d_global.shape[1] // 3
    acc_g[...] += dot(joined[0], d_out[0, :, cl:], ROWS_OF)
    for i in range(3):
        x = pad[y + i]
        acc_l[i] += dot(x, d_local, ROWS_OF)
        acc_c[i] += dot(x[:, :cl], d_global, ROWS_OF)

    def write(local, rest):
        ch = masked.shape[2]
        for i in range(3):
            local[i * ch : (i + 1) * ch, :] = acc_l[i].astype(BF)
            for j in range(3):
                at = (3 * i + j) * cl
                rest[at : at + cl, :] = acc_c[i, :, j * g : (j + 1) * g].astype(BF)
        at, size = 9 * cl, 192
        rest[at : at + size, :] = acc_g[0:size, :].astype(BF)
        rest[at + size :, :] = jnp.zeros((rest.shape[0] - at - size, g), BF)

    last = y == pl.num_programs(0) - 1

    @pl.when(last & (core[0, 0] == 0))
    def _():
        write(mine, other)

    @pl.when(last & (core[0, 0] == 1))
    def _():
        write(other, mine)


def unpack_kernel(cl, mine, other, core, g_local, g_cross, g_out):
    ch = g_local.shape[2]

    def write(local, rest):
        for at in range(0, 3 * ch, 64):
            block = local[at : at + 64, :].astype(F32)
            for j in range(3):
                g_local[at // ch, j, at % ch : at % ch + 64, :] = block[:, j * cl : (j + 1) * cl]
        g_cross[...] = rest[0 : 9 * cl, :].astype(F32)
        g_out[...] = rest[9 * cl : 9 * cl + g_out.shape[0], :].astype(F32)

    @pl.when(core[0, 0] == 0)
    def _():
        write(mine, other)

    @pl.when(core[0, 0] == 1)
    def _():
        write(other, mine)


def conv_back_kernel(cl, above, d_out, below, w_local, w_cross, d_conv, pad_l, pad_g):
    y = pl.program_id(0)
    rows = d_out.shape[0]

    @pl.when(y == 0)
    def _():
        for k in range(rows + 2):
            line = above[0] if k == 0 else below[0] if k == rows + 1 else d_out[k - 1]
            pad_l[k] = three(line[:, :cl])
            pad_g[k] = three(line[:, cl:])

    total = dot(pad_l[y + 2], w_local[0]) + dot(pad_l[y + 1], w_local[1]) + dot(pad_l[y], w_local[2])
    cross = dot(pad_g[y + 2], w_cross[0]) + dot(pad_g[y + 1], w_cross[1]) + dot(pad_g[y], w_cross[2])
    d_conv[0, :, :cl] = total[:, :cl] + cross
    d_conv[0, :, cl:] = total[:, cl:]


def swap(x, count):
    return lax.all_to_all(x.reshape(count, -1, x.shape[-1]), AXES, 0, 0, tiled=True).reshape(x.shape)


def to_rows(field, cols):
    h, w, c = field.shape
    return lax.all_to_all(field.reshape(cols, h // cols, w, c), "col", 0, 0, tiled=True)


def turn(field, cols, after):
    h, w, c = field.shape
    blocks = field.reshape(cols, h // cols, w, c)
    me = lax.axis_index("col")
    parts = [lax.dynamic_index_in_dim(blocks, (me + k) % cols, 0, keepdims=False) for k in range(cols)]
    parts = tied(*parts, after)[:-1]
    moves = [[(i, (i + k) % cols) for i in range(cols)] for k in range(cols)]
    return [lax.ppermute(part, "col", move) if k else part for k, (part, move) in enumerate(zip(parts, moves))]


def core_swap(x):
    return lax.ppermute(x, "row", [(i, i ^ 1) for i in range(lax.axis_size("row"))])


def core_exchange(x, count):
    pairs = lax.axis_size("row")
    cols = count // pairs
    groups = [[cols * r + c for r in range(k, pairs, 2) for c in range(cols)] for k in range(2)]
    x = x.reshape(count // 2, -1, x.shape[-1])
    return lax.all_to_all(x, AXES, 0, 0, axis_index_groups=groups, tiled=True)


def edges(field, count):
    down = lax.ppermute(field[-1:], AXES, [(i, i + 1) for i in range(count - 1)])
    up = lax.ppermute(field[:1], AXES, [(i + 1, i) for i in range(count - 1)])
    return down, up


def scatter_sum(x, count):
    x = lax.all_to_all(x.reshape(count, -1, x.shape[-1]), AXES, 0, 0, tiled=True)
    return x.astype(F32).sum(0).astype(BF)


def gather(x, count):
    x = lax.all_to_all(jnp.broadcast_to(x[None], (count,) + x.shape), AXES, 0, 0, tiled=True)
    return x.reshape(-1, x.shape[-1])


def tie(value, *after):
    return lax.optimization_barrier((value,) + after)[0]


def tied(*values):
    return lax.optimization_barrier(values)


def shards(features, hole_mask, cotangent, w_local, w_cross, w_in, w_freq, w_out):
    cols = lax.axis_size("col")
    count = lax.axis_size("row") * cols
    me = lax.axis_index(AXES)
    _, h, w, ch = features.shape
    rows, width = h // cols, w * cols
    height = rows * count
    cl, cg, cs = w_local.shape[3], w_cross.shape[3], w_in.shape[1]
    lines = -(-(width // 2 + 1) // count)
    slots = -(-(rows * lines) // 16) * 16
    n = count * slots
    sizes = (rows, lines, count, slots)
    tc, ts = line_tables(width, count, lines)
    tct, tst = jnp.asarray(tc.T), jnp.asarray(ts.T)
    tc, ts = jnp.asarray(tc), jnp.asarray(ts)
    hc, hs = (jnp.asarray(t) for t in column_tables(rows, count))
    norm_w, norm_h = 1.0 / math.sqrt(width), 1.0 / math.sqrt(height)
    freq = lines * me + jnp.arange(lines)
    weight = jnp.where((freq == 0) | (freq * 2 == width), 0.5, jnp.where(freq * 2 < width, 1.0, 0.0))
    weight = weight.astype(F32)[None]
    sign = np.where((np.arange(384) < 192), 1.0, -1.0).astype(np.float32)
    sign = jnp.asarray(sign[None])

    w_in_d = jnp.concatenate([w_in, w_in[:, 128:]], 1)
    w_in_t = jnp.pad(w_in.T, ((0, 64), (0, 0)))
    w_out_z = jnp.pad(w_out, ((0, 64), (0, 0)))
    w_out_t = jnp.concatenate([w_out, w_out[128:]], 0).T
    w_freq_p = pack_dim(pack_dim(w_freq, 0, cs), 1, cs)
    w_freq_t = w_freq_p.T
    wl = jnp.transpose(w_local, (0, 2, 1, 3)).reshape(3, ch, 3 * cl)
    wc = jnp.transpose(w_cross, (0, 2, 1, 3)).reshape(3 * cl, 3 * cg)
    wl_t = jnp.transpose(w_local, (0, 1, 3, 2)).reshape(3, 3 * cl, ch)
    wc_t = jnp.transpose(w_cross, (0, 1, 3, 2)).reshape(3, 3 * cg, cl)

    at_y = lambda y: (y, 0, 0)
    one_row = lambda c: (1, width, c)
    blocks = lambda c: (cols, 1, w, c)
    at_blocks = lambda y: (0, y, 0, 0)
    wide = (rows, width, ch)
    pix = rows * width
    vm = pltpu.VMEM
    lined = (rows, lines * count, 384)
    spectral = (lines, height, 384)
    used = rows * lines * count

    marked = jnp.where(hole_mask[0][..., None] == 1, HOLE, features[0]).astype(BF)
    marked = to_rows(marked, cols)
    w_in_d, w_in_t, w_out_z, w_out_t, w_freq_p, w_freq_t, wl, wc, wl_t, wc_t, weight = tied(
        w_in_d, w_in_t, w_out_z, w_out_t, w_freq_p, w_freq_t, wl, wc, wl_t, wc_t, weight
    )
    cots = turn(cotangent[0], cols, marked)
    my_col = lax.axis_index("col").astype(jnp.int32).reshape(1, 1)

    masked, unit, sent = call(
        functools.partial(head_kernel, norm_w, sizes, cl),
        "head",
        (rows,),
        [(marked, blocks(ch), at_blocks), (w_in_d, None, None), (tc, None, None), (ts, None, None)],
        [(wide, BF, one_row(ch), at_y), ((rows, width, 256), BF, one_row(256), at_y), ((n, 384), BF, None, None)],
        [vm(lined, F32), vm((3, n, 128), F32)],
        flops=1 << 30, bytes_=6 << 20,
    )
    near = [k for k in range(cols) if k in (0, 1, cols - 1)]
    sent, *moved = tied(sent, *[cots[k] for k in near])
    for k, c in zip(near, moved):
        cots[k] = c
    above, below = edges(masked, count)
    got = swap(sent, count)
    stacked, sent = call(
        functools.partial(frequency_kernel, norm_h, sizes),
        "frequency",
        (1,),
        [(got, None, None), (hc, None, None), (hs, None, None), (w_freq_p, None, None), (weight, None, None), (sign, None, None)],
        [(spectral, BF, None, None), ((n, 384), BF, None, None)],
        [vm((3, n, 128), F32), vm(spectral, F32)],
        flops=3 << 30, bytes_=7 << 20,
    )
    sent, above, below, *cots = tied(sent, above, below, *cots)
    got = swap(sent, count)
    (pre,) = call(
        functools.partial(conv_kernel, cl),
        "conv",
        (rows,),
        [(above, None, None), (masked, None, None), (below, None, None), (wl, None, None), (wc, None, None)],
        [(wide, F32, one_row(ch), at_y)],
        [vm((rows + 2, width, ch), BF)],
        flops=18 * pix * (ch * cl + cl * cg), bytes_=9 << 20,
    )
    output, d_out, d_joined, sent, joined = call(
        functools.partial(middle_kernel, norm_w, sizes, cl, cols),
        "middle",
        (rows,),
        [
            (got, None, None), (tct, None, None), (tst, None, None), (tc, None, None),
            (ts, None, None), (unit, one_row(256), at_y), (pre, one_row(ch), at_y),
            (w_out_z, None, None), (w_out_t, None, None), (my_col, None, None),
        ]
        + [(c, (1, w, ch), at_y) for c in cots],
        [
            (wide, BF, one_row(ch), at_y), (wide, BF, one_row(ch), at_y), ((rows, width, 256), BF, one_row(256), at_y),
            ((n, 384), BF, None, None), ((rows, width, 256), BF, one_row(256), at_y),
        ],
        [vm((used, 384), BF), vm((used, 256), BF), vm((width, ch), BF), vm(lined, F32), vm((3, n, 128), F32)],
        flops=3 << 30, bytes_=12 << 20,
    )
    got = swap(sent, count)
    d_above, d_below = edges(d_out, count)
    my_core = (lax.axis_index("row") % 2).astype(jnp.int32).reshape(1, 1)
    mine, other = call(
        functools.partial(conv_grad_kernel, cl),
        "conv_grad",
        (rows,),
        [(above, None, None), (masked, None, None), (below, None, None), (d_out, one_row(ch), at_y), (joined, one_row(256), at_y), (my_core, None, None)],
        [((3 * ch, 384), BF, None, None), ((3 * ch, 384), BF, None, None)],
        [vm((rows + 2, width, ch), BF), vm((3, ch, 3 * cl), F32), vm((3, cl, 3 * cg), F32), vm((256, cg), F32)],
        flops=18 * pix * (ch * cl + cl * cg), bytes_=7 << 20,
    )
    got, other = tied(got, other)
    got, total = tied(got, (mine.astype(F32) + core_swap(other).astype(F32)).astype(BF))
    early = core_exchange(total, count)
    sent, grad_freq = call(
        functools.partial(frequency_back_kernel, norm_h, sizes),
        "frequency_back",
        (1,),
        [
            (got, None, None), (hc, None, None), (hs, None, None), (w_freq_p, None, None), (w_freq_t, None, None),
            (weight, None, None), (sign, None, None), (stacked, None, None),
        ],
        [((n, 384), BF, None, None), ((384, 384), BF, None, None)],
        [vm((3, n, 128), F32), vm(spectral, F32), vm((256, 384), F32), vm((256, 384), F32)],
        flops=3 << 30, bytes_=8 << 20,
    )
    sent, early, d_above, d_below = tied(sent, early, d_above, d_below)
    got = swap(sent, count)
    (d_conv,) = call(
        functools.partial(conv_back_kernel, cl),
        "conv_back",
        (rows,),
        [(d_above, None, None), (d_out, None, None), (d_below, None, None), (wl_t, None, None), (wc_t, None, None)],
        [(wide, F32, one_row(ch), at_y)],
        [vm((rows + 2, width, 3 * cl), BF), vm((rows + 2, width, 3 * cg), BF)],
        flops=18 * pix * (ch * cl + cl * cg), bytes_=9 << 20,
    )
    early = jnp.tile(early.astype(F32).sum(0).astype(BF), (count // 2, 1))
    got, d_conv, early = tied(got, d_conv, early)
    early = core_exchange(early, count).reshape(-1, 384)
    late_rows = -(-(3 * 384 + 3 * cs) // (16 * count)) * 16 * count
    d_unit, late = call(
        functools.partial(tail_kernel, norm_w, sizes, cl),
        "tail",
        (rows,),
        [
            (got, None, None), (tct, None, None), (tst, None, None), (masked, one_row(ch), at_y),
            (d_joined, one_row(256), at_y), (w_in_d, None, None), (grad_freq, None, None),
        ],
        [((rows, width, 256), BF, one_row(256), at_y), ((late_rows, 128), BF, None, None)],
        [vm((used, 384), BF), vm((used, 256), BF), vm((3, n, 128), F32), vm((256, cg), F32)],
        flops=1 << 30, bytes_=5 << 20,
    )
    late, early = tied(late, early)
    other = core_swap(early)
    late = scatter_sum(late, count)
    (grad_features,) = call(
        functools.partial(finish_kernel, cl),
        "finish",
        (rows,),
        [
            (marked, blocks(128), at_blocks), (d_unit, one_row(256), at_y), (d_conv, one_row(ch), at_y),
            (w_in_t, None, None),
        ],
        [(wide, BF, one_row(ch), at_y)],
        flops=2 * pix * 256 * cg, bytes_=7 << 20,
    )
    late, grad_features = tied(late, grad_features)
    grad_local, grad_cross, grad_out = call(
        functools.partial(unpack_kernel, cl),
        "unpack",
        (1,),
        [(early, None, None), (other, None, None), (my_core, None, None)],
        [((3, 3, ch, cl), F32, None, None), ((9 * cl, cg), F32, None, None), ((cs, cg), F32, None, None)],
        flops=1, bytes_=7 << 20,
    )
    late = gather(late, count)
    late, grad_local, grad_cross, grad_out = tied(late, grad_local, grad_cross, grad_out)
    grad_freq = jnp.concatenate([late[k * 384 : (k + 1) * 384] for k in range(3)], 1).astype(F32)
    at = 3 * 384
    grad_in = jnp.concatenate([late[at + k * cs : at + (k + 1) * cs] for k in range(3)], 1).astype(F32).T
    grad_cross = grad_cross.reshape(3, 3, cl, cg)
    return output[None], grad_features[None], grad_local, grad_cross, grad_in, grad_freq, grad_out


def solution(mesh):
    return jax.shard_map(
        shards,
        mesh=mesh,
        in_specs=(
            P("dp", "row", "col", None),
            P("dp", "row", "col"),
            P("dp", "row", "col", None),
            P(),
            P(),
            P(),
            P(),
            P(),
        ),
        out_specs=(
            P("dp", ("row", "col"), None, None),
            P("dp", ("row", "col"), None, None),
            P("dp", None, None, None),
            P("dp", None, None, None),
            P("dp", None),
            P("dp", None),
            P("dp", None),
        ),
        check_vma=False,
    )
```

```python
import functools
import math

import jax
import jax.numpy as jnp
import numpy as np
from jax import lax
from jax.experimental import pallas as pl
from jax.experimental.pallas import tpu as pltpu
from jax.sharding import PartitionSpec as P

AXES = ("row", "col")
HOLE = 64.0
BF = jnp.bfloat16
F32 = jnp.float32
ROWS_OF = ((0,), (0,))


def dot(a, b, dims=((1,), (0,))):
    return lax.dot_general(a, b, (dims, ((), ())), preferred_element_type=F32)


def line_tables(width, count, lines):
    freq = (lines * np.arange(count)[None] + np.arange(lines)[:, None]).reshape(-1, 1)
    angle = 2.0 * np.pi * (freq * np.arange(width) % width) / width
    valid = freq <= width // 2
    return (np.cos(angle) * valid).astype(BF), (np.sin(angle) * valid).astype(BF)


def column_tables(rows, count):
    h = (rows * np.arange(count)[None] + np.arange(rows)[:, None]).reshape(-1)
    angle = 2.0 * np.pi * (h[:, None] * h[None] % (rows * count)) / (rows * count)
    return np.cos(angle).astype(BF), np.sin(angle).astype(BF)


def slope_and_silu(value):
    sigma = 0.5 + 0.5 * jnp.tanh(0.5 * value)
    return sigma * (1.0 + value * (1.0 - sigma)), value * sigma


def lanes_below(shape, bound):
    return lax.broadcasted_iota(jnp.int32, shape, 1) < bound


def packed(re, im):
    mid = jnp.where(lanes_below(re[:, 128:].shape, 64), re[:, 128:], im[:, 128:])
    return jnp.concatenate([re[:, :128], mid, im[:, :128]], 1)


def turned(p, q, sign):
    mid = pltpu.roll(q[:, 128:256], 64, 1)
    flip = jnp.where(lanes_below(mid.shape, 64), sign, -sign)
    return jnp.concatenate(
        [p[:, :128] + sign * q[:, 256:], p[:, 128:256] + flip * mid, p[:, 256:] - sign * q[:, :128]], 1
    )


def natural_lanes(x):
    mid, im = x[:, 128:256], pltpu.roll(x[:, 256:], 64, 1)
    low = lanes_below(mid.shape, 64)
    return jnp.concatenate([x[:, :128], jnp.where(low, mid, im), jnp.where(low, im, mid)], 1)


def pack_order(cs):
    return [(0, 128), (128, cs), (cs + 128, 2 * cs), (cs, cs + 128)]


def pack_dim(x, dim, cs):
    return jnp.concatenate([lax.slice_in_dim(x, a, b, axis=dim) for a, b in pack_order(cs)], dim)


def call(body, name, grid, ins, outs, scratch=(), flops=0, bytes_=0):
    def spec(shape, block, index):
        if shape[0] == 1 and shape[-1] < 8:
            return pl.BlockSpec(memory_space=pltpu.SMEM)
        if block is None:
            zeros = (0,) * len(shape)
            return pl.BlockSpec(shape, lambda *_: zeros)
        return pl.BlockSpec(block, index)

    return pl.pallas_call(
        body,
        grid=grid,
        in_specs=[spec(a.shape, block, index) for a, block, index in ins],
        out_specs=[spec(shape, block, index) for shape, _, block, index in outs],
        out_shape=[jax.ShapeDtypeStruct(shape, dtype) for shape, dtype, _, _ in outs],
        scratch_shapes=list(scratch),
        compiler_params=pltpu.CompilerParams(vmem_limit_bytes=56 << 20),
        cost_estimate=pl.CostEstimate(flops=flops, bytes_accessed=bytes_, transcendentals=0),
        name=name,
    )(*[a for a, _, _ in ins])


def put_slots(sizes, z, value_of, sent):
    rows, lines, count, slots = sizes
    for q in range(slots):
        value = value_of(q // lines, q % lines) if q < rows * lines else jnp.zeros((count, 384), F32)
        for k in range(3):
            z[k, pl.ds(q, count, stride=slots), :] = value[:, k * 128 : (k + 1) * 128]
    for k in range(3):
        sent[:, k * 128 : (k + 1) * 128] = z[k].astype(BF)


def spread(got, z):
    for k in range(3):
        z[k] = got[:, k * 128 : (k + 1) * 128].astype(F32)


def slot(sizes, z, q):
    _, _, count, slots = sizes
    return jnp.concatenate([z[k, pl.ds(q, count, stride=slots), :] for k in range(3)], 1)


def take_slots(sizes, got, z, x):
    rows, lines, count, slots = sizes
    spread(got, z)
    for q in range(rows * lines):
        x[q * count : (q + 1) * count, :] = slot(sizes, z, q).astype(BF)


def head_kernel(norm, sizes, cl, marked, w_in, tc, ts, masked, unit, sent, v, z):
    y = pl.program_id(0)
    x = marked[...].reshape(-1, marked.shape[-1])
    keep = x[:, :1].astype(F32) < 0.5 * HOLE
    x = jnp.where(keep, x, jnp.zeros_like(x))
    masked[0] = x
    u = slope_and_silu(dot(x[:, cl:], w_in[...]))[1].astype(BF)
    unit[0] = u
    transform_out(y, norm, sizes, u, tc, ts, sent, v, z)


def transform_out(y, norm, sizes, u, tc, ts, sent, v, z):
    count = sizes[2]
    v[y] = packed(dot(tc[...], u) * norm, dot(ts[...], u) * -norm)

    @pl.when(y == pl.num_programs(0) - 1)
    def _():
        put_slots(sizes, z, lambda row, j: v[row, j * count : (j + 1) * count, :], sent)


def column_line(sizes, z, j):
    rows, lines, count, slots = sizes
    parts = [slot(sizes, z, row * lines + j) for row in range(rows)]
    return jnp.concatenate(parts, 0).astype(BF)


def frequency_kernel(norm, sizes, got, hc, hs, w_freq, weight, sign, stacked, sent, z, v):
    count = sizes[2]
    spread(got, z)
    for j in range(sizes[1]):
        x = column_line(sizes, z, j)
        st = (turned(dot(hc[...], x), dot(hs[...], x), 1.0) * norm).astype(BF)
        stacked[j] = st
        pos = slope_and_silu(dot(st, w_freq[...]))[1]
        neg = slope_and_silu(dot((st.astype(F32) * sign[...]).astype(BF), w_freq[...]))[1]
        x = (weight[0, j] * (pos + sign[...] * neg)).astype(BF)
        v[j] = turned(dot(hc[...], x), dot(hs[...], x), -1.0) * norm
    put_slots(sizes, z, lambda row, j: v[j, row * count : (row + 1) * count, :], sent)


def frequency_back_kernel(
    norm, sizes, got, hc, hs, w_freq, w_freq_t, weight, sign, stacked, sent, grad, z, v, acc_p, acc_m
):
    count = sizes[2]
    spread(got, z)
    for j in range(sizes[1]):
        x = column_line(sizes, z, j)
        dz = turned(dot(hc[...], x), dot(hs[...], x), 1.0) * norm
        st = stacked[j]
        pos = slope_and_silu(dot(st, w_freq[...]))[0]
        neg = slope_and_silu(dot((st.astype(F32) * sign[...]).astype(BF), w_freq[...]))[0]
        pos = (dz * pos).astype(BF).astype(F32)
        neg = (dz * sign[...] * neg).astype(BF).astype(F32)
        total = (weight[0, j] * (pos + neg)).astype(BF)
        delta = (weight[0, j] * (pos - neg)).astype(BF)
        g_p = dot(st[:, :256], total, ROWS_OF)
        g_m = dot(st[:, 128:], delta, ROWS_OF)
        acc_p[...] = g_p if j == 0 else acc_p[...] + g_p
        acc_m[...] = g_m if j == 0 else acc_m[...] + g_m
        re = dot(total, w_freq_t[:, :256])
        im = dot(delta, w_freq_t[:, 128:])
        mid = jnp.where(lanes_below((re.shape[0], 128), 64), re[:, 128:], im[:, :128])
        x = jnp.concatenate([re[:, :128], mid, im[:, 128:]], 1).astype(BF)
        v[j] = turned(dot(hc[...], x), dot(hs[...], x), -1.0) * norm
    put_slots(sizes, z, lambda row, j: v[j, row * count : (row + 1) * count, :], sent)
    grad[0:192, :] = natural_lanes(acc_p[0:192, :]).astype(BF)
    grad[192:320, :] = natural_lanes(acc_m[128:256, :]).astype(BF)
    grad[320:384, :] = natural_lanes(acc_m[64:128, :]).astype(BF)


def imag_first(got):
    mid = pltpu.roll(got[:, 128:256].astype(F32), 64, 1).astype(BF)
    return jnp.concatenate([got[:, 256:], mid], 1)


def line_back(y, norm, sizes, got, tct, tst, z, got_x, got_s):
    @pl.when(y == 0)
    def _():
        take_slots(sizes, got, z, got_x)
        got_s[...] = imag_first(got_x[...])

    size = sizes[1] * sizes[2]
    at = pl.ds(pl.multiple_of(y * size, size), size)
    return ((dot(tct[...], got_x[at, :256]) - dot(tst[...], got_s[at, :])) * norm).astype(BF)


def middle_kernel(
    norm, sizes, cl, cols, got, tct, tst, tc, ts, unit, pre, w_out, w_out_t, my_col, *refs,
):
    cots = refs[:cols]
    output, d_out, d_joined, sent, grad, got_x, got_s, cot, v, z, acc_g = refs[cols:]
    y = pl.program_id(0)
    w = cots[0].shape[1]
    for k in range(cols):
        at = lax.rem(my_col[0, 0] + (cols - k), cols)
        cot[pl.ds(pl.multiple_of(at * w, w), w), :] = cots[k][0]

    back = line_back(y, norm, sizes, got, tct, tst, z, got_x, got_s)
    joined = (unit[0].astype(F32) + back.astype(F32)).astype(BF)
    pre_all = jnp.concatenate([pre[0, :, :cl], pre[0, :, cl:] + dot(joined, w_out[...])], 1)
    slope, silu = slope_and_silu(pre_all)
    output[0] = silu.astype(BF)
    d = (cot[...].astype(F32) * slope).astype(BF)
    d_out[0] = d
    dj = dot(d[:, cl:], w_out_t[...]).astype(BF)
    d_joined[0] = dj
    g = dot(joined, d[:, cl:], ROWS_OF)

    @pl.when(y == 0)
    def _():
        acc_g[...] = g

    @pl.when(y > 0)
    def _():
        acc_g[...] += g

    transform_out(y, norm, sizes, dj, tc, ts, sent, v, z)

    @pl.when(y == pl.num_programs(0) - 1)
    def _():
        grad[...] = acc_g[0 : grad.shape[0], :].astype(BF)


def tail_kernel(
    norm, sizes, cl, got, tct, tst, masked, d_joined, w_in, grad_freq, d_unit, late, got_x, got_s, z, acc_g
):
    y = pl.program_id(0)

    back = line_back(y, norm, sizes, got, tct, tst, z, got_x, got_s)
    x = masked[0, :, cl:]
    slope = slope_and_silu(dot(x, w_in[...]))[0]
    du = ((d_joined[0].astype(F32) + back.astype(F32)) * slope).astype(BF)
    g = dot(du, x, ROWS_OF)

    @pl.when(y == 0)
    def _():
        acc_g[...] = g

    @pl.when(y > 0)
    def _():
        acc_g[...] += g

    d_unit[0] = du

    @pl.when(y == pl.num_programs(0) - 1)
    def _():
        at = 0
        for part, size in ((grad_freq, 384), (acc_g, 192)):
            for k in range(3):
                late[at : at + size, :] = part[0:size, k * 128 : (k + 1) * 128].astype(BF)
                at += size
        late[at:, :] = jnp.zeros((late.shape[0] - at, 128), BF)


def finish_kernel(cl, marked, d_unit, d_conv, w_in_t, grad_features):
    keep = marked[...].reshape(-1, marked.shape[-1])[:, :1].astype(F32) < 0.5 * HOLE
    total = jnp.concatenate([d_conv[0, :, :cl], d_conv[0, :, cl:] + dot(d_unit[0], w_in_t[...])], 1)
    grad_features[0] = jnp.where(keep, total, 0.0).astype(BF)


def shifted(x, step):
    n = x.shape[0]
    at = lax.broadcasted_iota(jnp.int32, x.shape, 0)
    if step == 1:
        return jnp.where(at == 0, 0.0, pltpu.roll(x, 1, 0))
    return jnp.where(at == n - 1, 0.0, pltpu.roll(x, n - 1, 0))


def three(x):
    f = x.astype(F32)
    return jnp.concatenate([shifted(f, -1).astype(BF), x, shifted(f, 1).astype(BF)], 1)


def conv_kernel(cl, above, masked, below, w_local, w_cross, pre, pad):
    y = pl.program_id(0)
    rows = masked.shape[0]

    @pl.when(y == 0)
    def _():
        pad[0] = above[0]
        pad[1 : rows + 1] = masked[...]
        pad[rows + 1] = below[0]

    local = dot(pad[y], w_local[0]) + dot(pad[y + 1], w_local[1]) + dot(pad[y + 2], w_local[2])
    near = jnp.concatenate([pad[y, :, :cl], pad[y + 1, :, :cl], pad[y + 2, :, :cl]], 1)
    cross = dot(near, w_cross[...])
    c, g = cl, w_cross.shape[1] // 3
    pre[0, :, :cl] = shifted(local[:, :c], 1) + local[:, c : 2 * c] + shifted(local[:, 2 * c :], -1)
    pre[0, :, cl:] = shifted(cross[:, :g], 1) + cross[:, g : 2 * g] + shifted(cross[:, 2 * g :], -1)


def conv_grad_kernel(cl, above, masked, below, d_out, g_out, core, mine, other, pad, acc_l, acc_c):
    y = pl.program_id(0)
    rows = masked.shape[0]

    @pl.when(y == 0)
    def _():
        pad[0] = above[0]
        pad[1 : rows + 1] = masked[...]
        pad[rows + 1] = below[0]
        acc_l[...] = jnp.zeros_like(acc_l)
        acc_c[...] = jnp.zeros_like(acc_c)

    d_local = three(d_out[0, :, :cl])
    d_global = three(d_out[0, :, cl:])
    g = d_global.shape[1] // 3
    for i in range(3):
        x = pad[y + i]
        acc_l[i] += dot(x, d_local, ROWS_OF)
        acc_c[i] += dot(x[:, :cl], d_global, ROWS_OF)

    def write(local, rest):
        ch = masked.shape[2]
        for i in range(3):
            local[i * ch : (i + 1) * ch, :] = acc_l[i].astype(BF)
            for j in range(3):
                at = (3 * i + j) * cl
                rest[at : at + cl, :] = acc_c[i, :, j * g : (j + 1) * g].astype(BF)
        at, size = 9 * cl, g_out.shape[0]
        rest[at : at + size, :] = g_out[...]
        rest[at + size :, :] = jnp.zeros((rest.shape[0] - at - size, g), BF)

    last = y == pl.num_programs(0) - 1

    @pl.when(last & (core[0, 0] == 0))
    def _():
        write(mine, other)

    @pl.when(last & (core[0, 0] == 1))
    def _():
        write(other, mine)


def unpack_kernel(cl, mine, other, core, g_local, g_cross, g_out):
    ch = g_local.shape[2]

    def write(local, rest):
        for at in range(0, 3 * ch, 64):
            block = local[at : at + 64, :].astype(F32)
            for j in range(3):
                g_local[at // ch, j, at % ch : at % ch + 64, :] = block[:, j * cl : (j + 1) * cl]
        g_cross[...] = rest[0 : 9 * cl, :].astype(F32)
        g_out[...] = rest[9 * cl : 9 * cl + g_out.shape[0], :].astype(F32)

    @pl.when(core[0, 0] == 0)
    def _():
        write(mine, other)

    @pl.when(core[0, 0] == 1)
    def _():
        write(other, mine)


def conv_back_kernel(cl, above, d_out, below, w_local, w_cross, d_conv, pad_l, pad_g):
    y = pl.program_id(0)
    rows = d_out.shape[0]

    @pl.when(y == 0)
    def _():
        for k in range(rows + 2):
            line = above[0] if k == 0 else below[0] if k == rows + 1 else d_out[k - 1]
            pad_l[k] = three(line[:, :cl])
            pad_g[k] = three(line[:, cl:])

    total = dot(pad_l[y + 2], w_local[0]) + dot(pad_l[y + 1], w_local[1]) + dot(pad_l[y], w_local[2])
    cross = dot(pad_g[y + 2], w_cross[0]) + dot(pad_g[y + 1], w_cross[1]) + dot(pad_g[y], w_cross[2])
    d_conv[0, :, :cl] = total[:, :cl] + cross
    d_conv[0, :, cl:] = total[:, cl:]


def swap(x, count):
    return lax.all_to_all(x.reshape(count, -1, x.shape[-1]), AXES, 0, 0, tiled=True).reshape(x.shape)


def to_rows(field, cols):
    h, w, c = field.shape
    return lax.all_to_all(field.reshape(cols, h // cols, w, c), "col", 0, 0, tiled=True)


def turn(field, cols, after):
    h, w, c = field.shape
    blocks = field.reshape(cols, h // cols, w, c)
    me = lax.axis_index("col")
    parts = [lax.dynamic_index_in_dim(blocks, (me + k) % cols, 0, keepdims=False) for k in range(cols)]
    parts = tied(*parts, after)[:-1]
    moves = [[(i, (i + k) % cols) for i in range(cols)] for k in range(cols)]
    return [lax.ppermute(part, "col", move) if k else part for k, (part, move) in enumerate(zip(parts, moves))]


def core_swap(x):
    return lax.ppermute(x, "row", [(i, i ^ 1) for i in range(lax.axis_size("row"))])


def core_exchange(x, count):
    pairs = lax.axis_size("row")
    cols = count // pairs
    groups = [[cols * r + c for r in range(k, pairs, 2) for c in range(cols)] for k in range(2)]
    x = x.reshape(count // 2, -1, x.shape[-1])
    return lax.all_to_all(x, AXES, 0, 0, axis_index_groups=groups, tiled=True)


def edges(field, count):
    down = lax.ppermute(field[-1:], AXES, [(i, i + 1) for i in range(count - 1)])
    up = lax.ppermute(field[:1], AXES, [(i + 1, i) for i in range(count - 1)])
    return down, up


def scatter_sum(x, count):
    x = lax.all_to_all(x.reshape(count, -1, x.shape[-1]), AXES, 0, 0, tiled=True)
    return x.astype(F32).sum(0).astype(BF)


def gather(x, count):
    x = lax.all_to_all(jnp.broadcast_to(x[None], (count,) + x.shape), AXES, 0, 0, tiled=True)
    return x.reshape(-1, x.shape[-1])


def tie(value, *after):
    return lax.optimization_barrier((value,) + after)[0]


def tied(*values):
    return lax.optimization_barrier(values)


def shards(features, hole_mask, cotangent, w_local, w_cross, w_in, w_freq, w_out):
    cols = lax.axis_size("col")
    count = lax.axis_size("row") * cols
    me = lax.axis_index(AXES)
    _, h, w, ch = features.shape
    rows, width = h // cols, w * cols
    height = rows * count
    cl, cg, cs = w_local.shape[3], w_cross.shape[3], w_in.shape[1]
    lines = -(-(width // 2 + 1) // count)
    slots = -(-(rows * lines) // 16) * 16
    n = count * slots
    sizes = (rows, lines, count, slots)
    tc, ts = line_tables(width, count, lines)
    tct, tst = jnp.asarray(tc.T), jnp.asarray(ts.T)
    tc, ts = jnp.asarray(tc), jnp.asarray(ts)
    hc, hs = (jnp.asarray(t) for t in column_tables(rows, count))
    norm_w, norm_h = 1.0 / math.sqrt(width), 1.0 / math.sqrt(height)
    freq = lines * me + jnp.arange(lines)
    weight = jnp.where((freq == 0) | (freq * 2 == width), 0.5, jnp.where(freq * 2 < width, 1.0, 0.0))
    weight = weight.astype(F32)[None]
    sign = np.where((np.arange(384) < 192), 1.0, -1.0).astype(np.float32)
    sign = jnp.asarray(sign[None])

    w_in_d = jnp.concatenate([w_in, w_in[:, 128:]], 1)
    w_in_t = jnp.pad(w_in.T, ((0, 64), (0, 0)))
    w_out_z = jnp.pad(w_out, ((0, 64), (0, 0)))
    w_out_t = jnp.concatenate([w_out, w_out[128:]], 0).T
    w_freq_p = pack_dim(pack_dim(w_freq, 0, cs), 1, cs)
    w_freq_t = w_freq_p.T
    wl = jnp.transpose(w_local, (0, 2, 1, 3)).reshape(3, ch, 3 * cl)
    wc = jnp.transpose(w_cross, (0, 2, 1, 3)).reshape(3 * cl, 3 * cg)
    wl_t = jnp.transpose(w_local, (0, 1, 3, 2)).reshape(3, 3 * cl, ch)
    wc_t = jnp.transpose(w_cross, (0, 1, 3, 2)).reshape(3, 3 * cg, cl)

    at_y = lambda y: (y, 0, 0)
    one_row = lambda c: (1, width, c)
    blocks = lambda c: (cols, 1, w, c)
    at_blocks = lambda y: (0, y, 0, 0)
    wide = (rows, width, ch)
    pix = rows * width
    vm = pltpu.VMEM
    lined = (rows, lines * count, 384)
    spectral = (lines, height, 384)
    used = rows * lines * count

    marked = jnp.where(hole_mask[0][..., None] == 1, HOLE, features[0]).astype(BF)
    marked = to_rows(marked, cols)
    w_in_d, w_in_t, w_out_z, w_out_t, w_freq_p, w_freq_t, wl, wc, wl_t, wc_t, weight = tied(
        w_in_d, w_in_t, w_out_z, w_out_t, w_freq_p, w_freq_t, wl, wc, wl_t, wc_t, weight
    )
    cots = turn(cotangent[0], cols, marked)
    my_col = lax.axis_index("col").astype(jnp.int32).reshape(1, 1)

    masked, unit, sent = call(
        functools.partial(head_kernel, norm_w, sizes, cl),
        "head",
        (rows,),
        [(marked, blocks(ch), at_blocks), (w_in_d, None, None), (tc, None, None), (ts, None, None)],
        [(wide, BF, one_row(ch), at_y), ((rows, width, 256), BF, one_row(256), at_y), ((n, 384), BF, None, None)],
        [vm(lined, F32), vm((3, n, 128), F32)],
        flops=1 << 30, bytes_=6 << 20,
    )
    near = [k for k in range(cols) if k in (0, 1, cols - 1)]
    sent, *moved = tied(sent, *[cots[k] for k in near])
    for k, c in zip(near, moved):
        cots[k] = c
    above, below = edges(masked, count)
    got = swap(sent, count)
    stacked, sent = call(
        functools.partial(frequency_kernel, norm_h, sizes),
        "frequency",
        (1,),
        [(got, None, None), (hc, None, None), (hs, None, None), (w_freq_p, None, None), (weight, None, None), (sign, None, None)],
        [(spectral, BF, None, None), ((n, 384), BF, None, None)],
        [vm((3, n, 128), F32), vm(spectral, F32)],
        flops=3 << 30, bytes_=7 << 20,
    )
    sent, above, below, *cots = tied(sent, above, below, *cots)
    got = swap(sent, count)
    (pre,) = call(
        functools.partial(conv_kernel, cl),
        "conv",
        (rows,),
        [(above, None, None), (masked, None, None), (below, None, None), (wl, None, None), (wc, None, None)],
        [(wide, F32, one_row(ch), at_y)],
        [vm((rows + 2, width, ch), BF)],
        flops=18 * pix * (ch * cl + cl * cg), bytes_=9 << 20,
    )
    output, d_out, d_joined, sent, grad_out = call(
        functools.partial(middle_kernel, norm_w, sizes, cl, cols),
        "middle",
        (rows,),
        [
            (got, None, None), (tct, None, None), (tst, None, None), (tc, None, None),
            (ts, None, None), (unit, one_row(256), at_y), (pre, one_row(ch), at_y),
            (w_out_z, None, None), (w_out_t, None, None), (my_col, None, None),
        ]
        + [(c, (1, w, ch), at_y) for c in cots],
        [
            (wide, BF, one_row(ch), at_y), (wide, BF, one_row(ch), at_y), ((rows, width, 256), BF, one_row(256), at_y),
            ((n, 384), BF, None, None), ((cs, cg), BF, None, None),
        ],
        [vm((used, 384), BF), vm((used, 256), BF), vm((width, ch), BF), vm(lined, F32), vm((3, n, 128), F32), vm((256, cg), F32)],
        flops=3 << 30, bytes_=12 << 20,
    )
    got = swap(sent, count)
    d_above, d_below = edges(d_out, count)
    my_core = (lax.axis_index("row") % 2).astype(jnp.int32).reshape(1, 1)
    mine, other = call(
        functools.partial(conv_grad_kernel, cl),
        "conv_grad",
        (rows,),
        [(above, None, None), (masked, None, None), (below, None, None), (d_out, one_row(ch), at_y), (grad_out, None, None), (my_core, None, None)],
        [((3 * ch, 384), BF, None, None), ((3 * ch, 384), BF, None, None)],
        [vm((rows + 2, width, ch), BF), vm((3, ch, 3 * cl), F32), vm((3, cl, 3 * cg), F32)],
        flops=18 * pix * (ch * cl + cl * cg), bytes_=7 << 20,
    )
    got, other = tied(got, other)
    got, total = tied(got, (mine.astype(F32) + core_swap(other).astype(F32)).astype(BF))
    early = core_exchange(total, count)
    sent, grad_freq = call(
        functools.partial(frequency_back_kernel, norm_h, sizes),
        "frequency_back",
        (1,),
        [
            (got, None, None), (hc, None, None), (hs, None, None), (w_freq_p, None, None), (w_freq_t, None, None),
            (weight, None, None), (sign, None, None), (stacked, None, None),
        ],
        [((n, 384), BF, None, None), ((384, 384), BF, None, None)],
        [vm((3, n, 128), F32), vm(spectral, F32), vm((256, 384), F32), vm((256, 384), F32)],
        flops=3 << 30, bytes_=8 << 20,
    )
    sent, early, d_above, d_below = tied(sent, early, d_above, d_below)
    got = swap(sent, count)
    (d_conv,) = call(
        functools.partial(conv_back_kernel, cl),
        "conv_back",
        (rows,),
        [(d_above, None, None), (d_out, None, None), (d_below, None, None), (wl_t, None, None), (wc_t, None, None)],
        [(wide, F32, one_row(ch), at_y)],
        [vm((rows + 2, width, 3 * cl), BF), vm((rows + 2, width, 3 * cg), BF)],
        flops=18 * pix * (ch * cl + cl * cg), bytes_=9 << 20,
    )
    early = jnp.tile(early.astype(F32).sum(0).astype(BF), (count // 2, 1))
    got, d_conv, early = tied(got, d_conv, early)
    early = core_exchange(early, count).reshape(-1, 384)
    late_rows = -(-(3 * 384 + 3 * cs) // (16 * count)) * 16 * count
    d_unit, late = call(
        functools.partial(tail_kernel, norm_w, sizes, cl),
        "tail",
        (rows,),
        [
            (got, None, None), (tct, None, None), (tst, None, None), (masked, one_row(ch), at_y),
            (d_joined, one_row(256), at_y), (w_in_d, None, None), (grad_freq, None, None),
        ],
        [((rows, width, 256), BF, one_row(256), at_y), ((late_rows, 128), BF, None, None)],
        [vm((used, 384), BF), vm((used, 256), BF), vm((3, n, 128), F32), vm((256, cg), F32)],
        flops=1 << 30, bytes_=5 << 20,
    )
    late, early = tied(late, early)
    other = core_swap(early)
    late = scatter_sum(late, count)
    (grad_features,) = call(
        functools.partial(finish_kernel, cl),
        "finish",
        (rows,),
        [
            (marked, blocks(128), at_blocks), (d_unit, one_row(256), at_y), (d_conv, one_row(ch), at_y),
            (w_in_t, None, None),
        ],
        [(wide, BF, one_row(ch), at_y)],
        flops=2 * pix * 256 * cg, bytes_=7 << 20,
    )
    late, grad_features = tied(late, grad_features)
    grad_local, grad_cross, grad_out = call(
        functools.partial(unpack_kernel, cl),
        "unpack",
        (1,),
        [(early, None, None), (other, None, None), (my_core, None, None)],
        [((3, 3, ch, cl), F32, None, None), ((9 * cl, cg), F32, None, None), ((cs, cg), F32, None, None)],
        flops=1, bytes_=7 << 20,
    )
    late = gather(late, count)
    late, grad_local, grad_cross, grad_out = tied(late, grad_local, grad_cross, grad_out)
    grad_freq = jnp.concatenate([late[k * 384 : (k + 1) * 384] for k in range(3)], 1).astype(F32)
    at = 3 * 384
    grad_in = jnp.concatenate([late[at + k * cs : at + (k + 1) * cs] for k in range(3)], 1).astype(F32).T
    grad_cross = grad_cross.reshape(3, 3, cl, cg)
    return output[None], grad_features[None], grad_local, grad_cross, grad_in, grad_freq, grad_out


def solution(mesh):
    return jax.shard_map(
        shards,
        mesh=mesh,
        in_specs=(
            P("dp", "row", "col", None),
            P("dp", "row", "col"),
            P("dp", "row", "col", None),
            P(),
            P(),
            P(),
            P(),
            P(),
        ),
        out_specs=(
            P("dp", ("row", "col"), None, None),
            P("dp", ("row", "col"), None, None),
            P("dp", None, None, None),
            P("dp", None, None, None),
            P("dp", None),
            P("dp", None),
            P("dp", None),
        ),
        check_vma=False,
    )
```
